32 devices in a mesh: gx: 4 (over y, core), vert: 8 (over z, x).
Axes of the slice: x: 2, y: 2, z: 4, core: 2. Of those that a mesh axis runs over, the one named last changes fastest.
Arguments:
- dist: float32 [4096, 32, 128], P('vert', 'gx'), may hold values from 0.14 to 1.43
- inflow: float32 [4096, 128], P('vert'), may hold values from 0.25 to 1
- speed_x: float32 [4096], P('vert'), may hold values from 0.25 to 3
- transverse: float32 [2, 4096], P(None, 'vert'), may hold values from -1 to 1
- quad_weight: float32 [4096], P('vert'), may hold values from 0.5 to 2
- side: int32 [4096], P('vert'), may hold values from 0 to 1, as said below
Outputs:
- new_dist: float32 [4096, 32, 128], P('vert', 'gx')
- new_moments: float32 [13, 32, 128], P(None, 'gx')
The draws below stay inside these ranges and needn't reach their ends.
Inputs may be any that keep to these rules, and one draw needn't show every extreme that they name: `side`: all velocities within one shard of the vert axis share the same value, and half of those shards hold 1.
All inputs are finite; a program needn't handle non-finite values.
Results may differ from the reference program's by a relative error of at most 0.0003.
Values sent between devices are 32-bit elements; how exact they have to be, the bound alone decides.
No kernel may reach another device: no remote copies, remote signals or barrier semaphores. Data moves between devices by JAX's collectives and lax.ppermute only.
A program may use at most 64 MiB of HBM per device.

```python
import math
import jax
import jax.numpy as jnp
from jax import lax

V = 4096
NZ = 32
NX = 32
YZ = 128
N_VERT = 8


def draw_side(key, part):
    order = jax.random.permutation(jax.random.fold_in(key, 17), N_VERT)
    blocks = (order < N_VERT // 2).astype(jnp.int32)
    return jnp.repeat(blocks, V // N_VERT)


def velocity_set(key):
    speed_key = jax.random.fold_in(key, 101)
    cross_key = jax.random.fold_in(key, 202)
    speed = jnp.exp(jax.random.uniform(speed_key, (V,), jnp.float32, math.log(0.25), math.log(3.0)))
    unit = jax.random.uniform(cross_key, (2, V), jnp.float32)
    lower = jnp.array([-0.7, -1.0], jnp.float32)[:, None]
    cross = lower + 1.7 * unit
    return (speed, cross)


def draw_speed_x(key, part):
    return velocity_set(key)[0]


def draw_transverse(key, part):
    return velocity_set(key)[1]


def draw_dist(key, part):
    speed, cross = velocity_set(key)
    cell_key = jax.random.fold_in(key, 303)
    rough_key = jax.random.fold_in(key, 404)
    cell_scale = jnp.exp(jax.random.uniform(cell_key, (1, NX, YZ), jnp.float32, math.log(0.5), 0.0))
    rough = jnp.exp(jax.random.uniform(rough_key, (V, NX, YZ), jnp.float32, math.log(0.5), 0.0))
    tilt = 1.0 + 0.25 * (cross[0] + cross[1]) * (speed / 3.0)
    return cell_scale * rough * tilt[:, None, None]


def block_scale(stream_key, extent, split, low, high):
    loudness, own = 1.0, jax.random.fold_in(stream_key, 6)
    for dim, shards_of in split:
        draws = jnp.exp(jax.random.uniform(jax.random.fold_in(own, dim), (shards_of,), jnp.float32, low / len(split), high / len(split)))
        loudness = loudness * jnp.repeat(draws, extent[dim] // shards_of).reshape([-1 if axis == dim else 1 for axis in range(len(extent))])
    return loudness


def setup_inputs(seed: int = 0) -> dict:
    key_list = jax.random.split(jax.random.key(seed), 7)
    return {
        "dist": draw_dist(jax.random.fold_in(key_list[6], 71), 0),
        "inflow": jnp.clip(jnp.exp(math.log(1.0) - 1.3862944 * jax.random.uniform(key_list[1], (V, YZ), jnp.float32) ** block_scale(key_list[1], (V, YZ), ((0, 8),), -0.2, 0.2)), 0.25, 1.0),
        "speed_x": draw_speed_x(jax.random.fold_in(key_list[6], 71), 0),
        "transverse": draw_transverse(jax.random.fold_in(key_list[6], 71), 0),
        "quad_weight": jnp.clip(jnp.exp(math.log(2.0) - 1.3862944 * jax.random.uniform(key_list[4], (V,), jnp.float32) ** block_scale(key_list[4], (V,), ((0, 8),), -0.2, 0.2)), 0.5, 2.0),
        "side": draw_side(jax.random.fold_in(key_list[6], 71), 0),
    }


KAPPA_CELL = 0.02
DIFFUSIVITY_RATIO = 2.0 / 3.0
THERMAL_REFERENT = 1.0
SHEAR_EXPONENT = 0.81
HIGHEST_PREC = lax.Precision.HIGHEST


def components(speed_x, transverse, side):
    signed_x = jnp.where(side == 1, speed_x, -speed_x)
    return signed_x, transverse[0], transverse[1]


def basis_table(signed_x, cross_y, cross_z, quad_weight):
    square = signed_x * signed_x + cross_y * cross_y + cross_z * cross_z
    table = jnp.stack([jnp.ones_like(signed_x), signed_x, cross_y, cross_z,
                       signed_x * signed_x, cross_y * cross_y, cross_z * cross_z,
                       signed_x * cross_y, signed_x * cross_z, cross_y * cross_z,
                       signed_x * square, cross_y * square, cross_z * square])
    return table * (quad_weight / V)[None, :]


def moment_terms(table, distrib):
    flat = distrib.reshape(distrib.shape[0], distrib.shape[1] * distrib.shape[2])
    summed = jnp.dot(table, flat, precision=HIGHEST_PREC, preferred_element_type=jnp.float32)
    return summed.reshape(13, distrib.shape[1], distrib.shape[2])


def target_state(moments):
    particle_concentration = moments[0]
    mean_drift_vector = [moments[1] / particle_concentration, moments[2] / particle_concentration, moments[3] / particle_concentration]
    overall_internal_content = moments[4] + moments[5] + moments[6]
    mean_drift_norm = mean_drift_vector[0] * mean_drift_vector[0] + mean_drift_vector[1] * mean_drift_vector[1] + mean_drift_vector[2] * mean_drift_vector[2]
    cellwise_thermal_level = (overall_internal_content / particle_concentration - mean_drift_norm) / 3.0
    second = [[moments[4], moments[7], moments[8]],
              [moments[7], moments[5], moments[9]],
              [moments[8], moments[9], moments[6]]]
    heat_fluxes = []
    for component in range(3):
        inner = mean_drift_vector[0] * second[component][0] + mean_drift_vector[1] * second[component][1] + mean_drift_vector[2] * second[component][2]
        heat_fluxes.append(0.5 * (moments[10 + component] - 2.0 * inner - mean_drift_vector[component] * overall_internal_content
                             + 2.0 * particle_concentration * mean_drift_vector[component] * mean_drift_norm))
    collision_frequency = particle_concentration * cellwise_thermal_level ** (1.0 - SHEAR_EXPONENT)
    return jnp.stack([particle_concentration, mean_drift_vector[0], mean_drift_vector[1], mean_drift_vector[2], cellwise_thermal_level,
                      heat_fluxes[0], heat_fluxes[1], heat_fluxes[2], collision_frequency])


def shakhov(molecular_motion_field, signed_x, cross_y, cross_z):
    rel_x = signed_x[:, None, None] - molecular_motion_field[1][None]
    rel_y = cross_y[:, None, None] - molecular_motion_field[2][None]
    rel_z = cross_z[:, None, None] - molecular_motion_field[3][None]
    particle_concentration = molecular_motion_field[0][None]
    cellwise_thermal_level = molecular_motion_field[4][None]
    thermal_motion_norm = rel_x * rel_x + rel_y * rel_y + rel_z * rel_z
    equilibrium_distribution = particle_concentration * (THERMAL_REFERENT / cellwise_thermal_level) ** 1.5 * jnp.exp(-thermal_motion_norm / (2.0 * cellwise_thermal_level))
    axial_upwind_transfer = rel_x * molecular_motion_field[5][None] + rel_y * molecular_motion_field[6][None] + rel_z * molecular_motion_field[7][None]
    conduction_correction = 1.0 + (1.0 - DIFFUSIVITY_RATIO) * axial_upwind_transfer / (5.0 * particle_concentration * cellwise_thermal_level * cellwise_thermal_level) * (thermal_motion_norm / cellwise_thermal_level - 5.0)
    return equilibrium_distribution * conduction_correction


def lagged(distrib, cross_y, cross_z):
    z_index = lax.broadcasted_iota(jnp.int32, (1, 1, distrib.shape[2]), 2) % NZ
    y_prev = jnp.roll(distrib, NZ, axis=2)
    y_next = jnp.roll(distrib, -NZ, axis=2)
    z_prev = jnp.where(z_index == 0, jnp.roll(distrib, 1 - NZ, axis=2), jnp.roll(distrib, 1, axis=2))
    z_next = jnp.where(z_index == NZ - 1, jnp.roll(distrib, NZ - 1, axis=2), jnp.roll(distrib, -1, axis=2))
    coef_y = cross_y[:, None, None]
    coef_z = cross_z[:, None, None]
    diff_y = jnp.where(coef_y > 0, distrib - y_prev, y_next - distrib)
    diff_z = jnp.where(coef_z > 0, distrib - z_prev, z_next - distrib)
    return coef_y * diff_y + coef_z * diff_z


def coefficients(slope_term, molecular_motion_field, signed_x, cross_y, cross_z):
    target = shakhov(molecular_motion_field, signed_x, cross_y, cross_z)
    speed = jnp.abs(signed_x)[:, None, None]
    collision_frequency = KAPPA_CELL * molecular_motion_field[8][None]
    denom = speed + collision_frequency
    return speed / denom, (collision_frequency * target - KAPPA_CELL * slope_term) / denom


def reference(dist, inflow, speed_x, transverse, quad_weight, side):
    signed_x, cross_y, cross_z = components(speed_x, transverse, side)
    table = basis_table(signed_x, cross_y, cross_z, quad_weight)
    molecular_motion_field = target_state(moment_terms(table, dist))
    block_width = V // N_VERT
    block_count = V // block_width

    def one_block(block_index):
        start = (block_index * block_width).astype(jnp.int32)
        distrib = lax.dynamic_slice_in_dim(dist, start, block_width, 0)
        part_x = lax.dynamic_slice_in_dim(signed_x, start, block_width, 0)
        part_y = lax.dynamic_slice_in_dim(cross_y, start, block_width, 0)
        part_z = lax.dynamic_slice_in_dim(cross_z, start, block_width, 0)
        slope_term = lagged(distrib, part_y, part_z)
        decay_rate, source_term = coefficients(slope_term, molecular_motion_field, part_x, part_y, part_z)
        is_back = (lax.dynamic_slice_in_dim(side, start, block_width, 0) == 0)[:, None, None]
        decay_rate = jnp.where(is_back, decay_rate[:, ::-1], decay_rate)
        source_term = jnp.where(is_back, source_term[:, ::-1], source_term)
        entry_face = lax.dynamic_slice_in_dim(inflow, start, block_width, 0)

        def advance(carry, pair):
            value = pair[0] * carry + pair[1]
            return value, value

        _, swept_field = lax.scan(advance, entry_face,
                                  (jnp.moveaxis(decay_rate, 1, 0), jnp.moveaxis(source_term, 1, 0)))
        swept_field = jnp.moveaxis(swept_field, 0, 1)
        swept_field = jnp.where(is_back, swept_field[:, ::-1], swept_field)
        part_table = lax.dynamic_slice_in_dim(table, start, block_width, 1)
        return swept_field, moment_terms(part_table, swept_field)

    fields, partials = lax.map(one_block, jnp.arange(block_count, dtype=jnp.int32))
    new_dist = fields.reshape(V, NX, YZ)
    return new_dist, jnp.sum(partials, axis=0)
```

```python
import functools

import jax
import jax.numpy as jnp
from jax import lax
from jax.experimental import pallas as pl
from jax.experimental.pallas import tpu as pltpu
from jax.sharding import PartitionSpec as P

NZ = 32
KAPPA_CELL = 0.02
LOG2E = 1.4426950408889634
SHEAR = 0.19
NMOM = 13
ROWS = 16


def params(**kw):
    return pltpu.CompilerParams(vmem_limit_bytes=40 * 1024 * 1024, **kw)


def cost(flops, nbytes):
    return pl.CostEstimate(flops=flops, bytes_accessed=nbytes, transcendentals=0)


def split(a):
    high = a.astype(jnp.bfloat16)
    low = (a - high.astype(jnp.float32)).astype(jnp.bfloat16)
    return high, low


def project(table, plane):
    high, low = split(plane)
    first = jnp.dot(table, high, preferred_element_type=jnp.float32)
    second = jnp.dot(table[:ROWS], low, preferred_element_type=jnp.float32)
    return first[:ROWS] + first[ROWS:] + second


def moments_kernel(total, nx, side_ref, speed_ref, cross_ref, weight_ref, dist_ref, mom_ref, table_ref):
    count = speed_ref.shape[1]
    speed = speed_ref[...]
    x = jnp.where(side_ref[...] == 1, speed, -speed)
    y = cross_ref[0:1, :]
    z = cross_ref[1:2, :]
    xx, yy, zz = x * x, y * y, z * z
    square = xx + yy + zz
    rows = [jnp.ones_like(x), x, y, z, xx, yy, zz, x * y, x * z, y * z, x * square, y * square, z * square]
    rows += [jnp.zeros_like(x)] * (ROWS - NMOM)
    full = jnp.concatenate(rows, axis=0) * (weight_ref[...] * (1.0 / total))
    high, low = split(full)
    table = jnp.concatenate([high, low], axis=0)
    table_ref[...] = table
    first = pl.program_id(0) == 0
    for i in range(0, nx, 2):
        planes = [dist_ref[pl.ds(i + k, count, stride=nx), :] for k in range(min(2, nx - i))]
        lanes = planes[0].shape[1]
        got = project(table, jnp.concatenate(planes, axis=1))
        for k in range(len(planes)):
            part = got[:NMOM, k * lanes : (k + 1) * lanes]
            place = pl.ds(i + k, NMOM, stride=nx)

            @pl.when(first)
            def _():
                mom_ref[place, :] = part

            @pl.when(jnp.logical_not(first))
            def _():
                mom_ref[place, :] += part


def old_moments(total, nx, side, speed, cross, weight, dist):
    count, lanes = speed.shape[1], dist.shape[1]
    chunk = min(count, 256)
    steps = count // chunk
    vec = lambda r: pl.BlockSpec((r, chunk), lambda i: (0, i))
    return pl.pallas_call(
        functools.partial(moments_kernel, total, nx),
        grid=(steps,),
        in_specs=[vec(1), vec(1), vec(2), vec(1), pl.BlockSpec((chunk * nx, lanes), lambda i: (i, 0))],
        out_specs=[pl.BlockSpec((NMOM * nx, lanes), lambda i: (0, 0)), vec(2 * ROWS)],
        out_shape=[
            jax.ShapeDtypeStruct((NMOM * nx, lanes), jnp.float32),
            jax.ShapeDtypeStruct((2 * ROWS, count), jnp.bfloat16),
        ],
        compiler_params=params(),
        cost_estimate=cost(2 * 48 * count * nx * lanes, 4 * count * nx * lanes),
        name="moments",
    )(side, speed, cross, weight, dist)


def slope_kernel(nx, side_ref, speed_ref, cross_ref, dist_ref, slope_ref, comp_ref):
    count = speed_ref.shape[1]
    lanes = dist_ref.shape[1]
    speed = speed_ref[...]
    x = jnp.where(side_ref[...] == 1, speed, -speed)
    stacked = jnp.concatenate([x, cross_ref[...], jnp.zeros((5, count), jnp.float32)], axis=0)
    columns = jnp.transpose(stacked)
    for k in range(3):
        comp_ref[k] = jnp.broadcast_to(columns[:, k : k + 1], (count, lanes))
    group = 32

    def one(g, carry):
        at = pl.multiple_of(g * group, group)
        y = comp_ref[1, pl.ds(at, group), :]
        z = comp_ref[2, pl.ds(at, group), :]
        lane = lax.broadcasted_iota(jnp.int32, (group, lanes), 1)
        from_y = jnp.where(y > 0, lane + (lanes - NZ), lane + NZ) & (lanes - 1)
        from_z = (lane & ~(NZ - 1)) | (jnp.where(z > 0, lane + (NZ - 1), lane + 1) & (NZ - 1))
        ay, az = KAPPA_CELL * jnp.abs(y), KAPPA_CELL * jnp.abs(z)
        both = ay + az
        for i in range(nx):
            d = dist_ref[pl.ds(at * nx + i, group, stride=nx), :]
            near_y = jnp.take_along_axis(d, from_y, axis=1)
            near_z = jnp.take_along_axis(d, from_z, axis=1)
            slope_ref[i, pl.ds(at, group), :] = both * d - ay * near_y - az * near_z
        return carry

    lax.fori_loop(0, count // group, one, 0)


def slopes(nx, side, speed, cross, dist):
    count, lanes = speed.shape[1], dist.shape[1]
    chunk = min(count, 128)
    vec = lambda r: pl.BlockSpec((r, chunk), lambda i: (0, i))
    return pl.pallas_call(
        functools.partial(slope_kernel, nx),
        grid=(count // chunk,),
        in_specs=[vec(1), vec(1), vec(2), pl.BlockSpec((chunk * nx, lanes), lambda i: (i, 0))],
        out_specs=[
            pl.BlockSpec((nx, chunk, lanes), lambda i: (0, i, 0)),
            pl.BlockSpec((3, chunk, lanes), lambda i: (0, i, 0)),
        ],
        out_shape=[
            jax.ShapeDtypeStruct((nx, count, lanes), jnp.float32),
            jax.ShapeDtypeStruct((3, count, lanes), jnp.float32),
        ],
        compiler_params=params(),
        cost_estimate=cost(20 * count * nx * lanes, 8 * count * nx * lanes),
        name="slope",
    )(side, speed, cross, dist)


def map_kernel(nx, side_ref, ma_ref, mb_ref, comp_ref, slope_ref, inflow_ref,
               decay_ref, source_ref, face_ref, state):
    lanes = inflow_ref.shape[1]
    count = inflow_ref.shape[0]
    m = [ma_ref[k * nx : (k + 1) * nx, :] + mb_ref[k * nx : (k + 1) * nx, :] for k in range(NMOM)]
    n = m[0]
    inv_n = 1.0 / n
    u = [m[1] * inv_n, m[2] * inv_n, m[3] * inv_n]
    energy = m[4] + m[5] + m[6]
    uu = u[0] * u[0] + u[1] * u[1] + u[2] * u[2]
    temp = (energy * inv_n - uu) * (1.0 / 3.0)
    second = ((m[4], m[7], m[8]), (m[7], m[5], m[9]), (m[8], m[9], m[6]))
    inv_t = 1.0 / temp
    flux_scale = inv_n * inv_t * inv_t * (1.0 / 15.0)
    nu = KAPPA_CELL * n * jnp.exp(SHEAR * jnp.log(temp))
    for k in range(3):
        inner = u[0] * second[k][0] + u[1] * second[k][1] + u[2] * second[k][2]
        q = 0.5 * (m[10 + k] - 2.0 * inner - u[k] * energy + 2.0 * n * u[k] * uu)
        state[k] = u[k]
        state[3 + k] = q * flux_scale
    state[6] = inv_t
    state[7] = inv_t * (-0.5 * LOG2E)
    state[8] = nu * n * inv_t * jnp.sqrt(inv_t)
    state[9] = nu
    forward = side_ref[0, 0] == 1
    group = 32

    for j in range(nx):
        at_x = jnp.where(forward, j, nx - 1 - j)
        before = jnp.where(forward, j - 1, nx - j)
        s = [jnp.broadcast_to(state[k, pl.ds(at_x, 1), :], (8, lanes)) for k in range(10)]
        s = [jnp.concatenate([a] * (group // 8), axis=0) for a in s]

        def one(g, carry):
            at = pl.multiple_of(g * group, group)
            rows = pl.ds(at, group)
            cx = comp_ref[0, rows, :]
            wx = cx - s[0]
            wy = comp_ref[1, rows, :] - s[1]
            wz = comp_ref[2, rows, :] - s[2]
            ww = wx * wx + wy * wy + wz * wz
            wq = wx * s[3] + wy * s[4] + wz * s[5]
            shape = 1.0 + wq * (ww * s[6] - 5.0)
            target = s[8] * jnp.exp2(ww * s[7]) * shape
            speed = jnp.abs(cx)
            inv = 1.0 / (speed + s[9])
            decay = speed * inv
            source = (target - slope_ref[at_x, rows, :]) * inv
            if j > 0:
                source = decay * source_ref[before, rows, :] + source
                decay = decay * decay_ref[before, rows, :]
            decay_ref[at_x, rows, :] = decay
            source_ref[at_x, rows, :] = source
            if j == nx - 1:
                face_ref[rows, :] = decay * inflow_ref[rows, :] + source
            return carry

        lax.fori_loop(0, count // group, one, 0)


def maps(nx, side, ma, mb, comp, slope, inflow):
    count, lanes = inflow.shape
    whole = pl.BlockSpec(memory_space=pltpu.VMEM)
    return pl.pallas_call(
        functools.partial(map_kernel, nx),
        in_specs=[pl.BlockSpec(memory_space=pltpu.SMEM)] + [whole] * 5,
        out_specs=[whole] * 3,
        out_shape=[
            jax.ShapeDtypeStruct((nx, count, lanes), jnp.float32),
            jax.ShapeDtypeStruct((nx, count, lanes), jnp.float32),
            jax.ShapeDtypeStruct((count, lanes), jnp.float32),
        ],
        scratch_shapes=[pltpu.VMEM((10, nx, lanes), jnp.float32)],
        compiler_params=params(),
        cost_estimate=cost(40 * count * nx * lanes, 12 * count * nx * lanes),
        name="maps",
    )(side, ma, mb, comp, slope, inflow)


def finish_kernel(nx, table_ref, entry_ref, decay_ref, source_ref, dist_ref, mom_ref):
    entry = entry_ref[...]
    count, lanes = entry.shape
    table = table_ref[...]
    for i in range(0, nx, 2):
        planes = []
        for k in range(min(2, nx - i)):
            plane = decay_ref[i + k] * entry + source_ref[i + k]
            dist_ref[pl.ds(i + k, count, stride=nx), :] = plane
            planes.append(plane)
        got = project(table, jnp.concatenate(planes, axis=1))
        for k in range(len(planes)):
            mom_ref[pl.ds(i + k, NMOM, stride=nx), :] = got[:NMOM, k * lanes : (k + 1) * lanes]


def finish(nx, table, entry, decay, source):
    count, lanes = entry.shape
    whole = pl.BlockSpec(memory_space=pltpu.VMEM)
    return pl.pallas_call(
        functools.partial(finish_kernel, nx),
        in_specs=[whole] * 4,
        out_specs=[whole] * 2,
        out_shape=[
            jax.ShapeDtypeStruct((count * nx, lanes), jnp.float32),
            jax.ShapeDtypeStruct((NMOM * nx, lanes), jnp.float32),
        ],
        compiler_params=params(),
        cost_estimate=cost(2 * 48 * count * nx * lanes, 12 * count * nx * lanes),
        name="finish",
    )(table, entry, decay, source)


def stages_of(n):
    out, bit = [], 1
    while bit < n:
        if bit * 4 <= n:
            out.append((bit, 2 * bit, 3 * bit))
            bit *= 4
        else:
            out.append((bit,))
            bit *= 2
    return out


def exchange(a, axis, mask):
    n = lax.axis_size(axis)
    return lax.ppermute(a, axis, [(i, i ^ mask) for i in range(n)])


def partial_sums(a, axis):
    n = lax.axis_size(axis)
    if n & (n - 1) or n == 1:
        total = lax.psum(a, axis)
        return total, jnp.zeros_like(total)
    stages = stages_of(n)
    for masks in stages[:-1]:
        a = functools.reduce(jnp.add, [exchange(a, axis, m) for m in masks], a)
    other = functools.reduce(jnp.add, [exchange(a, axis, m) for m in stages[-1]])
    return a, other


def hop(face, n, step):
    up = [(step, step + 1)]
    down = [(n - 1 - step, n - 2 - step)]
    if n % 2 == 0:
        got = lax.ppermute(face, "gx", up + down)
        return got, got
    return lax.ppermute(face, "gx", up), lax.ppermute(face, "gx", down)


def local(total, dist, inflow, speed_x, transverse, quad_weight, side):
    count, nx, lanes = dist.shape
    flat = dist.reshape(count * nx, lanes)
    side_row = side.reshape(1, count)
    speed = speed_x.reshape(1, count)
    weight = quad_weight.reshape(1, count)
    partial, table = old_moments(total, nx, side_row, speed, transverse, weight, flat)
    slope, comp = slopes(nx, side_row, speed, transverse, flat)
    ma, mb = partial_sums(partial, "vert")
    decay, source, face = maps(nx, side_row[:, :1], ma, mb, comp, slope, inflow)
    n = lax.axis_size("gx")
    place = lax.axis_index("gx")
    forward = side[0] == 1
    place = jnp.where(forward, place, n - 1 - place)
    entry = inflow
    if n > 1:
        last_decay = jnp.where(forward, decay[nx - 1], decay[0])
        last_source = jnp.where(forward, source[nx - 1], source[0])
    for step in range(n - 1):
        low, high = hop(face, n, step)
        entry = jnp.where(place == step + 1, jnp.where(forward, low, high), entry)
        if step < n - 2:
            face = last_decay * entry + last_source
    new_flat, new_partial = finish(nx, table, entry, decay, source)
    na, nb = partial_sums(new_partial, "vert")
    return new_flat.reshape(count, nx, lanes), (na + nb).reshape(NMOM, nx, lanes)


def solution(mesh):
    def whole(dist, inflow, speed_x, transverse, quad_weight, side):
        body = functools.partial(local, dist.shape[0])
        return jax.shard_map(
            body,
            mesh=mesh,
            in_specs=(P("vert", "gx", None), P("vert", None), P("vert"), P(None, "vert"), P("vert"), P("vert")),
            out_specs=(P("vert", "gx", None), P(None, "gx", None)),
            check_vma=False,
        )(dist, inflow, speed_x, transverse, quad_weight, side)

    return whole
```

```python
import functools

import jax
import jax.numpy as jnp
from jax import lax
from jax.experimental import pallas as pl
from jax.experimental.pallas import tpu as pltpu
from jax.sharding import PartitionSpec as P

NZ = 32
KAPPA_CELL = 0.02
LOG2E = 1.4426950408889634
SHEAR = 0.19
NMOM = 13
ROWS = 16


def params(**kw):
    return pltpu.CompilerParams(vmem_limit_bytes=20 * 1024 * 1024, **kw)


def cost(flops, nbytes):
    return pl.CostEstimate(flops=flops, bytes_accessed=nbytes, transcendentals=0)


def split(a):
    high = a.astype(jnp.bfloat16)
    low = (a - high.astype(jnp.float32)).astype(jnp.bfloat16)
    return high, low


def project(table, plane):
    high, low = split(plane)
    first = jnp.dot(table, high, preferred_element_type=jnp.float32)
    second = jnp.dot(table[:ROWS], low, preferred_element_type=jnp.float32)
    return first[:ROWS] + first[ROWS:] + second


def moments_kernel(total, nx, chunks, side_hbm, speed_hbm, cross_hbm, weight_hbm, dist_hbm,
                   mom_ref, table_ref, side_ref, speed_ref, cross_ref, weight_ref, dist_ref, sems):
    count = speed_ref.shape[1]
    chunk = count // chunks
    small = [(side_hbm, side_ref), (speed_hbm, speed_ref), (cross_hbm, cross_ref), (weight_hbm, weight_ref)]
    copies = [pltpu.make_async_copy(a, b, sems.at[chunks + i]) for i, (a, b) in enumerate(small)]
    parts = []
    for i in range(chunks):
        rows = pl.ds(i * chunk * nx, chunk * nx)
        parts.append(pltpu.make_async_copy(dist_hbm.at[rows, :], dist_ref.at[rows, :], sems.at[i]))
    for c in copies + parts:
        c.start()
    for c in copies:
        c.wait()
    speed = speed_ref[...]
    x = jnp.where(side_ref[...] == 1, speed, -speed)
    y = cross_ref[0:1, :]
    z = cross_ref[1:2, :]
    xx, yy, zz = x * x, y * y, z * z
    square = xx + yy + zz
    rows = [jnp.ones_like(x), x, y, z, xx, yy, zz, x * y, x * z, y * z, x * square, y * square, z * square]
    rows += [jnp.zeros_like(x)] * (ROWS - NMOM)
    full = jnp.concatenate(rows, axis=0) * (weight_ref[...] * (1.0 / total))
    high, low = split(full)
    table = jnp.concatenate([high, low], axis=0)
    table_ref[...] = table
    for c in range(chunks):
        parts[c].wait()
        tab = table[:, c * chunk : (c + 1) * chunk]
        for i in range(0, nx, 2):
            pair = range(min(2, nx - i))
            planes = [dist_ref[pl.ds(c * chunk * nx + i + k, chunk, stride=nx), :] for k in pair]
            lanes = planes[0].shape[1]
            got = project(tab, jnp.concatenate(planes, axis=1))
            for k in pair:
                part = got[:NMOM, k * lanes : (k + 1) * lanes]
                place = pl.ds(i + k, NMOM, stride=nx)
                if c == 0:
                    mom_ref[place, :] = part
                else:
                    mom_ref[place, :] += part


def old_moments(total, nx, side, speed, cross, weight, dist):
    count, lanes = speed.shape[1], dist.shape[1]
    chunks = max(1, count // 256)
    whole = pl.BlockSpec(memory_space=pltpu.VMEM)
    return pl.pallas_call(
        functools.partial(moments_kernel, total, nx, chunks),
        in_specs=[pl.BlockSpec(memory_space=pltpu.HBM)] * 5,
        out_specs=[whole] * 2,
        out_shape=[
            jax.ShapeDtypeStruct((NMOM * nx, lanes), jnp.float32),
            jax.ShapeDtypeStruct((2 * ROWS, count), jnp.bfloat16),
        ],
        scratch_shapes=[
            pltpu.VMEM(side.shape, jnp.int32),
            pltpu.VMEM(speed.shape, jnp.float32),
            pltpu.VMEM(cross.shape, jnp.float32),
            pltpu.VMEM(weight.shape, jnp.float32),
            pltpu.VMEM(dist.shape, jnp.float32),
            pltpu.SemaphoreType.DMA((chunks + 4,)),
        ],
        compiler_params=params(),
        cost_estimate=cost(2 * 48 * count * nx * lanes, 4 * count * nx * lanes),
        name="moments",
    )(*[pltpu.with_memory_space_constraint(a, pltpu.HBM) for a in (side, speed, cross, weight, dist)])


def slope_kernel(nx, side_ref, speed_ref, cross_ref, dist_ref, slope_ref, comp_ref):
    count = speed_ref.shape[1]
    lanes = dist_ref.shape[1]
    speed = speed_ref[...]
    x = jnp.where(side_ref[...] == 1, speed, -speed)
    stacked = jnp.concatenate([x, cross_ref[...], jnp.zeros((5, count), jnp.float32)], axis=0)
    columns = jnp.transpose(stacked)
    for k in range(3):
        comp_ref[k] = jnp.broadcast_to(columns[:, k : k + 1], (count, lanes))
    group = 32

    def one(g, carry):
        at = pl.multiple_of(g * group, group)
        y = comp_ref[1, pl.ds(at, group), :]
        z = comp_ref[2, pl.ds(at, group), :]
        lane = lax.broadcasted_iota(jnp.int32, (group, lanes), 1)
        from_y = jnp.where(y > 0, lane + (lanes - NZ), lane + NZ) & (lanes - 1)
        from_z = (lane & ~(NZ - 1)) | (jnp.where(z > 0, lane + (NZ - 1), lane + 1) & (NZ - 1))
        ay, az = KAPPA_CELL * jnp.abs(y), KAPPA_CELL * jnp.abs(z)
        both = ay + az
        for i in range(nx):
            d = dist_ref[pl.ds(at * nx + i, group, stride=nx), :]
            near_y = jnp.take_along_axis(d, from_y, axis=1)
            near_z = jnp.take_along_axis(d, from_z, axis=1)
            slope_ref[i, pl.ds(at, group), :] = both * d - ay * near_y - az * near_z
        return carry

    lax.fori_loop(0, count // group, one, 0)


def slopes(nx, half, halves, side, speed, cross, dist):
    count, lanes = speed.shape[1] // halves, dist.shape[1]
    chunk = min(count, 128)
    steps = count // chunk
    vec = lambda r: pl.BlockSpec((r, chunk), lambda i: (0, half * steps + i))
    return pl.pallas_call(
        functools.partial(slope_kernel, nx),
        grid=(steps,),
        in_specs=[vec(1), vec(1), vec(2), pl.BlockSpec((chunk * nx, lanes), lambda i: (half * steps + i, 0))],
        out_specs=[
            pl.BlockSpec((nx, chunk, lanes), lambda i: (0, i, 0)),
            pl.BlockSpec((3, chunk, lanes), lambda i: (0, i, 0)),
        ],
        out_shape=[
            jax.ShapeDtypeStruct((nx, count, lanes), jnp.float32),
            jax.ShapeDtypeStruct((3, count, lanes), jnp.float32),
        ],
        compiler_params=params(),
        cost_estimate=cost(20 * count * nx * lanes, 8 * count * nx * lanes),
        name="slope",
    )(side, speed, cross, dist)


def map_kernel(nx, halves, ma_ref, mb_ref, *refs):
    comps, slopes_in = refs[:halves], refs[halves : 2 * halves]
    inflow_ref, decay_ref, source_ref, face_ref, last_decay_ref, last_source_ref, place_ref, state = refs[2 * halves :]
    here, there = lax.axis_index("gx"), lax.axis_size("gx") - 1 - lax.axis_index("gx")
    place_ref[...] = jnp.where(comps[0][0, 0:8, :] > 0, here, there)
    lanes = inflow_ref.shape[1]
    count = inflow_ref.shape[0]
    m = [ma_ref[k * nx : (k + 1) * nx, :] + mb_ref[k * nx : (k + 1) * nx, :] for k in range(NMOM)]
    n = m[0]
    inv_n = 1.0 / n
    u = [m[1] * inv_n, m[2] * inv_n, m[3] * inv_n]
    energy = m[4] + m[5] + m[6]
    uu = u[0] * u[0] + u[1] * u[1] + u[2] * u[2]
    temp = (energy * inv_n - uu) * (1.0 / 3.0)
    second = ((m[4], m[7], m[8]), (m[7], m[5], m[9]), (m[8], m[9], m[6]))
    inv_t = 1.0 / temp
    flux_scale = inv_n * inv_t * inv_t * (1.0 / 15.0)
    nu = KAPPA_CELL * n * jnp.exp(SHEAR * jnp.log(temp))
    for k in range(3):
        inner = u[0] * second[k][0] + u[1] * second[k][1] + u[2] * second[k][2]
        q = 0.5 * (m[10 + k] - 2.0 * inner - u[k] * energy + 2.0 * n * u[k] * uu)
        state[k] = u[k]
        state[3 + k] = q * flux_scale
    state[6] = inv_t
    state[7] = inv_t * (-0.5 * LOG2E)
    state[8] = nu * n * inv_t * jnp.sqrt(inv_t)
    state[9] = nu
    forward = comps[0][0, 0:1, 0:1][0, 0] > 0
    group = 32
    part = count // halves

    for j in range(nx):
        at_x = jnp.where(forward, j, nx - 1 - j)
        before = jnp.where(forward, j - 1, nx - j)
        s = [jnp.broadcast_to(state[k, pl.ds(at_x, 1), :], (8, lanes)) for k in range(10)]
        s = [jnp.concatenate([a] * (group // 8), axis=0) for a in s]

        for h in range(halves):
            comp_ref, slope_ref = comps[h], slopes_in[h]

            def one(g, carry):
                at = pl.multiple_of(g * group, group)
                own = pl.ds(at, group)
                rows = pl.ds(h * part + at, group)
                cx = comp_ref[0, own, :]
                wx = cx - s[0]
                wy = comp_ref[1, own, :] - s[1]
                wz = comp_ref[2, own, :] - s[2]
                ww = wx * wx + wy * wy + wz * wz
                wq = wx * s[3] + wy * s[4] + wz * s[5]
                shape = 1.0 + wq * (ww * s[6] - 5.0)
                target = s[8] * jnp.exp2(ww * s[7]) * shape
                speed = jnp.abs(cx)
                inv = 1.0 / (speed + s[9])
                decay = speed * inv
                source = (target - slope_ref[at_x, own, :]) * inv
                if j > 0:
                    source = decay * source_ref[before, rows, :] + source
                    decay = decay * decay_ref[before, rows, :]
                decay_ref[at_x, rows, :] = decay
                source_ref[at_x, rows, :] = source
                if j == nx - 1:
                    last_decay_ref[rows, :] = decay
                    last_source_ref[rows, :] = source
                    face_ref[rows, :] = decay * inflow_ref[rows, :] + source
                return carry

            lax.fori_loop(0, part // group, one, 0)


def maps(nx, ma, mb, comps, slopes_in, inflow):
    count, lanes = inflow.shape
    halves = len(comps)
    whole = pl.BlockSpec(memory_space=pltpu.VMEM)
    field = pltpu.VMEM((nx, count, lanes), jnp.float32)
    face = pltpu.VMEM((count, lanes), jnp.float32)
    return pl.pallas_call(
        functools.partial(map_kernel, nx, halves),
        in_specs=[whole] * (3 + 2 * halves),
        out_specs=[whole] * 6,
        out_shape=[field, field, face, face, face, pltpu.VMEM((8, lanes), jnp.int32)],
        scratch_shapes=[pltpu.VMEM((10, nx, lanes), jnp.float32)],
        compiler_params=params(),
        cost_estimate=cost(40 * count * nx * lanes, 12 * count * nx * lanes),
        name="maps",
    )(ma, mb, *comps, *slopes_in, inflow)


def entry_of(step, place_ref, got_ref, entry_ref):
    return jnp.where(place_ref[0:1, :] == step, got_ref[...], entry_ref[...])


def face_kernel(step, place_ref, got_ref, entry_ref, decay_ref, source_ref, next_ref, face_ref):
    entry = entry_of(step, place_ref, got_ref, entry_ref)
    next_ref[...] = entry
    face_ref[...] = decay_ref[...] * entry + source_ref[...]


def pass_face(step, place, got, entry, decay, source):
    whole = pl.BlockSpec(memory_space=pltpu.VMEM)
    out = pltpu.VMEM(entry.shape, jnp.float32)
    return pl.pallas_call(
        functools.partial(face_kernel, step),
        in_specs=[whole] * 5,
        out_specs=[whole] * 2,
        out_shape=[out, out],
        compiler_params=params(),
        cost_estimate=cost(2 * entry.size, 20 * entry.size),
        name="face",
    )(place, got, entry, decay, source)


def new_moments_kernel(nx, step, place_ref, got_ref, entry_ref, table_ref, decay_ref, source_ref, mom_ref):
    entry = entry_of(step, place_ref, got_ref, entry_ref)
    lanes = entry.shape[1]
    table = table_ref[...]
    for i in range(0, nx, 2):
        pair = range(min(2, nx - i))
        planes = [decay_ref[i + k] * entry + source_ref[i + k] for k in pair]
        got = project(table, jnp.concatenate(planes, axis=1))
        for k in pair:
            mom_ref[pl.ds(i + k, NMOM, stride=nx), :] = got[:NMOM, k * lanes : (k + 1) * lanes]


def new_moments(nx, step, face_in, table, decay, source):
    count, lanes = decay.shape[1:]
    whole = pl.BlockSpec(memory_space=pltpu.VMEM)
    return pl.pallas_call(
        functools.partial(new_moments_kernel, nx, step),
        in_specs=[whole] * 6,
        out_specs=whole,
        out_shape=jax.ShapeDtypeStruct((NMOM * nx, lanes), jnp.float32),
        compiler_params=params(),
        cost_estimate=cost(2 * 48 * count * nx * lanes, 8 * count * nx * lanes),
        name="new_moments",
    )(*face_in, table, decay, source)


def write_kernel(nx, step, place_ref, got_ref, entry_ref, decay_ref, source_ref, dist_ref):
    entry = entry_of(step, place_ref, got_ref, entry_ref)
    count = entry.shape[0]
    for i in range(nx):
        dist_ref[pl.ds(i, count, stride=nx), :] = decay_ref[i] * entry + source_ref[i]


def write_dist(nx, step, place, got, entry, decay, source):
    count, lanes = entry.shape
    chunk = min(count, 128)
    field = pl.BlockSpec((nx, chunk, lanes), lambda i: (0, i, 0))
    face = pl.BlockSpec((chunk, lanes), lambda i: (i, 0))
    return pl.pallas_call(
        functools.partial(write_kernel, nx, step),
        grid=(count // chunk,),
        in_specs=[pl.BlockSpec((8, lanes), lambda i: (0, 0)), face, face, field, field],
        out_specs=pl.BlockSpec((chunk * nx, lanes), lambda i: (i, 0)),
        out_shape=jax.ShapeDtypeStruct((count * nx, lanes), jnp.float32),
        compiler_params=params(),
        cost_estimate=cost(2 * count * nx * lanes, 12 * count * nx * lanes),
        name="write_dist",
    )(place, got, entry, decay, source)


def stages_of(n):
    out, bit = [], 1
    while bit < n:
        if bit * 4 <= n:
            out.append((bit, 2 * bit, 3 * bit))
            bit *= 4
        else:
            out.append((bit,))
            bit *= 2
    return out


def exchange(a, axis, mask):
    n = lax.axis_size(axis)
    return lax.ppermute(a, axis, [(i, i ^ mask) for i in range(n)])


def partial_sums(a, axis, beside=()):
    n = lax.axis_size(axis)
    beside = list(beside)
    if n & (n - 1) or n == 1:
        total = lax.psum(a, axis)
        return (total, jnp.zeros_like(total)), [f(a) for f in beside]
    stages = stages_of(n)
    done = []
    for i, masks in enumerate(stages):
        got = [exchange(a, axis, m) for m in masks]
        take = beside if i == len(stages) - 1 else beside[:1]
        beside = beside[len(take) :]
        made = [f(a) for f in take]
        got, made = lax.optimization_barrier((got, made))
        done += made
        other = functools.reduce(jnp.add, got)
        if i == len(stages) - 1:
            return (a, other), done
        a = a + other


def hop(face, side, step):
    n = lax.axis_size("gx")
    up = [(step, step + 1)]
    down = [(n - 1 - step, n - 2 - step)]
    if n % 2 == 0:
        return lax.ppermute(face, "gx", up + down)
    return jnp.where(side[0] == 1, lax.ppermute(face, "gx", up), lax.ppermute(face, "gx", down))


def local(total, dist, inflow, speed_x, transverse, quad_weight, side):
    count, nx, lanes = dist.shape
    flat = dist.reshape(count * nx, lanes)
    side_row = side.reshape(1, count)
    speed = speed_x.reshape(1, count)
    weight = quad_weight.reshape(1, count)
    partial, table = old_moments(total, nx, side_row, speed, transverse, weight, flat)

    def slope_part(half, halves):
        def make(sent):
            args = lax.optimization_barrier((side_row, speed, transverse, flat, sent))[:4]
            return slopes(nx, half, halves, *args)

        return make

    n = lax.axis_size("gx")
    halves = 2 if count % 256 == 0 else 1
    parts = [slope_part(h, halves) for h in range(halves)]
    (ma, mb), made = partial_sums(partial, "vert", parts)
    decay, source, face, last_decay, last_source, place = maps(
        nx, ma, mb, [m[1] for m in made], [m[0] for m in made], inflow
    )
    got, entry = inflow, inflow
    for step in range(n - 1):
        if step > 0:
            entry, face = pass_face(step, place, got, entry, last_decay, last_source)
        got = hop(face, side, step)
    new_partial = new_moments(nx, n - 1, (place, got, entry), table, decay, source)

    def write(sent):
        args = lax.optimization_barrier((place, got, entry, decay, source, sent))[:5]
        return write_dist(nx, n - 1, *args)

    (na, nb), (new_flat,) = partial_sums(new_partial, "vert", [write])
    return new_flat.reshape(count, nx, lanes), (na + nb).reshape(NMOM, nx, lanes)


def solution(mesh):
    def whole(dist, inflow, speed_x, transverse, quad_weight, side):
        body = functools.partial(local, dist.shape[0])
        return jax.shard_map(
            body,
            mesh=mesh,
            in_specs=(P("vert", "gx", None), P("vert", None), P("vert"), P(None, "vert"), P("vert"), P("vert")),
            out_specs=(P("vert", "gx", None), P(None, "gx", None)),
            check_vma=False,
        )(dist, inflow, speed_x, transverse, quad_weight, side)

    return whole
```

```python
import functools

import jax
import jax.numpy as jnp
from jax import lax
from jax.experimental import pallas as pl
from jax.experimental.pallas import tpu as pltpu
from jax.sharding import PartitionSpec as P

NZ = 32
KAPPA_CELL = 0.02
LOG2E = 1.4426950408889634
SHEAR = 0.19
NMOM = 13
ROWS = 16


def params(**kw):
    return pltpu.CompilerParams(vmem_limit_bytes=20 * 1024 * 1024, **kw)


def cost(flops, nbytes):
    return pl.CostEstimate(flops=flops, bytes_accessed=nbytes, transcendentals=0)


def split(a):
    high = a.astype(jnp.bfloat16)
    low = (a - high.astype(jnp.float32)).astype(jnp.bfloat16)
    return high, low


def project(table, plane):
    high, low = split(plane)
    first = jnp.dot(table, high, preferred_element_type=jnp.float32)
    second = jnp.dot(table[:ROWS], low, preferred_element_type=jnp.float32)
    return first[:ROWS] + first[ROWS:] + second


def moments_kernel(total, nx, chunks, side_hbm, speed_hbm, cross_hbm, weight_hbm, dist_hbm,
                   mom_ref, table_ref, rows_ref, dist_ref, side_ref, speed_ref, cross_ref, weight_ref, sems):
    count = speed_ref.shape[1]
    chunk = count // chunks
    small = [(side_hbm, side_ref), (speed_hbm, speed_ref), (cross_hbm, cross_ref), (weight_hbm, weight_ref)]
    copies = [pltpu.make_async_copy(a, b, sems.at[chunks + i]) for i, (a, b) in enumerate(small)]
    parts = []
    for i in range(chunks):
        rows = pl.ds(i * chunk * nx, chunk * nx)
        parts.append(pltpu.make_async_copy(dist_hbm.at[rows, :], dist_ref.at[rows, :], sems.at[i]))
    for c in copies + parts:
        c.start()
    for c in copies:
        c.wait()
    speed = speed_ref[...]
    x = jnp.where(side_ref[...] == 1, speed, -speed)
    y = cross_ref[0:1, :]
    z = cross_ref[1:2, :]
    xx, yy, zz = x * x, y * y, z * z
    square = xx + yy + zz
    rows_ref[...] = jnp.concatenate([x, y, z] + [jnp.zeros_like(x)] * 5, axis=0)
    rows = [jnp.ones_like(x), x, y, z, xx, yy, zz, x * y, x * z, y * z, x * square, y * square, z * square]
    rows += [jnp.zeros_like(x)] * (ROWS - NMOM)
    full = jnp.concatenate(rows, axis=0) * (weight_ref[...] * (1.0 / total))
    high, low = split(full)
    table = jnp.concatenate([high, low], axis=0)
    table_ref[...] = table
    for c in range(chunks):
        parts[c].wait()
        tab = table[:, c * chunk : (c + 1) * chunk]
        for i in range(0, nx, 2):
            pair = range(min(2, nx - i))
            planes = [dist_ref[pl.ds(c * chunk * nx + i + k, chunk, stride=nx), :] for k in pair]
            lanes = planes[0].shape[1]
            got = project(tab, jnp.concatenate(planes, axis=1))
            for k in pair:
                part = got[:NMOM, k * lanes : (k + 1) * lanes]
                place = pl.ds(i + k, NMOM, stride=nx)
                if c == 0:
                    mom_ref[place, :] = part
                else:
                    mom_ref[place, :] += part


def old_moments(total, nx, side, speed, cross, weight, dist):
    count, lanes = speed.shape[1], dist.shape[1]
    chunks = max(1, count // 128)
    whole = pl.BlockSpec(memory_space=pltpu.VMEM)
    return pl.pallas_call(
        functools.partial(moments_kernel, total, nx, chunks),
        in_specs=[pl.BlockSpec(memory_space=pltpu.HBM)] * 5,
        out_specs=[whole] * 4,
        out_shape=[
            pltpu.VMEM((NMOM * nx, lanes), jnp.float32),
            pltpu.VMEM((2 * ROWS, count), jnp.bfloat16),
            pltpu.VMEM((8, count), jnp.float32),
            pltpu.VMEM(dist.shape, jnp.float32),
        ],
        scratch_shapes=[
            pltpu.VMEM(side.shape, jnp.int32),
            pltpu.VMEM(speed.shape, jnp.float32),
            pltpu.VMEM(cross.shape, jnp.float32),
            pltpu.VMEM(weight.shape, jnp.float32),
            pltpu.SemaphoreType.DMA((chunks + 4,)),
        ],
        compiler_params=params(),
        cost_estimate=cost(2 * 48 * count * nx * lanes, 4 * count * nx * lanes),
        name="moments",
    )(*[pltpu.with_memory_space_constraint(a, pltpu.HBM) for a in (side, speed, cross, weight, dist)])


def slope_kernel(nx, start, rows_ref, dist_ref, slope_ref, comp_ref):
    count = slope_ref.shape[1]
    lanes = dist_ref.shape[1]
    columns = jnp.transpose(rows_ref[:, start : start + count])
    for k in range(3):
        comp_ref[k] = jnp.broadcast_to(columns[:, k : k + 1], (count, lanes))
    group = 32

    def one(g, carry):
        at = pl.multiple_of(g * group, group)
        y = comp_ref[1, pl.ds(at, group), :]
        z = comp_ref[2, pl.ds(at, group), :]
        lane = lax.broadcasted_iota(jnp.int32, (group, lanes), 1)
        from_y = jnp.where(y > 0, lane + (lanes - NZ), lane + NZ) & (lanes - 1)
        from_z = (lane & ~(NZ - 1)) | (jnp.where(z > 0, lane + (NZ - 1), lane + 1) & (NZ - 1))
        ay, az = KAPPA_CELL * jnp.abs(y), KAPPA_CELL * jnp.abs(z)
        both = ay + az
        for i in range(nx):
            d = dist_ref[pl.ds((start + at) * nx + i, group, stride=nx), :]
            near_y = jnp.take_along_axis(d, from_y, axis=1)
            near_z = jnp.take_along_axis(d, from_z, axis=1)
            slope_ref[i, pl.ds(at, group), :] = both * d - ay * near_y - az * near_z
        return carry

    lax.fori_loop(0, count // group, one, 0)


def slopes(nx, half, halves, rows, dist):
    count, lanes = rows.shape[1] // halves, dist.shape[1]
    whole = pl.BlockSpec(memory_space=pltpu.VMEM)
    return pl.pallas_call(
        functools.partial(slope_kernel, nx, half * count),
        in_specs=[whole] * 2,
        out_specs=[whole] * 2,
        out_shape=[
            pltpu.VMEM((nx, count, lanes), jnp.float32),
            pltpu.VMEM((3, count, lanes), jnp.float32),
        ],
        compiler_params=params(),
        cost_estimate=cost(20 * count * nx * lanes, 8 * count * nx * lanes),
        name="slope",
    )(rows, dist)


def map_kernel(nx, halves, ma_ref, mb_ref, *refs):
    comps, slopes_in = refs[:halves], refs[halves : 2 * halves]
    decay_ref, source_ref, send_ref, sign_ref, state = refs[2 * halves :]
    count, lanes = decay_ref.shape[1:]
    sign_ref[...] = comps[0][0, 0:8, :]
    m = [ma_ref[k * nx : (k + 1) * nx, :] + mb_ref[k * nx : (k + 1) * nx, :] for k in range(NMOM)]
    n = m[0]
    inv_n = 1.0 / n
    u = [m[1] * inv_n, m[2] * inv_n, m[3] * inv_n]
    energy = m[4] + m[5] + m[6]
    uu = u[0] * u[0] + u[1] * u[1] + u[2] * u[2]
    temp = (energy * inv_n - uu) * (1.0 / 3.0)
    second = ((m[4], m[7], m[8]), (m[7], m[5], m[9]), (m[8], m[9], m[6]))
    inv_t = 1.0 / temp
    flux_scale = inv_n * inv_t * inv_t * (1.0 / 15.0)
    nu = KAPPA_CELL * n * jnp.exp(SHEAR * jnp.log(temp))
    for k in range(3):
        inner = u[0] * second[k][0] + u[1] * second[k][1] + u[2] * second[k][2]
        q = 0.5 * (m[10 + k] - 2.0 * inner - u[k] * energy + 2.0 * n * u[k] * uu)
        state[k] = u[k]
        state[3 + k] = q * flux_scale
    state[6] = inv_t
    state[7] = inv_t * (-0.5 * LOG2E)
    state[8] = nu * n * inv_t * jnp.sqrt(inv_t)
    state[9] = nu
    forward = comps[0][0, 0:1, 0:1][0, 0] > 0
    group = 32
    part = count // halves

    for j in range(nx):
        at_x = jnp.where(forward, j, nx - 1 - j)
        before = jnp.where(forward, j - 1, nx - j)
        s = [jnp.broadcast_to(state[k, pl.ds(at_x, 1), :], (8, lanes)) for k in range(10)]
        s = [jnp.concatenate([a] * (group // 8), axis=0) for a in s]

        for h in range(halves):
            comp_ref, slope_ref = comps[h], slopes_in[h]

            def one(g, carry):
                at = pl.multiple_of(g * group, group)
                own = pl.ds(at, group)
                rows = pl.ds(h * part + at, group)
                cx = comp_ref[0, own, :]
                wx = cx - s[0]
                wy = comp_ref[1, own, :] - s[1]
                wz = comp_ref[2, own, :] - s[2]
                ww = wx * wx + wy * wy + wz * wz
                wq = wx * s[3] + wy * s[4] + wz * s[5]
                shape = 1.0 + wq * (ww * s[6] - 5.0)
                target = s[8] * jnp.exp2(ww * s[7]) * shape
                speed = jnp.abs(cx)
                inv = 1.0 / (speed + s[9])
                decay = speed * inv
                source = (target - slope_ref[at_x, own, :]) * inv
                if j > 0:
                    source = decay * source_ref[before, rows, :] + source
                    decay = decay * decay_ref[before, rows, :]
                decay_ref[at_x, rows, :] = decay
                source_ref[at_x, rows, :] = source
                return carry

            lax.fori_loop(0, part // group, one, 0)

    last = jnp.where(forward, nx - 1, 0)
    theirs = pl.ds(pl.multiple_of((1 - lax.axis_index("gx") % 2) * (count // 2), count // 2), count // 2)
    send_ref[0] = decay_ref[last, theirs, :]
    send_ref[1] = source_ref[last, theirs, :]


def maps(nx, ma, mb, comps, slopes_in):
    lanes = ma.shape[1]
    halves = len(comps)
    count = halves * comps[0].shape[1]
    whole = pl.BlockSpec(memory_space=pltpu.VMEM)
    field = pltpu.VMEM((nx, count, lanes), jnp.float32)
    return pl.pallas_call(
        functools.partial(map_kernel, nx, halves),
        in_specs=[whole] * (2 + 2 * halves),
        out_specs=[whole] * 4,
        out_shape=[
            field,
            field,
            pltpu.VMEM((2, count // 2, lanes), jnp.float32),
            pltpu.VMEM((8, lanes), jnp.float32),
        ],
        scratch_shapes=[pltpu.VMEM((10, nx, lanes), jnp.float32)],
        compiler_params=params(),
        cost_estimate=cost(40 * count * nx * lanes, 12 * count * nx * lanes),
        name="maps",
    )(ma, mb, *comps, *slopes_in)


def standing(sign_ref):
    place, chips = lax.axis_index("gx"), lax.axis_size("gx") // 2
    chip, core = place // 2, place % 2
    forward = sign_ref[0:1, :] > 0
    return jnp.where(forward, core, 1 - core) == 0, jnp.where(forward, chip, chips - 1 - chip)


def half_of(ref_rows, which):
    half = ref_rows // 2
    return pl.ds(pl.multiple_of(which * half, half), half)


def compose_kernel(nx, sign_ref, got_ref, decay_ref, source_ref, inflow_ref, near_ref, face_ref, entry_ref, *chip_ref):
    first, _ = standing(sign_ref)
    core = lax.axis_index("gx") % 2
    mine = half_of(inflow_ref.shape[0], core)
    last = jnp.where(sign_ref[0:1, 0:1][0, 0] > 0, nx - 1, 0)
    decay, source = decay_ref[last, mine, :], source_ref[last, mine, :]
    got_decay, got_source = got_ref[0], got_ref[1]
    near_decay = jnp.where(first, decay, got_decay)
    near_source = jnp.where(first, source, got_source)
    far_decay = jnp.where(first, got_decay, decay)
    far_source = jnp.where(first, got_source, source)
    chip_decay, chip_source = far_decay * near_decay, far_decay * near_source + far_source
    near_ref[0], near_ref[1] = near_decay, near_source
    if chip_ref:
        chip_ref[0][0], chip_ref[0][1] = chip_decay, chip_source
    entry = inflow_ref[mine, :]
    entry_ref[...] = entry
    face_ref[...] = chip_decay * entry + chip_source


def compose_chip(nx, sign, got, decay, source, inflow):
    _, half, lanes = got.shape
    whole = pl.BlockSpec(memory_space=pltpu.VMEM)
    pair = pltpu.VMEM((2, half, lanes), jnp.float32)
    outs = [pair] + [pltpu.VMEM((half, lanes), jnp.float32)] * 2
    if lax.axis_size("gx") > 4:
        outs.append(pair)
    return pl.pallas_call(
        functools.partial(compose_kernel, nx),
        in_specs=[whole] * 5,
        out_specs=[whole] * len(outs),
        out_shape=outs,
        compiler_params=params(),
        cost_estimate=cost(10 * half * lanes, 40 * half * lanes),
        name="compose",
    )(sign, got, decay, source, inflow)


def pass_kernel(step, sign_ref, got_ref, entry_ref, chip_ref, next_ref, face_ref):
    _, before = standing(sign_ref)
    entry = jnp.where(before == step, got_ref[...], entry_ref[...])
    next_ref[...] = entry
    face_ref[...] = chip_ref[0] * entry + chip_ref[1]


def pass_face(step, sign, got, entry, chip):
    whole = pl.BlockSpec(memory_space=pltpu.VMEM)
    out = pltpu.VMEM(entry.shape, jnp.float32)
    return pl.pallas_call(
        functools.partial(pass_kernel, step),
        in_specs=[whole] * 4,
        out_specs=[whole] * 2,
        out_shape=[out, out],
        compiler_params=params(),
        cost_estimate=cost(3 * entry.size, 20 * entry.size),
        name="face",
    )(sign, got, entry, chip)


def share_kernel(step, sign_ref, got_ref, entry_ref, near_ref, keep_ref, send_ref):
    first, before = standing(sign_ref)
    entry = jnp.where(before == step, got_ref[...], entry_ref[...])
    middle = near_ref[0] * entry + near_ref[1]
    keep_ref[...] = jnp.where(first, entry, middle)
    send_ref[...] = jnp.where(first, middle, entry)


def share_entry(step, sign, got, entry, near):
    whole = pl.BlockSpec(memory_space=pltpu.VMEM)
    out = pltpu.VMEM(entry.shape, jnp.float32)
    return pl.pallas_call(
        functools.partial(share_kernel, step),
        in_specs=[whole] * 4,
        out_specs=[whole] * 2,
        out_shape=[out, out],
        compiler_params=params(),
        cost_estimate=cost(3 * entry.size, 20 * entry.size),
        name="share",
    )(sign, got, entry, near)


def chip_exchange(a):
    n = lax.axis_size("gx")
    return lax.ppermute(a, "gx", [(i, i ^ 1) for i in range(n)])


def chip_hop(face, step):
    chips = lax.axis_size("gx") // 2
    up, down = (step, step + 1), (chips - 1 - step, chips - 2 - step)
    pairs = [(2 * a + c, 2 * b + c) for a, b in (up, down) for c in range(2)]
    if chips % 2 == 0:
        got = lax.ppermute(face, "gx", pairs)
        return got, got
    return lax.ppermute(face, "gx", pairs[:2]), lax.ppermute(face, "gx", pairs[2:])


def entries(nx, sign, decay, source, send, inflow, side):
    near, face, entry, *chip = compose_chip(nx, sign, chip_exchange(send), decay, source, inflow)
    got = entry
    chips = lax.axis_size("gx") // 2
    for step in range(chips - 1):
        if step > 0:
            entry, face = pass_face(step, sign, got, entry, chip[0])
        low, high = chip_hop(face, step)
        got = low if low is high else jnp.where(side[0] == 1, low, high)
    keep, share = share_entry(chips - 1, sign, got, entry, near)
    return keep, chip_exchange(share)


def whole_entry(keep_ref, got_ref, entry_ref):
    count = entry_ref.shape[0]
    core = lax.axis_index("gx") % 2
    entry_ref[half_of(count, core), :] = keep_ref[...]
    entry_ref[half_of(count, 1 - core), :] = got_ref[...]


def new_moments_kernel(nx, keep_ref, got_ref, table_ref, decay_ref, source_ref, mom_ref, entry_ref):
    whole_entry(keep_ref, got_ref, entry_ref)
    entry = entry_ref[...]
    lanes = entry.shape[1]
    table = table_ref[...]
    for i in range(0, nx, 2):
        pair = range(min(2, nx - i))
        planes = [decay_ref[i + k] * entry + source_ref[i + k] for k in pair]
        got = project(table, jnp.concatenate(planes, axis=1))
        for k in pair:
            mom_ref[pl.ds(i + k, NMOM, stride=nx), :] = got[:NMOM, k * lanes : (k + 1) * lanes]


def new_moments(nx, keep, got, table, decay, source):
    count, lanes = decay.shape[1:]
    whole = pl.BlockSpec(memory_space=pltpu.VMEM)
    return pl.pallas_call(
        functools.partial(new_moments_kernel, nx),
        in_specs=[whole] * 5,
        out_specs=[whole] * 2,
        out_shape=[pltpu.VMEM((NMOM * nx, lanes), jnp.float32), pltpu.VMEM((count, lanes), jnp.float32)],
        compiler_params=params(),
        cost_estimate=cost(2 * 48 * count * nx * lanes, 8 * count * nx * lanes),
        name="new_moments",
    )(keep, got, table, decay, source)


def write_kernel(nx, entry_ref, decay_ref, source_ref, dist_ref):
    entry = entry_ref[...]
    count = entry.shape[0]
    for i in range(nx):
        dist_ref[pl.ds(i, count, stride=nx), :] = decay_ref[i] * entry + source_ref[i]


def write_dist(nx, entry, decay, source):
    count, lanes = entry.shape
    chunk = min(count, 128)
    field = pl.BlockSpec((nx, chunk, lanes), lambda i: (0, i, 0))
    return pl.pallas_call(
        functools.partial(write_kernel, nx),
        grid=(count // chunk,),
        in_specs=[pl.BlockSpec((chunk, lanes), lambda i: (i, 0)), field, field],
        out_specs=pl.BlockSpec((chunk * nx, lanes), lambda i: (i, 0)),
        out_shape=jax.ShapeDtypeStruct((count * nx, lanes), jnp.float32),
        compiler_params=params(),
        cost_estimate=cost(2 * count * nx * lanes, 12 * count * nx * lanes),
        name="write_dist",
    )(entry, decay, source)


def stages_of(n):
    out, bit = [], 1
    while bit < n:
        if bit * 4 <= n:
            out.append((bit, 2 * bit, 3 * bit))
            bit *= 4
        else:
            out.append((bit,))
            bit *= 2
    return out


def exchange(a, axis, mask):
    n = lax.axis_size(axis)
    return lax.ppermute(a, axis, [(i, i ^ mask) for i in range(n)])


def partial_sums(a, axis, beside=()):
    n = lax.axis_size(axis)
    beside = list(beside)
    if n & (n - 1) or n == 1:
        total = lax.psum(a, axis)
        return (total, jnp.zeros_like(total)), [f(a) for f in beside]
    stages = stages_of(n)
    done = []
    for i, masks in enumerate(stages):
        got = [exchange(a, axis, m) for m in masks]
        take = beside if i == len(stages) - 1 else beside[:1]
        beside = beside[len(take) :]
        made = [f(a) for f in take]
        got, made = lax.optimization_barrier((got, made))
        done += made
        other = functools.reduce(jnp.add, got)
        if i == len(stages) - 1:
            return (a, other), done
        a = a + other


def local(total, dist, inflow, speed_x, transverse, quad_weight, side):
    count, nx, lanes = dist.shape
    flat = dist.reshape(count * nx, lanes)
    row = lambda a: a.reshape(1, count)
    partial, table, rows, held = old_moments(total, nx, row(side), row(speed_x), transverse, row(quad_weight), flat)
    halves = 2 if count % 256 == 0 else 1

    def slope_part(h):
        return lambda sent: slopes(nx, h, halves, *lax.optimization_barrier((rows, held, sent))[:2])

    (ma, mb), made = partial_sums(partial, "vert", [slope_part(h) for h in range(halves)])
    decay, source, send, sign = maps(nx, ma, mb, [m[1] for m in made], [m[0] for m in made])
    keep, got = entries(nx, sign, decay, source, send, inflow, side)
    new_partial, entry = new_moments(nx, keep, got, table, decay, source)

    def write(sent):
        return write_dist(nx, *lax.optimization_barrier((entry, decay, source, sent))[:3])

    (na, nb), (new_flat,) = partial_sums(new_partial, "vert", [write])
    return new_flat.reshape(count, nx, lanes), (na + nb).reshape(NMOM, nx, lanes)


def solution(mesh):
    def whole(dist, inflow, speed_x, transverse, quad_weight, side):
        body = functools.partial(local, dist.shape[0])
        return jax.shard_map(
            body,
            mesh=mesh,
            in_specs=(P("vert", "gx", None), P("vert", None), P("vert"), P(None, "vert"), P("vert"), P("vert")),
            out_specs=(P("vert", "gx", None), P(None, "gx", None)),
            check_vma=False,
        )(dist, inflow, speed_x, transverse, quad_weight, side)

    return whole
```

```python
import functools

import jax
import jax.numpy as jnp
from jax import lax
from jax.experimental import pallas as pl
from jax.experimental.pallas import tpu as pltpu
from jax.sharding import PartitionSpec as P

NZ = 32
KAPPA_CELL = 0.02
LOG2E = 1.4426950408889634
SHEAR = 0.19
NMOM = 13
ROWS = 16
TERMS = 5
DEPTH = 128


def params(**kw):
    return pltpu.CompilerParams(vmem_limit_bytes=20 * 1024 * 1024, **kw)


def cost(flops, nbytes):
    return pl.CostEstimate(flops=flops, bytes_accessed=nbytes, transcendentals=0)


def split(a):
    high = a.astype(jnp.bfloat16)
    low = (a - high.astype(jnp.float32)).astype(jnp.bfloat16)
    return high, low


def split3(a):
    high, rest = split(a)
    mid, low = split(a - high.astype(jnp.float32))
    return [high.astype(jnp.float32), mid.astype(jnp.float32), low.astype(jnp.float32)]


def project(table, plane):
    high, low = split(plane)
    first = jnp.dot(table, high, preferred_element_type=jnp.float32)
    second = jnp.dot(table[:ROWS], low, preferred_element_type=jnp.float32)
    return first[:ROWS] + first[ROWS:] + second


def moments_kernel(total, nx, chunks, side_hbm, speed_hbm, cross_hbm, weight_hbm, dist_hbm,
                   mom_ref, table_ref, rows_ref, dist_ref, side_ref, speed_ref, cross_ref, weight_ref, sems):
    count = speed_ref.shape[1]
    chunk = count // chunks
    small = [(side_hbm, side_ref), (speed_hbm, speed_ref), (cross_hbm, cross_ref), (weight_hbm, weight_ref)]
    copies = [pltpu.make_async_copy(a, b, sems.at[chunks + i]) for i, (a, b) in enumerate(small)]
    parts = []
    for i in range(chunks):
        rows = pl.ds(i * chunk * nx, chunk * nx)
        parts.append(pltpu.make_async_copy(dist_hbm.at[rows, :], dist_ref.at[rows, :], sems.at[i]))
    for c in copies + parts:
        c.start()
    for c in copies:
        c.wait()
    speed = speed_ref[...]
    x = jnp.where(side_ref[...] == 1, speed, -speed)
    y = cross_ref[0:1, :]
    z = cross_ref[1:2, :]
    xx, yy, zz = x * x, y * y, z * z
    square = xx + yy + zz
    rows_ref[...] = jnp.concatenate([x, y, z] + [jnp.zeros_like(x)] * 5, axis=0)
    rows = [jnp.ones_like(x), x, y, z, xx, yy, zz, x * y, x * z, y * z, x * square, y * square, z * square]
    rows += [jnp.zeros_like(x)] * (ROWS - NMOM)
    full = jnp.concatenate(rows, axis=0) * (weight_ref[...] * (1.0 / total))
    high, low = split(full)
    table = jnp.concatenate([high, low], axis=0)
    table_ref[...] = table
    for c in range(chunks):
        parts[c].wait()
        tab = table[:, c * chunk : (c + 1) * chunk]
        for i in range(0, nx, 2):
            pair = range(min(2, nx - i))
            planes = [dist_ref[pl.ds(c * chunk * nx + i + k, chunk, stride=nx), :] for k in pair]
            lanes = planes[0].shape[1]
            got = project(tab, jnp.concatenate(planes, axis=1))
            for k in pair:
                part = got[:NMOM, k * lanes : (k + 1) * lanes]
                place = pl.ds(i + k, NMOM, stride=nx)
                if c == 0:
                    mom_ref[place, :] = part
                else:
                    mom_ref[place, :] += part


def old_moments(total, nx, side, speed, cross, weight, dist):
    count, lanes = speed.shape[1], dist.shape[1]
    chunks = max(1, count // 256)
    whole = pl.BlockSpec(memory_space=pltpu.VMEM)
    return pl.pallas_call(
        functools.partial(moments_kernel, total, nx, chunks),
        in_specs=[pl.BlockSpec(memory_space=pltpu.HBM)] * 5,
        out_specs=[whole] * 4,
        out_shape=[
            pltpu.VMEM((NMOM * nx, lanes), jnp.float32),
            pltpu.VMEM((2 * ROWS, count), jnp.bfloat16),
            pltpu.VMEM((8, count), jnp.float32),
            pltpu.VMEM(dist.shape, jnp.float32),
        ],
        scratch_shapes=[
            pltpu.VMEM(side.shape, jnp.int32),
            pltpu.VMEM(speed.shape, jnp.float32),
            pltpu.VMEM(cross.shape, jnp.float32),
            pltpu.VMEM(weight.shape, jnp.float32),
            pltpu.SemaphoreType.DMA((chunks + 4,)),
        ],
        compiler_params=params(),
        cost_estimate=cost(2 * 48 * count * nx * lanes, 4 * count * nx * lanes),
        name="moments",
    )(*[pltpu.with_memory_space_constraint(a, pltpu.HBM) for a in (side, speed, cross, weight, dist)])


def slope_kernel(nx, start, rows_ref, dist_ref, slope_ref, speed_ref, feature_ref, comp_ref):
    count = slope_ref.shape[1]
    lanes = dist_ref.shape[1]
    rows = rows_ref[:, start : start + count]
    columns = jnp.transpose(rows)
    speed_ref[...] = jnp.broadcast_to(jnp.abs(columns[:, 0:1]), (count, lanes))
    for k in range(2):
        comp_ref[k] = jnp.broadcast_to(columns[:, k + 1 : k + 2], (count, lanes))
    x, y, z = rows[0:1], rows[1:2], rows[2:3]
    high, mid, low = split3(jnp.concatenate([x * x + y * y + z * z, x, y, z, jnp.ones_like(x)], axis=0))
    terms = jnp.concatenate([high, high, mid, mid, high, low], axis=0)
    terms = jnp.concatenate([terms, jnp.zeros((DEPTH - 6 * TERMS, count), jnp.float32)], axis=0)
    feature_ref[...] = jnp.transpose(terms).astype(jnp.bfloat16)
    group = 32

    def one(g, carry):
        at = pl.multiple_of(g * group, group)
        y = comp_ref[0, pl.ds(at, group), :]
        z = comp_ref[1, pl.ds(at, group), :]
        lane = lax.broadcasted_iota(jnp.int32, (group, lanes), 1)
        from_y = jnp.where(y > 0, lane + (lanes - NZ), lane + NZ) & (lanes - 1)
        from_z = (lane & ~(NZ - 1)) | (jnp.where(z > 0, lane + (NZ - 1), lane + 1) & (NZ - 1))
        ay, az = KAPPA_CELL * jnp.abs(y), KAPPA_CELL * jnp.abs(z)
        both = ay + az
        for i in range(nx):
            d = dist_ref[pl.ds((start + at) * nx + i, group, stride=nx), :]
            near_y = jnp.take_along_axis(d, from_y, axis=1)
            near_z = jnp.take_along_axis(d, from_z, axis=1)
            slope_ref[i, pl.ds(at, group), :] = both * d - ay * near_y - az * near_z
        return carry

    lax.fori_loop(0, count // group, one, 0)


def slopes(nx, half, halves, rows, dist):
    count, lanes = rows.shape[1] // halves, dist.shape[1]
    whole = pl.BlockSpec(memory_space=pltpu.VMEM)
    return pl.pallas_call(
        functools.partial(slope_kernel, nx, half * count),
        in_specs=[whole] * 2,
        out_specs=[whole] * 3,
        out_shape=[
            pltpu.VMEM((nx, count, lanes), jnp.float32),
            pltpu.VMEM((count, lanes), jnp.float32),
            pltpu.VMEM((count, DEPTH), jnp.bfloat16),
        ],
        scratch_shapes=[pltpu.VMEM((2, count, lanes), jnp.float32)],
        compiler_params=params(),
        cost_estimate=cost(20 * count * nx * lanes, 8 * count * nx * lanes),
        name="slope",
    )(rows, dist)


def map_kernel(nx, halves, ma_ref, mb_ref, rows_ref, *refs):
    slopes_in, speeds, features = (refs[i * halves : (i + 1) * halves] for i in range(3))
    decay_ref, source_ref, send_ref, sign_ref, state, bulk_terms, flux_terms = refs[3 * halves :]
    count, lanes = decay_ref.shape[1:]
    part = count // halves
    m = [ma_ref[k * nx : (k + 1) * nx, :] + mb_ref[k * nx : (k + 1) * nx, :] for k in range(NMOM)]
    n = m[0]
    inv_n = 1.0 / n
    u = [m[1] * inv_n, m[2] * inv_n, m[3] * inv_n]
    energy = m[4] + m[5] + m[6]
    uu = u[0] * u[0] + u[1] * u[1] + u[2] * u[2]
    temp = (energy * inv_n - uu) * (1.0 / 3.0)
    second = ((m[4], m[7], m[8]), (m[7], m[5], m[9]), (m[8], m[9], m[6]))
    inv_t = 1.0 / temp
    nu = KAPPA_CELL * n * jnp.exp(SHEAR * jnp.log(temp))
    rate = inv_t * (-0.5 * LOG2E)
    ratio = -2.0 / LOG2E
    flux_scale = inv_n * inv_t * inv_t * (ratio / 15.0)
    q = []
    for k in range(3):
        inner = u[0] * second[k][0] + u[1] * second[k][1] + u[2] * second[k][2]
        q.append(0.5 * flux_scale * (m[10 + k] - 2.0 * inner - u[k] * energy + 2.0 * n * u[k] * uu))
    twice = -2.0 * rate
    bulk = [rate, twice * u[0], twice * u[1], twice * u[2], rate * uu]
    flux = [jnp.zeros_like(n), q[0], q[1], q[2], -(u[0] * q[0] + u[1] * q[1] + u[2] * q[2])]
    for terms, ref in ((bulk, bulk_terms), (flux, flux_terms)):
        for k in range(TERMS):
            high, mid, low = split3(terms[k])
            for i, one in enumerate((high, mid, high, mid, low, high)):
                ref[(i * TERMS + k) * nx : (i * TERMS + k + 1) * nx, :] = one
        ref[6 * TERMS * nx :, :] = jnp.zeros(((32 - 6 * TERMS) * nx, lanes), jnp.float32)
    state[0] = nu * n * inv_t * jnp.sqrt(inv_t)
    state[1] = nu
    sign_ref[...] = jnp.broadcast_to(rows_ref[0:1, 0:1], (8, lanes))
    forward = rows_ref[0:1, 0:1][0, 0] > 0
    rest = jnp.zeros((DEPTH - 32, 2 * lanes), jnp.bfloat16)
    group = 32

    for j in range(nx):
        at_x = jnp.where(forward, j, nx - 1 - j)
        before = jnp.where(forward, j - 1, nx - j)
        scale = jnp.broadcast_to(state[0, pl.ds(at_x, 1), :], (group, lanes))
        rate_x = jnp.broadcast_to(state[1, pl.ds(at_x, 1), :], (group, lanes))
        cells = jnp.concatenate([ref[pl.ds(at_x, 32, stride=nx), :] for ref in (bulk_terms, flux_terms)], axis=1)
        cells = jnp.concatenate([cells.astype(jnp.bfloat16), rest], axis=0)
        for h in range(halves):
            both = jnp.dot(features[h][...], cells, preferred_element_type=jnp.float32)
            for at in range(0, part, group):
                own = slice(at, at + group)
                rows = slice(h * part + at, h * part + at + group)
                exponent, wq = both[own, :lanes], both[own, lanes:]
                shape = 1.0 + wq * (exponent - 5.0 / ratio)
                target = scale * jnp.exp2(exponent) * shape
                speed = speeds[h][own, :]
                inv = 1.0 / (speed + rate_x)
                decay = speed * inv
                source = (target - slopes_in[h][at_x, own, :]) * inv
                if j > 0:
                    source = decay * source_ref[before, rows, :] + source
                    decay = decay * decay_ref[before, rows, :]
                decay_ref[at_x, rows, :] = decay
                source_ref[at_x, rows, :] = source

    last = jnp.where(forward, nx - 1, 0)
    theirs = pl.ds(pl.multiple_of((1 - lax.axis_index("gx") % 2) * (count // 2), count // 2), count // 2)
    send_ref[0] = decay_ref[last, theirs, :]
    send_ref[1] = source_ref[last, theirs, :]


def maps(nx, ma, mb, rows, parts):
    lanes = ma.shape[1]
    halves, count = len(parts), rows.shape[1]
    whole = pl.BlockSpec(memory_space=pltpu.VMEM)
    field = pltpu.VMEM((nx, count, lanes), jnp.float32)
    return pl.pallas_call(
        functools.partial(map_kernel, nx, halves),
        in_specs=[whole] * (3 + 3 * halves),
        out_specs=[whole] * 4,
        out_shape=[
            field,
            field,
            pltpu.VMEM((2, count // 2, lanes), jnp.float32),
            pltpu.VMEM((8, lanes), jnp.float32),
        ],
        scratch_shapes=[
            pltpu.VMEM((2, nx, lanes), jnp.float32),
            pltpu.VMEM((32 * nx, lanes), jnp.float32),
            pltpu.VMEM((32 * nx, lanes), jnp.float32),
        ],
        compiler_params=params(),
        cost_estimate=cost(40 * count * nx * lanes, 12 * count * nx * lanes),
        name="maps",
    )(ma, mb, rows, *[p[i] for i in range(3) for p in parts])


def standing(sign_ref):
    place, chips = lax.axis_index("gx"), lax.axis_size("gx") // 2
    chip, core = place // 2, place % 2
    forward = sign_ref[0:1, :] > 0
    return jnp.where(forward, core, 1 - core) == 0, jnp.where(forward, chip, chips - 1 - chip)


def half_of(ref_rows, which):
    half = ref_rows // 2
    return pl.ds(pl.multiple_of(which * half, half), half)


def compose_kernel(nx, sign_ref, got_ref, decay_ref, source_ref, inflow_ref, near_ref, face_ref, entry_ref, *chip_ref):
    first, _ = standing(sign_ref)
    core = lax.axis_index("gx") % 2
    mine = half_of(inflow_ref.shape[0], core)
    last = jnp.where(sign_ref[0:1, 0:1][0, 0] > 0, nx - 1, 0)
    decay, source = decay_ref[last, mine, :], source_ref[last, mine, :]
    got_decay, got_source = got_ref[0], got_ref[1]
    near_decay = jnp.where(first, decay, got_decay)
    near_source = jnp.where(first, source, got_source)
    far_decay = jnp.where(first, got_decay, decay)
    far_source = jnp.where(first, got_source, source)
    chip_decay, chip_source = far_decay * near_decay, far_decay * near_source + far_source
    near_ref[0], near_ref[1] = near_decay, near_source
    if chip_ref:
        chip_ref[0][0], chip_ref[0][1] = chip_decay, chip_source
    entry = inflow_ref[mine, :]
    entry_ref[...] = entry
    face_ref[...] = chip_decay * entry + chip_source


def compose_chip(nx, sign, got, decay, source, inflow):
    _, half, lanes = got.shape
    whole = pl.BlockSpec(memory_space=pltpu.VMEM)
    pair = pltpu.VMEM((2, half, lanes), jnp.float32)
    outs = [pair] + [pltpu.VMEM((half, lanes), jnp.float32)] * 2
    if lax.axis_size("gx") > 4:
        outs.append(pair)
    return pl.pallas_call(
        functools.partial(compose_kernel, nx),
        in_specs=[whole] * 5,
        out_specs=[whole] * len(outs),
        out_shape=outs,
        compiler_params=params(),
        cost_estimate=cost(10 * half * lanes, 40 * half * lanes),
        name="compose",
    )(sign, got, decay, source, inflow)


def pass_kernel(step, sign_ref, got_ref, entry_ref, chip_ref, next_ref, face_ref):
    _, before = standing(sign_ref)
    entry = jnp.where(before == step, got_ref[...], entry_ref[...])
    next_ref[...] = entry
    face_ref[...] = chip_ref[0] * entry + chip_ref[1]


def pass_face(step, sign, got, entry, chip):
    whole = pl.BlockSpec(memory_space=pltpu.VMEM)
    out = pltpu.VMEM(entry.shape, jnp.float32)
    return pl.pallas_call(
        functools.partial(pass_kernel, step),
        in_specs=[whole] * 4,
        out_specs=[whole] * 2,
        out_shape=[out, out],
        compiler_params=params(),
        cost_estimate=cost(3 * entry.size, 20 * entry.size),
        name="face",
    )(sign, got, entry, chip)


def share_kernel(step, sign_ref, got_ref, entry_ref, near_ref, keep_ref, send_ref):
    first, before = standing(sign_ref)
    entry = jnp.where(before == step, got_ref[...], entry_ref[...])
    middle = near_ref[0] * entry + near_ref[1]
    keep_ref[...] = jnp.where(first, entry, middle)
    send_ref[...] = jnp.where(first, middle, entry)


def share_entry(step, sign, got, entry, near):
    whole = pl.BlockSpec(memory_space=pltpu.VMEM)
    out = pltpu.VMEM(entry.shape, jnp.float32)
    return pl.pallas_call(
        functools.partial(share_kernel, step),
        in_specs=[whole] * 4,
        out_specs=[whole] * 2,
        out_shape=[out, out],
        compiler_params=params(),
        cost_estimate=cost(3 * entry.size, 20 * entry.size),
        name="share",
    )(sign, got, entry, near)


def chip_exchange(a):
    n = lax.axis_size("gx")
    return lax.ppermute(a, "gx", [(i, i ^ 1) for i in range(n)])


def chip_hop(face, step):
    chips = lax.axis_size("gx") // 2
    up, down = (step, step + 1), (chips - 1 - step, chips - 2 - step)
    pairs = [(2 * a + c, 2 * b + c) for a, b in (up, down) for c in range(2)]
    if chips % 2 == 0:
        got = lax.ppermute(face, "gx", pairs)
        return got, got
    return lax.ppermute(face, "gx", pairs[:2]), lax.ppermute(face, "gx", pairs[2:])


def entries(nx, sign, decay, source, send, inflow, side):
    near, face, entry, *chip = compose_chip(nx, sign, chip_exchange(send), decay, source, inflow)
    got = entry
    chips = lax.axis_size("gx") // 2
    for step in range(chips - 1):
        if step > 0:
            entry, face = pass_face(step, sign, got, entry, chip[0])
        low, high = chip_hop(face, step)
        got = low if low is high else jnp.where(side[0] == 1, low, high)
    keep, share = share_entry(chips - 1, sign, got, entry, near)
    return keep, chip_exchange(share)


def whole_entry(keep_ref, got_ref, entry_ref):
    count = entry_ref.shape[0]
    core = lax.axis_index("gx") % 2
    entry_ref[half_of(count, core), :] = keep_ref[...]
    entry_ref[half_of(count, 1 - core), :] = got_ref[...]


def new_moments_kernel(nx, keep_ref, got_ref, table_ref, decay_ref, source_ref, mom_ref, entry_ref):
    whole_entry(keep_ref, got_ref, entry_ref)
    entry = entry_ref[...]
    lanes = entry.shape[1]
    table = table_ref[...]
    for i in range(0, nx, 2):
        pair = range(min(2, nx - i))
        planes = [decay_ref[i + k] * entry + source_ref[i + k] for k in pair]
        got = project(table, jnp.concatenate(planes, axis=1))
        for k in pair:
            mom_ref[pl.ds(i + k, NMOM, stride=nx), :] = got[:NMOM, k * lanes : (k + 1) * lanes]


def new_moments(nx, keep, got, table, decay, source):
    count, lanes = decay.shape[1:]
    whole = pl.BlockSpec(memory_space=pltpu.VMEM)
    return pl.pallas_call(
        functools.partial(new_moments_kernel, nx),
        in_specs=[whole] * 5,
        out_specs=[whole] * 2,
        out_shape=[pltpu.VMEM((NMOM * nx, lanes), jnp.float32), pltpu.VMEM((count, lanes), jnp.float32)],
        compiler_params=params(),
        cost_estimate=cost(2 * 48 * count * nx * lanes, 8 * count * nx * lanes),
        name="new_moments",
    )(keep, got, table, decay, source)


def write_kernel(nx, entry_ref, decay_ref, source_ref, dist_ref):
    entry = entry_ref[...]
    count = entry.shape[0]
    for i in range(nx):
        dist_ref[pl.ds(i, count, stride=nx), :] = decay_ref[i] * entry + source_ref[i]


def write_dist(nx, entry, decay, source):
    count, lanes = entry.shape
    chunk = min(count, 128)
    field = pl.BlockSpec((nx, chunk, lanes), lambda i: (0, i, 0))
    return pl.pallas_call(
        functools.partial(write_kernel, nx),
        grid=(count // chunk,),
        in_specs=[pl.BlockSpec((chunk, lanes), lambda i: (i, 0)), field, field],
        out_specs=pl.BlockSpec((chunk * nx, lanes), lambda i: (i, 0)),
        out_shape=jax.ShapeDtypeStruct((count * nx, lanes), jnp.float32),
        compiler_params=params(),
        cost_estimate=cost(2 * count * nx * lanes, 12 * count * nx * lanes),
        name="write_dist",
    )(entry, decay, source)


def stages_of(n):
    out, bit = [], 1
    while bit < n:
        if bit * 4 <= n:
            out.append((bit, 2 * bit, 3 * bit))
            bit *= 4
        else:
            out.append((bit,))
            bit *= 2
    return out


def exchange(a, axis, mask):
    n = lax.axis_size(axis)
    return lax.ppermute(a, axis, [(i, i ^ mask) for i in range(n)])


def partial_sums(a, axis, beside=()):
    n = lax.axis_size(axis)
    beside = list(beside)
    if n & (n - 1) or n == 1:
        total = lax.psum(a, axis)
        return (total, jnp.zeros_like(total)), [f(a) for f in beside]
    stages = stages_of(n)
    done = []
    for i, masks in enumerate(stages):
        got = [exchange(a, axis, m) for m in masks]
        take = beside if i == len(stages) - 1 else beside[:1]
        beside = beside[len(take) :]
        made = [f(a) for f in take]
        got, made = lax.optimization_barrier((got, made))
        done += made
        other = functools.reduce(jnp.add, got)
        if i == len(stages) - 1:
            return (a, other), done
        a = a + other


def local(total, dist, inflow, speed_x, transverse, quad_weight, side):
    count, nx, lanes = dist.shape
    flat = dist.reshape(count * nx, lanes)
    row = lambda a: a.reshape(1, count)
    partial, table, rows, held = old_moments(total, nx, row(side), row(speed_x), transverse, row(quad_weight), flat)
    halves = 2 if count % 256 == 0 else 1

    def slope_part(h):
        return lambda sent: slopes(nx, h, halves, *lax.optimization_barrier((rows, held, sent))[:2])

    (ma, mb), made = partial_sums(partial, "vert", [slope_part(h) for h in range(halves)])
    decay, source, send, sign = maps(nx, ma, mb, rows, made)
    keep, got = entries(nx, sign, decay, source, send, inflow, side)
    new_partial, entry = new_moments(nx, keep, got, table, decay, source)

    def write(sent):
        return write_dist(nx, *lax.optimization_barrier((entry, decay, source, sent))[:3])

    (na, nb), (new_flat,) = partial_sums(new_partial, "vert", [write])
    return new_flat.reshape(count, nx, lanes), (na + nb).reshape(NMOM, nx, lanes)


def solution(mesh):
    def whole(dist, inflow, speed_x, transverse, quad_weight, side):
        body = functools.partial(local, dist.shape[0])
        return jax.shard_map(
            body,
            mesh=mesh,
            in_specs=(P("vert", "gx", None), P("vert", None), P("vert"), P(None, "vert"), P("vert"), P("vert")),
            out_specs=(P("vert", "gx", None), P(None, "gx", None)),
            check_vma=False,
        )(dist, inflow, speed_x, transverse, quad_weight, side)

    return whole
```

```python
import functools

import jax
import jax.numpy as jnp
from jax import lax
from jax.experimental import pallas as pl
from jax.experimental.pallas import tpu as pltpu
from jax.sharding import PartitionSpec as P

NZ = 32
KAPPA_CELL = 0.02
LOG2E = 1.4426950408889634
RATIO = -2.0 / LOG2E
SHEAR = 0.19
NMOM = 13
ROWS = 16
TERMS = 5
DEPTH = 128


def params(**kw):
    return pltpu.CompilerParams(vmem_limit_bytes=20 * 1024 * 1024, **kw)


def cost(flops, nbytes):
    return pl.CostEstimate(flops=flops, bytes_accessed=nbytes, transcendentals=0)


def split(a):
    high = a.astype(jnp.bfloat16)
    low = (a - high.astype(jnp.float32)).astype(jnp.bfloat16)
    return high, low


def split3(a):
    high, rest = split(a)
    mid, low = split(a - high.astype(jnp.float32))
    return [high.astype(jnp.float32), mid.astype(jnp.float32), low.astype(jnp.float32)]


def project(table, plane):
    high, low = split(plane)
    first = jnp.dot(table, high, preferred_element_type=jnp.float32)
    second = jnp.dot(table[:ROWS], low, preferred_element_type=jnp.float32)
    return first[:ROWS] + first[ROWS:] + second


def moments_kernel(total, nx, chunks, side_hbm, speed_hbm, cross_hbm, weight_hbm, dist_hbm,
                   mom_ref, table_ref, rows_ref, dist_ref, side_ref, speed_ref, cross_ref, weight_ref, sems):
    count = speed_ref.shape[1]
    chunk = count // chunks
    small = [(side_hbm, side_ref), (speed_hbm, speed_ref), (cross_hbm, cross_ref), (weight_hbm, weight_ref)]
    copies = [pltpu.make_async_copy(a, b, sems.at[chunks + i]) for i, (a, b) in enumerate(small)]
    parts = []
    for i in range(chunks):
        rows = pl.ds(i * chunk * nx, chunk * nx)
        parts.append(pltpu.make_async_copy(dist_hbm.at[rows, :], dist_ref.at[rows, :], sems.at[i]))
    for c in copies + parts:
        c.start()
    for c in copies:
        c.wait()
    speed = speed_ref[...]
    x = jnp.where(side_ref[...] == 1, speed, -speed)
    y = cross_ref[0:1, :]
    z = cross_ref[1:2, :]
    xx, yy, zz = x * x, y * y, z * z
    square = xx + yy + zz
    stacked = jnp.concatenate([x, y, z] + [jnp.zeros_like(x)] * 5, axis=0)
    for h in range(2):
        rows_ref[h] = stacked[:, h * (count // 2) : (h + 1) * (count // 2)]
    rows = [jnp.ones_like(x), x, y, z, xx, yy, zz, x * y, x * z, y * z, x * square, y * square, z * square]
    rows += [jnp.zeros_like(x)] * (ROWS - NMOM)
    full = jnp.concatenate(rows, axis=0) * (weight_ref[...] * (1.0 / total))
    high, low = split(full)
    table = jnp.concatenate([high, low], axis=0)
    for h in range(2):
        table_ref[h] = table[:, h * (count // 2) : (h + 1) * (count // 2)]
    for c in range(chunks):
        parts[c].wait()
        tab = table[:, c * chunk : (c + 1) * chunk]
        for i in range(0, nx, 2):
            pair = range(min(2, nx - i))
            planes = [dist_ref[pl.ds(c * chunk * nx + i + k, chunk, stride=nx), :] for k in pair]
            lanes = planes[0].shape[1]
            got = project(tab, jnp.concatenate(planes, axis=1))
            for k in pair:
                part = got[:NMOM, k * lanes : (k + 1) * lanes]
                place = pl.ds(i + k, NMOM, stride=nx)
                if c == 0:
                    mom_ref[place, :] = part
                else:
                    mom_ref[place, :] += part


def old_moments(total, nx, side, speed, cross, weight, dist):
    count, lanes = speed.shape[1], dist.shape[1]
    chunks = max(1, count // 256)
    whole = pl.BlockSpec(memory_space=pltpu.VMEM)
    return pl.pallas_call(
        functools.partial(moments_kernel, total, nx, chunks),
        in_specs=[pl.BlockSpec(memory_space=pltpu.HBM)] * 5,
        out_specs=[whole] * 4,
        out_shape=[
            pltpu.VMEM((NMOM * nx, lanes), jnp.float32),
            pltpu.VMEM((2, 2 * ROWS, count // 2), jnp.bfloat16),
            pltpu.VMEM((2, 8, count // 2), jnp.float32),
            pltpu.VMEM(dist.shape, jnp.float32),
        ],
        scratch_shapes=[
            pltpu.VMEM(side.shape, jnp.int32),
            pltpu.VMEM(speed.shape, jnp.float32),
            pltpu.VMEM(cross.shape, jnp.float32),
            pltpu.VMEM(weight.shape, jnp.float32),
            pltpu.SemaphoreType.DMA((chunks + 4,)),
        ],
        compiler_params=params(),
        cost_estimate=cost(2 * 48 * count * nx * lanes, 4 * count * nx * lanes),
        name="moments",
    )(*[pltpu.with_memory_space_constraint(a, pltpu.HBM) for a in (side, speed, cross, weight, dist)])


def half_index(own):
    core = lax.axis_index("gx") % 2
    return core if own else 1 - core


def slope_kernel(nx, own, rows_ref, dist_ref, slope_ref, speed_ref, feature_ref, comp_ref):
    count = slope_ref.shape[1]
    lanes = dist_ref.shape[1]
    half = half_index(own)
    start = pl.multiple_of(half * count, count)
    rows = rows_ref[half]
    columns = jnp.transpose(rows)
    speed_ref[...] = jnp.broadcast_to(jnp.abs(columns[:, 0:1]), (count, lanes))
    for k in range(2):
        comp_ref[k] = jnp.broadcast_to(columns[:, k + 1 : k + 2], (count, lanes))
    x, y, z = rows[0:1], rows[1:2], rows[2:3]
    high, mid, low = split3(jnp.concatenate([x * x + y * y + z * z, x, y, z, jnp.ones_like(x)], axis=0))
    terms = jnp.concatenate([high, high, mid, mid, high, low], axis=0)
    terms = jnp.concatenate([terms, jnp.zeros((DEPTH - 6 * TERMS, count), jnp.float32)], axis=0)
    feature_ref[...] = jnp.transpose(terms).astype(jnp.bfloat16)
    group = 32

    def one(g, carry):
        at = pl.multiple_of(g * group, group)
        y = comp_ref[0, pl.ds(at, group), :]
        z = comp_ref[1, pl.ds(at, group), :]
        lane = lax.broadcasted_iota(jnp.int32, (group, lanes), 1)
        from_y = jnp.where(y > 0, lane + (lanes - NZ), lane + NZ) & (lanes - 1)
        from_z = (lane & ~(NZ - 1)) | (jnp.where(z > 0, lane + (NZ - 1), lane + 1) & (NZ - 1))
        ay, az = KAPPA_CELL * jnp.abs(y), KAPPA_CELL * jnp.abs(z)
        both = ay + az
        for i in range(nx):
            d = dist_ref[pl.ds((start + at) * nx + i, group, stride=nx), :]
            near_y = jnp.take_along_axis(d, from_y, axis=1)
            near_z = jnp.take_along_axis(d, from_z, axis=1)
            slope_ref[i, pl.ds(at, group), :] = both * d - ay * near_y - az * near_z
        return carry

    lax.fori_loop(0, count // group, one, 0)


def slopes(nx, own, rows, dist):
    count, lanes = rows.shape[2], dist.shape[1]
    whole = pl.BlockSpec(memory_space=pltpu.VMEM)
    return pl.pallas_call(
        functools.partial(slope_kernel, nx, own),
        in_specs=[whole] * 2,
        out_specs=[whole] * 3,
        out_shape=[
            pltpu.VMEM((nx, count, lanes), jnp.float32),
            pltpu.VMEM((count, lanes), jnp.float32),
            pltpu.VMEM((count, DEPTH), jnp.bfloat16),
        ],
        scratch_shapes=[pltpu.VMEM((2, count, lanes), jnp.float32)],
        compiler_params=params(),
        cost_estimate=cost(20 * count * nx * lanes, 8 * count * nx * lanes),
        name="slope",
    )(rows, dist)


def state_of(nx, ma_ref, mb_ref, state, bulk_terms, flux_terms):
    lanes = ma_ref.shape[1]
    m = [ma_ref[k * nx : (k + 1) * nx, :] + mb_ref[k * nx : (k + 1) * nx, :] for k in range(NMOM)]
    n = m[0]
    inv_n = 1.0 / n
    u = [m[1] * inv_n, m[2] * inv_n, m[3] * inv_n]
    energy = m[4] + m[5] + m[6]
    uu = u[0] * u[0] + u[1] * u[1] + u[2] * u[2]
    temp = (energy * inv_n - uu) * (1.0 / 3.0)
    second = ((m[4], m[7], m[8]), (m[7], m[5], m[9]), (m[8], m[9], m[6]))
    inv_t = 1.0 / temp
    nu = KAPPA_CELL * n * jnp.exp(SHEAR * jnp.log(temp))
    rate = inv_t * (-0.5 * LOG2E)
    flux_scale = inv_n * inv_t * inv_t * (RATIO / 15.0)
    q = []
    for k in range(3):
        inner = u[0] * second[k][0] + u[1] * second[k][1] + u[2] * second[k][2]
        q.append(0.5 * flux_scale * (m[10 + k] - 2.0 * inner - u[k] * energy + 2.0 * n * u[k] * uu))
    twice = -2.0 * rate
    bulk = [rate, twice * u[0], twice * u[1], twice * u[2], rate * uu]
    flux = [jnp.zeros_like(n), q[0], q[1], q[2], -(u[0] * q[0] + u[1] * q[1] + u[2] * q[2])]
    for terms, ref in ((bulk, bulk_terms), (flux, flux_terms)):
        for k in range(TERMS):
            high, mid, low = split3(terms[k])
            for i, one in enumerate((high, mid, high, mid, low, high)):
                ref[(i * TERMS + k) * nx : (i * TERMS + k + 1) * nx, :] = one
        ref[6 * TERMS * nx :, :] = jnp.zeros(((32 - 6 * TERMS) * nx, lanes), jnp.float32)
    state[0] = nu * n * inv_t * jnp.sqrt(inv_t)
    state[1] = nu


def sweep(nx, sign_ref, state, bulk_terms, flux_terms, slope_ref, speed_ref, feature_ref, decay_ref, source_ref, send_ref):
    count, lanes = speed_ref.shape
    forward = sign_ref[0:1, 0:1][0, 0] > 0
    rest = jnp.zeros((DEPTH - 32, 2 * lanes), jnp.bfloat16)
    group = 32
    for j in range(nx):
        at_x = jnp.where(forward, j, nx - 1 - j)
        before = jnp.where(forward, j - 1, nx - j)
        scale = jnp.broadcast_to(state[0, pl.ds(at_x, 1), :], (group, lanes))
        rate_x = jnp.broadcast_to(state[1, pl.ds(at_x, 1), :], (group, lanes))
        cells = jnp.concatenate([ref[pl.ds(at_x, 32, stride=nx), :] for ref in (bulk_terms, flux_terms)], axis=1)
        cells = jnp.concatenate([cells.astype(jnp.bfloat16), rest], axis=0)
        both = jnp.dot(feature_ref[...], cells, preferred_element_type=jnp.float32)
        for at in range(0, count, group):
            rows = slice(at, at + group)
            exponent, wq = both[rows, :lanes], both[rows, lanes:]
            shape = 1.0 + wq * (exponent - 5.0 / RATIO)
            target = scale * jnp.exp2(exponent) * shape
            speed = speed_ref[rows, :]
            inv = 1.0 / (speed + rate_x)
            decay = speed * inv
            source = (target - slope_ref[at_x, rows, :]) * inv
            if j > 0:
                source = decay * source_ref[before, rows, :] + source
                decay = decay * decay_ref[before, rows, :]
            decay_ref[at_x, rows, :] = decay
            source_ref[at_x, rows, :] = source
            if send_ref is not None and j == nx - 1:
                send_ref[0, rows, :] = decay
                send_ref[1, rows, :] = source


def partner_kernel(nx, ma_ref, mb_ref, rows_ref, slope_ref, speed_ref, feature_ref,
                   decay_ref, source_ref, send_ref, sign_ref, state, bulk_terms, flux_terms):
    state_of(nx, ma_ref, mb_ref, state, bulk_terms, flux_terms)
    sign_ref[...] = jnp.broadcast_to(rows_ref[0, 0:1, 0:1], sign_ref.shape)
    sweep(nx, sign_ref, state, bulk_terms, flux_terms, slope_ref, speed_ref, feature_ref, decay_ref, source_ref, send_ref)


def partner_maps(nx, ma, mb, rows, part):
    count, lanes = part[1].shape
    whole = pl.BlockSpec(memory_space=pltpu.VMEM)
    field = pltpu.VMEM((nx, count, lanes), jnp.float32)
    terms = pltpu.VMEM((32 * nx, lanes), jnp.float32)
    return pl.pallas_call(
        functools.partial(partner_kernel, nx),
        in_specs=[whole] * 6,
        out_specs=[whole] * 7,
        out_shape=[
            field,
            field,
            pltpu.VMEM((2, count, lanes), jnp.float32),
            pltpu.VMEM((8, lanes), jnp.float32),
            pltpu.VMEM((2, nx, lanes), jnp.float32),
            terms,
            terms,
        ],
        compiler_params=params(),
        cost_estimate=cost(40 * count * nx * lanes, 12 * count * nx * lanes),
        name="partner_maps",
    )(ma, mb, rows, *part)


def own_kernel(nx, sign_ref, state, bulk_terms, flux_terms, slope_ref, speed_ref, feature_ref, decay_ref, source_ref):
    sweep(nx, sign_ref, state, bulk_terms, flux_terms, slope_ref, speed_ref, feature_ref, decay_ref, source_ref, None)


def own_maps(nx, sign, state, part):
    count, lanes = part[1].shape
    whole = pl.BlockSpec(memory_space=pltpu.VMEM)
    field = pltpu.VMEM((nx, count, lanes), jnp.float32)
    return pl.pallas_call(
        functools.partial(own_kernel, nx),
        in_specs=[whole] * 7,
        out_specs=[whole] * 2,
        out_shape=[field, field],
        compiler_params=params(),
        cost_estimate=cost(40 * count * nx * lanes, 12 * count * nx * lanes),
        name="own_maps",
    )(sign, *state, *part)


def standing(sign_ref):
    place, chips = lax.axis_index("gx"), lax.axis_size("gx") // 2
    chip, core = place // 2, place % 2
    forward = sign_ref[0:1, :] > 0
    return jnp.where(forward, core, 1 - core) == 0, jnp.where(forward, chip, chips - 1 - chip)


def compose_kernel(nx, sign_ref, got_ref, decay_ref, source_ref, inflow_ref, near_ref, face_ref, entry_ref, *chip_ref):
    first, _ = standing(sign_ref)
    half = entry_ref.shape[0]
    mine = pl.ds(pl.multiple_of(half_index(True) * half, half), half)
    last = jnp.where(sign_ref[0:1, 0:1][0, 0] > 0, nx - 1, 0)
    decay, source = decay_ref[last], source_ref[last]
    got_decay, got_source = got_ref[0], got_ref[1]
    near_decay = jnp.where(first, decay, got_decay)
    near_source = jnp.where(first, source, got_source)
    far_decay = jnp.where(first, got_decay, decay)
    far_source = jnp.where(first, got_source, source)
    chip_decay, chip_source = far_decay * near_decay, far_decay * near_source + far_source
    near_ref[0], near_ref[1] = near_decay, near_source
    if chip_ref:
        chip_ref[0][0], chip_ref[0][1] = chip_decay, chip_source
    entry = inflow_ref[mine, :]
    entry_ref[...] = entry
    face_ref[...] = chip_decay * entry + chip_source


def compose_chip(nx, sign, got, decay, source, inflow):
    _, half, lanes = got.shape
    whole = pl.BlockSpec(memory_space=pltpu.VMEM)
    pair = pltpu.VMEM((2, half, lanes), jnp.float32)
    outs = [pair] + [pltpu.VMEM((half, lanes), jnp.float32)] * 2
    if lax.axis_size("gx") > 4:
        outs.append(pair)
    return pl.pallas_call(
        functools.partial(compose_kernel, nx),
        in_specs=[whole] * 5,
        out_specs=[whole] * len(outs),
        out_shape=outs,
        compiler_params=params(),
        cost_estimate=cost(10 * half * lanes, 40 * half * lanes),
        name="compose",
    )(sign, got, decay, source, inflow)


def pass_kernel(step, sign_ref, got_ref, entry_ref, chip_ref, next_ref, face_ref):
    _, before = standing(sign_ref)
    entry = jnp.where(before == step, got_ref[...], entry_ref[...])
    next_ref[...] = entry
    face_ref[...] = chip_ref[0] * entry + chip_ref[1]


def pass_face(step, sign, got, entry, chip):
    whole = pl.BlockSpec(memory_space=pltpu.VMEM)
    out = pltpu.VMEM(entry.shape, jnp.float32)
    return pl.pallas_call(
        functools.partial(pass_kernel, step),
        in_specs=[whole] * 4,
        out_specs=[whole] * 2,
        out_shape=[out, out],
        compiler_params=params(),
        cost_estimate=cost(3 * entry.size, 20 * entry.size),
        name="face",
    )(sign, got, entry, chip)


def share_kernel(step, sign_ref, got_ref, entry_ref, near_ref, keep_ref, send_ref):
    first, before = standing(sign_ref)
    entry = jnp.where(before == step, got_ref[...], entry_ref[...])
    middle = near_ref[0] * entry + near_ref[1]
    keep_ref[...] = jnp.where(first, entry, middle)
    send_ref[...] = jnp.where(first, middle, entry)


def share_entry(step, sign, got, entry, near):
    whole = pl.BlockSpec(memory_space=pltpu.VMEM)
    out = pltpu.VMEM(entry.shape, jnp.float32)
    return pl.pallas_call(
        functools.partial(share_kernel, step),
        in_specs=[whole] * 4,
        out_specs=[whole] * 2,
        out_shape=[out, out],
        compiler_params=params(),
        cost_estimate=cost(3 * entry.size, 20 * entry.size),
        name="share",
    )(sign, got, entry, near)


def chip_exchange(a):
    n = lax.axis_size("gx")
    return lax.ppermute(a, "gx", [(i, i ^ 1) for i in range(n)])


def chip_hop(face, step):
    chips = lax.axis_size("gx") // 2
    up, down = (step, step + 1), (chips - 1 - step, chips - 2 - step)
    pairs = [(2 * a + c, 2 * b + c) for a, b in (up, down) for c in range(2)]
    if chips % 2 == 0:
        got = lax.ppermute(face, "gx", pairs)
        return got, got
    return lax.ppermute(face, "gx", pairs[:2]), lax.ppermute(face, "gx", pairs[2:])


def new_moments_kernel(nx, own, entry_ref, table_ref, decay_ref, source_ref, *refs):
    mom_ref = refs[-1]
    entry = entry_ref[...]
    lanes = entry.shape[1]
    table = table_ref[half_index(own)]
    for i in range(0, nx, 2):
        pair = range(min(2, nx - i))
        planes = [decay_ref[i + k] * entry + source_ref[i + k] for k in pair]
        got = project(table, jnp.concatenate(planes, axis=1))
        for k in pair:
            part = got[:NMOM, k * lanes : (k + 1) * lanes]
            place = pl.ds(i + k, NMOM, stride=nx)
            mom_ref[place, :] = part + refs[0][place, :] if len(refs) > 1 else part


def new_moments(nx, own, entry, table, decay, source, *more):
    count, lanes = entry.shape
    whole = pl.BlockSpec(memory_space=pltpu.VMEM)
    return pl.pallas_call(
        functools.partial(new_moments_kernel, nx, own),
        in_specs=[whole] * (4 + len(more)),
        out_specs=whole,
        out_shape=pltpu.VMEM((NMOM * nx, lanes), jnp.float32),
        compiler_params=params(),
        cost_estimate=cost(2 * 48 * count * nx * lanes, 8 * count * nx * lanes),
        name="new_moments",
    )(entry, table, decay, source, *more)


def write_kernel(nx, pieces, *refs):
    halves, (out_hbm, held, sems) = (refs[:3], refs[3:6]), refs[6:]
    half, lanes = halves[0][0].shape
    size = half // pieces
    copies = []
    for h, (entry_ref, decay_ref, source_ref) in enumerate(halves):
        start = half_index(h == 0) * half
        for p in range(pieces):
            rows = slice(p * size, (p + 1) * size)
            entry = entry_ref[rows, :]
            base = (h * half + p * size) * nx
            for i in range(nx):
                held[pl.ds(base + i, size, stride=nx), :] = decay_ref[i, rows, :] * entry + source_ref[i, rows, :]
            to = pl.ds(pl.multiple_of((start + p * size) * nx, size * nx), size * nx)
            copy = pltpu.make_async_copy(
                held.at[pl.ds(base, size * nx), :], out_hbm.at[to, :], sems.at[h * pieces + p]
            )
            copy.start()
            copies.append(copy)
    for copy in copies:
        copy.wait()


def write_dist(nx, *halves):
    half, lanes = halves[0].shape
    pieces = max(1, half // 64)
    whole = pl.BlockSpec(memory_space=pltpu.VMEM)
    return pl.pallas_call(
        functools.partial(write_kernel, nx, pieces),
        in_specs=[whole] * 6,
        out_specs=pl.BlockSpec(memory_space=pltpu.HBM),
        out_shape=jax.ShapeDtypeStruct((2 * half * nx, lanes), jnp.float32),
        scratch_shapes=[
            pltpu.VMEM((2 * half * nx, lanes), jnp.float32),
            pltpu.SemaphoreType.DMA((2 * pieces,)),
        ],
        compiler_params=params(),
        cost_estimate=cost(4 * half * nx * lanes, 24 * half * nx * lanes),
        name="write_dist",
    )(*halves)


def stages_of(n):
    out, bit = [], 1
    while bit < n:
        if bit * 4 <= n:
            out.append((bit, 2 * bit, 3 * bit))
            bit *= 4
        else:
            out.append((bit,))
            bit *= 2
    return out


def exchange(a, axis, mask):
    n = lax.axis_size(axis)
    return lax.ppermute(a, axis, [(i, i ^ mask) for i in range(n)])


def partial_sums(a, axis, beside=()):
    n = lax.axis_size(axis)
    beside = list(beside)
    if n & (n - 1) or n == 1:
        total = lax.psum(a, axis)
        return (total, jnp.zeros_like(total)), [f(a) for f in beside]
    stages = stages_of(n)
    done = []
    for i, masks in enumerate(stages):
        got = [exchange(a, axis, m) for m in masks]
        take = beside if i == len(stages) - 1 else beside[:1]
        beside = beside[len(take) :]
        made = [f(a) for f in take]
        got, made = lax.optimization_barrier((got, made))
        done += made
        other = functools.reduce(jnp.add, got)
        if i == len(stages) - 1:
            return (a, other), done
        a = a + other


def local(total, dist, inflow, speed_x, transverse, quad_weight, side):
    count, nx, lanes = dist.shape
    flat = dist.reshape(count * nx, lanes)
    row = lambda a: a.reshape(1, count)
    partial, table, rows, held = old_moments(total, nx, row(side), row(speed_x), transverse, row(quad_weight), flat)

    def slope_half(own):
        return lambda sent: slopes(nx, own, *lax.optimization_barrier((rows, held, sent))[:2])

    (ma, mb), (part, own_part) = partial_sums(partial, "vert", [slope_half(False), slope_half(True)])
    decay, source, send, sign, *state = partner_maps(nx, ma, mb, rows, part)
    arrived = chip_exchange(send)
    own_decay, own_source = own_maps(nx, sign, state, own_part)
    arrived, own_decay, own_source = lax.optimization_barrier((arrived, own_decay, own_source))
    near, face, entry, *chip = compose_chip(nx, sign, arrived, own_decay, own_source, inflow)
    got = entry
    chips = lax.axis_size("gx") // 2
    for step in range(chips - 1):
        if step > 0:
            entry, face = pass_face(step, sign, got, entry, chip[0])
        low, high = chip_hop(face, step)
        got = low if low is high else jnp.where(side[0] == 1, low, high)
    keep, share = share_entry(chips - 1, sign, got, entry, near)
    other = chip_exchange(share)
    own_moments = new_moments(nx, True, keep, table, own_decay, own_source)
    other, own_moments = lax.optimization_barrier((other, own_moments))
    new_partial = new_moments(nx, False, other, table, decay, source, own_moments)

    def write(sent):
        args = lax.optimization_barrier((keep, own_decay, own_source, other, decay, source, sent))[:6]
        return write_dist(nx, *args)

    (na, nb), (new_flat,) = partial_sums(new_partial, "vert", [write])
    return new_flat.reshape(count, nx, lanes), (na + nb).reshape(NMOM, nx, lanes)


def solution(mesh):
    def whole(dist, inflow, speed_x, transverse, quad_weight, side):
        body = functools.partial(local, dist.shape[0])
        return jax.shard_map(
            body,
            mesh=mesh,
            in_specs=(P("vert", "gx", None), P("vert", None), P("vert"), P(None, "vert"), P("vert"), P("vert")),
            out_specs=(P("vert", "gx", None), P(None, "gx", None)),
            check_vma=False,
        )(dist, inflow, speed_x, transverse, quad_weight, side)

    return whole
```

```python
import functools

import jax
import jax.numpy as jnp
from jax import lax
from jax.experimental import pallas as pl
from jax.experimental.pallas import tpu as pltpu
from jax.sharding import PartitionSpec as P

NZ = 32
KAPPA_CELL = 0.02
LOG2E = 1.4426950408889634
RATIO = -2.0 / LOG2E
SHEAR = 0.19
NMOM = 13
ROWS = 16
TERMS = 5
DEPTH = 128


def params(**kw):
    return pltpu.CompilerParams(vmem_limit_bytes=20 * 1024 * 1024, **kw)


def cost(flops, nbytes):
    return pl.CostEstimate(flops=flops, bytes_accessed=nbytes, transcendentals=0)


def split(a):
    high = a.astype(jnp.bfloat16)
    low = (a - high.astype(jnp.float32)).astype(jnp.bfloat16)
    return high, low


def split3(a):
    high, rest = split(a)
    mid, low = split(a - high.astype(jnp.float32))
    return [high.astype(jnp.float32), mid.astype(jnp.float32), low.astype(jnp.float32)]


def project(table, plane):
    high, low = split(plane)
    first = jnp.dot(table, high, preferred_element_type=jnp.float32)
    second = jnp.dot(table[:ROWS], low, preferred_element_type=jnp.float32)
    return first[:ROWS] + first[ROWS:] + second


def moments_kernel(total, nx, chunks, side_hbm, speed_hbm, cross_hbm, weight_hbm, dist_hbm,
                   mom_ref, table_ref, rows_ref, dist_ref, side_ref, speed_ref, cross_ref, weight_ref, sems):
    count = speed_ref.shape[1]
    chunk = count // chunks
    small = [(side_hbm, side_ref), (speed_hbm, speed_ref), (cross_hbm, cross_ref), (weight_hbm, weight_ref)]
    copies = [pltpu.make_async_copy(a, b, sems.at[chunks + i]) for i, (a, b) in enumerate(small)]
    parts = []
    for i in range(chunks):
        rows = pl.ds(i * chunk * nx, chunk * nx)
        parts.append(pltpu.make_async_copy(dist_hbm.at[rows, :], dist_ref.at[rows, :], sems.at[i]))
    for c in copies + parts:
        c.start()
    for c in copies:
        c.wait()
    speed = speed_ref[...]
    x = jnp.where(side_ref[...] == 1, speed, -speed)
    y = cross_ref[0:1, :]
    z = cross_ref[1:2, :]
    xx, yy, zz = x * x, y * y, z * z
    square = xx + yy + zz
    stacked = jnp.concatenate([x, y, z] + [jnp.zeros_like(x)] * 5, axis=0)
    for h in range(2):
        rows_ref[h] = stacked[:, h * (count // 2) : (h + 1) * (count // 2)]
    rows = [jnp.ones_like(x), x, y, z, xx, yy, zz, x * y, x * z, y * z, x * square, y * square, z * square]
    rows += [jnp.zeros_like(x)] * (ROWS - NMOM)
    full = jnp.concatenate(rows, axis=0) * (weight_ref[...] * (1.0 / total))
    high, low = split(full)
    table = jnp.concatenate([high, low], axis=0)
    for h in range(2):
        table_ref[h] = table[:, h * (count // 2) : (h + 1) * (count // 2)]
    for c in range(chunks):
        parts[c].wait()
        tab = table[:, c * chunk : (c + 1) * chunk]
        for i in range(0, nx, 2):
            pair = range(min(2, nx - i))
            planes = [dist_ref[pl.ds(c * chunk * nx + i + k, chunk, stride=nx), :] for k in pair]
            lanes = planes[0].shape[1]
            got = project(tab, jnp.concatenate(planes, axis=1))
            for k in pair:
                part = got[:NMOM, k * lanes : (k + 1) * lanes]
                place = pl.ds(i + k, NMOM, stride=nx)
                if c == 0:
                    mom_ref[place, :] = part
                else:
                    mom_ref[place, :] += part


def old_moments(total, nx, side, speed, cross, weight, dist):
    count, lanes = speed.shape[1], dist.shape[1]
    chunks = max(1, count // 256)
    whole = pl.BlockSpec(memory_space=pltpu.VMEM)
    return pl.pallas_call(
        functools.partial(moments_kernel, total, nx, chunks),
        in_specs=[pl.BlockSpec(memory_space=pltpu.HBM)] * 5,
        out_specs=[whole] * 4,
        out_shape=[
            pltpu.VMEM((NMOM * nx, lanes), jnp.float32),
            pltpu.VMEM((2, 2 * ROWS, count // 2), jnp.bfloat16),
            pltpu.VMEM((2, 8, count // 2), jnp.float32),
            pltpu.VMEM(dist.shape, jnp.float32),
        ],
        scratch_shapes=[
            pltpu.VMEM(side.shape, jnp.int32),
            pltpu.VMEM(speed.shape, jnp.float32),
            pltpu.VMEM(cross.shape, jnp.float32),
            pltpu.VMEM(weight.shape, jnp.float32),
            pltpu.SemaphoreType.DMA((chunks + 4,)),
        ],
        compiler_params=params(),
        cost_estimate=cost(2 * 48 * count * nx * lanes, 4 * count * nx * lanes),
        name="moments",
    )(*[pltpu.with_memory_space_constraint(a, pltpu.HBM) for a in (side, speed, cross, weight, dist)])


def half_index(own):
    core = lax.axis_index("gx") % 2
    return core if own else 1 - core


def slope_kernel(nx, own, rows_ref, dist_ref, slope_ref, speed_ref, feature_ref, comp_ref):
    count = slope_ref.shape[1]
    lanes = dist_ref.shape[1]
    half = half_index(own)
    start = pl.multiple_of(half * count, count)
    rows = rows_ref[half]
    columns = jnp.transpose(rows)
    speed_ref[...] = jnp.broadcast_to(jnp.abs(columns[:, 0:1]), (count, lanes))
    for k in range(2):
        comp_ref[k] = jnp.broadcast_to(columns[:, k + 1 : k + 2], (count, lanes))
    x, y, z = rows[0:1], rows[1:2], rows[2:3]
    high, mid, low = split3(jnp.concatenate([x * x + y * y + z * z, x, y, z, jnp.ones_like(x)], axis=0))
    terms = jnp.concatenate([high, high, mid, mid, high, low], axis=0)
    terms = jnp.concatenate([terms, jnp.zeros((DEPTH - 6 * TERMS, count), jnp.float32)], axis=0)
    feature_ref[...] = jnp.transpose(terms).astype(jnp.bfloat16)
    group = 32

    def one(g, carry):
        at = pl.multiple_of(g * group, group)
        y = comp_ref[0, pl.ds(at, group), :]
        z = comp_ref[1, pl.ds(at, group), :]
        lane = lax.broadcasted_iota(jnp.int32, (group, lanes), 1)
        from_y = jnp.where(y > 0, lane + (lanes - NZ), lane + NZ) & (lanes - 1)
        from_z = (lane & ~(NZ - 1)) | (jnp.where(z > 0, lane + (NZ - 1), lane + 1) & (NZ - 1))
        ay, az = KAPPA_CELL * jnp.abs(y), KAPPA_CELL * jnp.abs(z)
        both = ay + az
        for i in range(nx):
            d = dist_ref[pl.ds((start + at) * nx + i, group, stride=nx), :]
            near_y = jnp.take_along_axis(d, from_y, axis=1)
            near_z = jnp.take_along_axis(d, from_z, axis=1)
            slope_ref[i, pl.ds(at, group), :] = both * d - ay * near_y - az * near_z
        return carry

    lax.fori_loop(0, count // group, one, 0)


def slopes(nx, own, rows, dist):
    count, lanes = rows.shape[2], dist.shape[1]
    whole = pl.BlockSpec(memory_space=pltpu.VMEM)
    return pl.pallas_call(
        functools.partial(slope_kernel, nx, own),
        in_specs=[whole] * 2,
        out_specs=[whole] * 3,
        out_shape=[
            pltpu.VMEM((nx, count, lanes), jnp.float32),
            pltpu.VMEM((count, lanes), jnp.float32),
            pltpu.VMEM((count, DEPTH), jnp.bfloat16),
        ],
        scratch_shapes=[pltpu.VMEM((2, count, lanes), jnp.float32)],
        compiler_params=params(),
        cost_estimate=cost(20 * count * nx * lanes, 8 * count * nx * lanes),
        name="slope",
    )(rows, dist)


def state_of(nx, ma_ref, mb_ref, state, bulk_terms, flux_terms):
    lanes = ma_ref.shape[1]
    m = [ma_ref[k * nx : (k + 1) * nx, :] + mb_ref[k * nx : (k + 1) * nx, :] for k in range(NMOM)]
    n = m[0]
    inv_n = 1.0 / n
    u = [m[1] * inv_n, m[2] * inv_n, m[3] * inv_n]
    energy = m[4] + m[5] + m[6]
    uu = u[0] * u[0] + u[1] * u[1] + u[2] * u[2]
    temp = (energy * inv_n - uu) * (1.0 / 3.0)
    second = ((m[4], m[7], m[8]), (m[7], m[5], m[9]), (m[8], m[9], m[6]))
    inv_t = 1.0 / temp
    nu = KAPPA_CELL * n * jnp.exp(SHEAR * jnp.log(temp))
    rate = inv_t * (-0.5 * LOG2E)
    flux_scale = inv_n * inv_t * inv_t * (RATIO / 15.0)
    q = []
    for k in range(3):
        inner = u[0] * second[k][0] + u[1] * second[k][1] + u[2] * second[k][2]
        q.append(0.5 * flux_scale * (m[10 + k] - 2.0 * inner - u[k] * energy + 2.0 * n * u[k] * uu))
    twice = -2.0 * rate
    bulk = [rate, twice * u[0], twice * u[1], twice * u[2], rate * uu]
    flux = [jnp.zeros_like(n), q[0], q[1], q[2], -(u[0] * q[0] + u[1] * q[1] + u[2] * q[2])]
    for terms, ref in ((bulk, bulk_terms), (flux, flux_terms)):
        for k in range(TERMS):
            high, mid, low = split3(terms[k])
            for i, one in enumerate((high, mid, high, mid, low, high)):
                ref[(i * TERMS + k) * nx : (i * TERMS + k + 1) * nx, :] = one
        ref[6 * TERMS * nx :, :] = jnp.zeros(((32 - 6 * TERMS) * nx, lanes), jnp.float32)
    state[0] = nu * n * inv_t * jnp.sqrt(inv_t)
    state[1] = nu


def sweep(nx, sign_ref, state, bulk_terms, flux_terms, slope_ref, speed_ref, feature_ref, decay_ref, source_ref, send_ref):
    count, lanes = speed_ref.shape
    forward = sign_ref[0:1, 0:1][0, 0] > 0
    rest = jnp.zeros((DEPTH - 32, 2 * lanes), jnp.bfloat16)
    group = 32
    places, cells = [], []
    for j in range(nx):
        at_x = jnp.where(forward, j, nx - 1 - j)
        both = jnp.concatenate([ref[pl.ds(at_x, 32, stride=nx), :] for ref in (bulk_terms, flux_terms)], axis=1)
        places.append(at_x)
        cells.append(jnp.concatenate([both.astype(jnp.bfloat16), rest], axis=0))
    group = 64
    for at in range(0, count, group):
        rows = slice(at, at + group)
        speed = speed_ref[rows, :]
        run_decay = run_source = None
        for j in range(nx):
            at_x = places[j]
            both = jnp.dot(feature_ref[rows, :], cells[j], preferred_element_type=jnp.float32)
            exponent, wq = both[:, :lanes], both[:, lanes:]
            shape = 1.0 + wq * (exponent - 5.0 / RATIO)
            target = state[0, pl.ds(at_x, 1), :] * jnp.exp2(exponent) * shape
            inv = 1.0 / (speed + state[1, pl.ds(at_x, 1), :])
            decay = speed * inv
            source = (target - slope_ref[at_x, rows, :]) * inv
            if j > 0:
                source = decay * run_source + source
                decay = decay * run_decay
            run_decay, run_source = decay, source
            decay_ref[at_x, rows, :] = decay
            source_ref[at_x, rows, :] = source
        if send_ref is not None:
            send_ref[0, rows, :] = run_decay
            send_ref[1, rows, :] = run_source


def partner_kernel(nx, ma_ref, mb_ref, rows_ref, slope_ref, speed_ref, feature_ref,
                   decay_ref, source_ref, send_ref, sign_ref, state, bulk_terms, flux_terms):
    state_of(nx, ma_ref, mb_ref, state, bulk_terms, flux_terms)
    sign_ref[...] = jnp.broadcast_to(rows_ref[0, 0:1, 0:1], sign_ref.shape)
    sweep(nx, sign_ref, state, bulk_terms, flux_terms, slope_ref, speed_ref, feature_ref, decay_ref, source_ref, send_ref)


def partner_maps(nx, ma, mb, rows, part):
    count, lanes = part[1].shape
    whole = pl.BlockSpec(memory_space=pltpu.VMEM)
    field = pltpu.VMEM((nx, count, lanes), jnp.float32)
    terms = pltpu.VMEM((32 * nx, lanes), jnp.float32)
    return pl.pallas_call(
        functools.partial(partner_kernel, nx),
        in_specs=[whole] * 6,
        out_specs=[whole] * 7,
        out_shape=[
            field,
            field,
            pltpu.VMEM((2, count, lanes), jnp.float32),
            pltpu.VMEM((8, lanes), jnp.float32),
            pltpu.VMEM((2, nx, lanes), jnp.float32),
            terms,
            terms,
        ],
        compiler_params=params(),
        cost_estimate=cost(40 * count * nx * lanes, 12 * count * nx * lanes),
        name="partner_maps",
    )(ma, mb, rows, *part)


def own_kernel(nx, sign_ref, state, bulk_terms, flux_terms, slope_ref, speed_ref, feature_ref, decay_ref, source_ref):
    sweep(nx, sign_ref, state, bulk_terms, flux_terms, slope_ref, speed_ref, feature_ref, decay_ref, source_ref, None)


def own_maps(nx, sign, state, part):
    count, lanes = part[1].shape
    whole = pl.BlockSpec(memory_space=pltpu.VMEM)
    field = pltpu.VMEM((nx, count, lanes), jnp.float32)
    return pl.pallas_call(
        functools.partial(own_kernel, nx),
        in_specs=[whole] * 7,
        out_specs=[whole] * 2,
        out_shape=[field, field],
        compiler_params=params(),
        cost_estimate=cost(40 * count * nx * lanes, 12 * count * nx * lanes),
        name="own_maps",
    )(sign, *state, *part)


def standing(sign_ref):
    place, chips = lax.axis_index("gx"), lax.axis_size("gx") // 2
    chip, core = place // 2, place % 2
    forward = sign_ref[0:1, :] > 0
    return jnp.where(forward, core, 1 - core) == 0, jnp.where(forward, chip, chips - 1 - chip)


def compose_kernel(nx, sign_ref, got_ref, decay_ref, source_ref, inflow_ref, near_ref, face_ref, entry_ref, *chip_ref):
    first, _ = standing(sign_ref)
    half = entry_ref.shape[0]
    mine = pl.ds(pl.multiple_of(half_index(True) * half, half), half)
    last = jnp.where(sign_ref[0:1, 0:1][0, 0] > 0, nx - 1, 0)
    decay, source = decay_ref[last], source_ref[last]
    got_decay, got_source = got_ref[0], got_ref[1]
    near_decay = jnp.where(first, decay, got_decay)
    near_source = jnp.where(first, source, got_source)
    far_decay = jnp.where(first, got_decay, decay)
    far_source = jnp.where(first, got_source, source)
    chip_decay, chip_source = far_decay * near_decay, far_decay * near_source + far_source
    near_ref[0], near_ref[1] = near_decay, near_source
    if chip_ref:
        chip_ref[0][0], chip_ref[0][1] = chip_decay, chip_source
    entry = inflow_ref[mine, :]
    entry_ref[...] = entry
    face_ref[...] = chip_decay * entry + chip_source


def compose_chip(nx, sign, got, decay, source, inflow):
    _, half, lanes = got.shape
    whole = pl.BlockSpec(memory_space=pltpu.VMEM)
    pair = pltpu.VMEM((2, half, lanes), jnp.float32)
    outs = [pair] + [pltpu.VMEM((half, lanes), jnp.float32)] * 2
    if lax.axis_size("gx") > 4:
        outs.append(pair)
    return pl.pallas_call(
        functools.partial(compose_kernel, nx),
        in_specs=[whole] * 5,
        out_specs=[whole] * len(outs),
        out_shape=outs,
        compiler_params=params(),
        cost_estimate=cost(10 * half * lanes, 40 * half * lanes),
        name="compose",
    )(sign, got, decay, source, inflow)


def pass_kernel(step, sign_ref, got_ref, entry_ref, chip_ref, next_ref, face_ref):
    _, before = standing(sign_ref)
    entry = jnp.where(before == step, got_ref[...], entry_ref[...])
    next_ref[...] = entry
    face_ref[...] = chip_ref[0] * entry + chip_ref[1]


def pass_face(step, sign, got, entry, chip):
    whole = pl.BlockSpec(memory_space=pltpu.VMEM)
    out = pltpu.VMEM(entry.shape, jnp.float32)
    return pl.pallas_call(
        functools.partial(pass_kernel, step),
        in_specs=[whole] * 4,
        out_specs=[whole] * 2,
        out_shape=[out, out],
        compiler_params=params(),
        cost_estimate=cost(3 * entry.size, 20 * entry.size),
        name="face",
    )(sign, got, entry, chip)


def share_kernel(step, sign_ref, got_ref, entry_ref, near_ref, keep_ref, send_ref):
    first, before = standing(sign_ref)
    entry = jnp.where(before == step, got_ref[...], entry_ref[...])
    middle = near_ref[0] * entry + near_ref[1]
    keep_ref[...] = jnp.where(first, entry, middle)
    send_ref[...] = jnp.where(first, middle, entry)


def share_entry(step, sign, got, entry, near):
    whole = pl.BlockSpec(memory_space=pltpu.VMEM)
    out = pltpu.VMEM(entry.shape, jnp.float32)
    return pl.pallas_call(
        functools.partial(share_kernel, step),
        in_specs=[whole] * 4,
        out_specs=[whole] * 2,
        out_shape=[out, out],
        compiler_params=params(),
        cost_estimate=cost(3 * entry.size, 20 * entry.size),
        name="share",
    )(sign, got, entry, near)


def chip_exchange(a):
    n = lax.axis_size("gx")
    return lax.ppermute(a, "gx", [(i, i ^ 1) for i in range(n)])


def chip_hop(face, step):
    chips = lax.axis_size("gx") // 2
    up, down = (step, step + 1), (chips - 1 - step, chips - 2 - step)
    pairs = [(2 * a + c, 2 * b + c) for a, b in (up, down) for c in range(2)]
    if chips % 2 == 0:
        got = lax.ppermute(face, "gx", pairs)
        return got, got
    return lax.ppermute(face, "gx", pairs[:2]), lax.ppermute(face, "gx", pairs[2:])


def new_moments_kernel(nx, own, entry_ref, table_ref, decay_ref, source_ref, *refs):
    mom_ref = refs[-1]
    entry = entry_ref[...]
    lanes = entry.shape[1]
    table = table_ref[half_index(own)]
    for i in range(0, nx, 2):
        pair = range(min(2, nx - i))
        planes = [decay_ref[i + k] * entry + source_ref[i + k] for k in pair]
        got = project(table, jnp.concatenate(planes, axis=1))
        for k in pair:
            part = got[:NMOM, k * lanes : (k + 1) * lanes]
            place = pl.ds(i + k, NMOM, stride=nx)
            mom_ref[place, :] = part + refs[0][place, :] if len(refs) > 1 else part


def new_moments(nx, own, entry, table, decay, source, *more):
    count, lanes = entry.shape
    whole = pl.BlockSpec(memory_space=pltpu.VMEM)
    return pl.pallas_call(
        functools.partial(new_moments_kernel, nx, own),
        in_specs=[whole] * (4 + len(more)),
        out_specs=whole,
        out_shape=pltpu.VMEM((NMOM * nx, lanes), jnp.float32),
        compiler_params=params(),
        cost_estimate=cost(2 * 48 * count * nx * lanes, 8 * count * nx * lanes),
        name="new_moments",
    )(entry, table, decay, source, *more)


def write_kernel(nx, pieces, *refs):
    halves, (out_hbm, held, sems) = (refs[:3], refs[3:6]), refs[6:]
    half, lanes = halves[0][0].shape
    size = half // pieces
    copies = []
    for h, (entry_ref, decay_ref, source_ref) in enumerate(halves):
        start = half_index(h == 0) * half
        for p in range(pieces):
            rows = slice(p * size, (p + 1) * size)
            entry = entry_ref[rows, :]
            base = (h * half + p * size) * nx
            for i in range(nx):
                held[pl.ds(base + i, size, stride=nx), :] = decay_ref[i, rows, :] * entry + source_ref[i, rows, :]
            to = pl.ds(pl.multiple_of((start + p * size) * nx, size * nx), size * nx)
            copy = pltpu.make_async_copy(
                held.at[pl.ds(base, size * nx), :], out_hbm.at[to, :], sems.at[h * pieces + p]
            )
            copy.start()
            copies.append(copy)
    for copy in copies:
        copy.wait()


def write_dist(nx, *halves):
    half, lanes = halves[0].shape
    pieces = max(1, half // 64)
    whole = pl.BlockSpec(memory_space=pltpu.VMEM)
    return pl.pallas_call(
        functools.partial(write_kernel, nx, pieces),
        in_specs=[whole] * 6,
        out_specs=pl.BlockSpec(memory_space=pltpu.HBM),
        out_shape=jax.ShapeDtypeStruct((2 * half * nx, lanes), jnp.float32),
        scratch_shapes=[
            pltpu.VMEM((2 * half * nx, lanes), jnp.float32),
            pltpu.SemaphoreType.DMA((2 * pieces,)),
        ],
        compiler_params=params(),
        cost_estimate=cost(4 * half * nx * lanes, 24 * half * nx * lanes),
        name="write_dist",
    )(*halves)


def stages_of(n):
    out, bit = [], 1
    while bit < n:
        if bit * 4 <= n:
            out.append((bit, 2 * bit, 3 * bit))
            bit *= 4
        else:
            out.append((bit,))
            bit *= 2
    return out


def exchange(a, axis, mask):
    n = lax.axis_size(axis)
    return lax.ppermute(a, axis, [(i, i ^ mask) for i in range(n)])


def partial_sums(a, axis, beside=()):
    n = lax.axis_size(axis)
    beside = list(beside)
    if n & (n - 1) or n == 1:
        total = lax.psum(a, axis)
        return (total, jnp.zeros_like(total)), [f(a) for f in beside]
    stages = stages_of(n)
    done = []
    for i, masks in enumerate(stages):
        got = [exchange(a, axis, m) for m in masks]
        take = beside if i == len(stages) - 1 else beside[:1]
        beside = beside[len(take) :]
        made = [f(a) for f in take]
        got, made = lax.optimization_barrier((got, made))
        done += made
        other = functools.reduce(jnp.add, got)
        if i == len(stages) - 1:
            return (a, other), done
        a = a + other


def local(total, dist, inflow, speed_x, transverse, quad_weight, side):
    count, nx, lanes = dist.shape
    flat = dist.reshape(count * nx, lanes)
    row = lambda a: a.reshape(1, count)
    partial, table, rows, held = old_moments(total, nx, row(side), row(speed_x), transverse, row(quad_weight), flat)

    def slope_half(own):
        return lambda sent: slopes(nx, own, *lax.optimization_barrier((rows, held, sent))[:2])

    (ma, mb), (part, own_part) = partial_sums(partial, "vert", [slope_half(False), slope_half(True)])
    decay, source, send, sign, *state = partner_maps(nx, ma, mb, rows, part)
    arrived = chip_exchange(send)
    own_decay, own_source = own_maps(nx, sign, state, own_part)
    arrived, own_decay, own_source = lax.optimization_barrier((arrived, own_decay, own_source))
    near, face, entry, *chip = compose_chip(nx, sign, arrived, own_decay, own_source, inflow)
    got = entry
    chips = lax.axis_size("gx") // 2
    for step in range(chips - 1):
        if step > 0:
            entry, face = pass_face(step, sign, got, entry, chip[0])
        low, high = chip_hop(face, step)
        got = low if low is high else jnp.where(side[0] == 1, low, high)
    keep, share = share_entry(chips - 1, sign, got, entry, near)
    other = chip_exchange(share)
    own_moments = new_moments(nx, True, keep, table, own_decay, own_source)
    other, own_moments = lax.optimization_barrier((other, own_moments))
    new_partial = new_moments(nx, False, other, table, decay, source, own_moments)

    def write(sent):
        args = lax.optimization_barrier((keep, own_decay, own_source, other, decay, source, sent))[:6]
        return write_dist(nx, *args)

    (na, nb), (new_flat,) = partial_sums(new_partial, "vert", [write])
    return new_flat.reshape(count, nx, lanes), (na + nb).reshape(NMOM, nx, lanes)


def solution(mesh):
    def whole(dist, inflow, speed_x, transverse, quad_weight, side):
        body = functools.partial(local, dist.shape[0])
        return jax.shard_map(
            body,
            mesh=mesh,
            in_specs=(P("vert", "gx", None), P("vert", None), P("vert"), P(None, "vert"), P("vert"), P("vert")),
            out_specs=(P("vert", "gx", None), P(None, "gx", None)),
            check_vma=False,
        )(dist, inflow, speed_x, transverse, quad_weight, side)

    return whole
```

```python
import functools

import jax
import jax.numpy as jnp
from jax import lax
from jax.experimental import pallas as pl
from jax.experimental.pallas import tpu as pltpu
from jax.sharding import PartitionSpec as P

NZ = 32
KAPPA_CELL = 0.02
LOG2E = 1.4426950408889634
RATIO = -2.0 / LOG2E
SHEAR = 0.19
NMOM = 13
ROWS = 16
TERMS = 5
DEPTH = 128


def params(**kw):
    return pltpu.CompilerParams(vmem_limit_bytes=20 * 1024 * 1024, **kw)


def cost(flops, nbytes):
    return pl.CostEstimate(flops=flops, bytes_accessed=nbytes, transcendentals=0)


def split(a):
    high = a.astype(jnp.bfloat16)
    low = (a - high.astype(jnp.float32)).astype(jnp.bfloat16)
    return high, low


def split3(a):
    high, rest = split(a)
    mid, low = split(a - high.astype(jnp.float32))
    return [high.astype(jnp.float32), mid.astype(jnp.float32), low.astype(jnp.float32)]


def project(table, plane):
    high, low = split(plane)
    first = jnp.dot(table, high, preferred_element_type=jnp.float32)
    second = jnp.dot(table[:ROWS], low, preferred_element_type=jnp.float32)
    return first[:ROWS] + first[ROWS:] + second


def moments_kernel(total, nx, chunks, side_hbm, speed_hbm, cross_hbm, weight_hbm, dist_hbm,
                   mom_ref, table_ref, rows_ref, dist_ref, side_ref, speed_ref, cross_ref, weight_ref, sems):
    count = speed_ref.shape[1]
    chunk = count // chunks
    small = [(side_hbm, side_ref), (speed_hbm, speed_ref), (cross_hbm, cross_ref), (weight_hbm, weight_ref)]
    copies = [pltpu.make_async_copy(a, b, sems.at[chunks + i]) for i, (a, b) in enumerate(small)]
    parts = []
    for i in range(chunks):
        rows = pl.ds(i * chunk * nx, chunk * nx)
        parts.append(pltpu.make_async_copy(dist_hbm.at[rows, :], dist_ref.at[rows, :], sems.at[i]))
    for c in copies + parts:
        c.start()
    for c in copies:
        c.wait()
    speed = speed_ref[...]
    x = jnp.where(side_ref[...] == 1, speed, -speed)
    y = cross_ref[0:1, :]
    z = cross_ref[1:2, :]
    xx, yy, zz = x * x, y * y, z * z
    square = xx + yy + zz
    stacked = jnp.concatenate([x, y, z] + [jnp.zeros_like(x)] * 5, axis=0)
    for h in range(2):
        rows_ref[h] = stacked[:, h * (count // 2) : (h + 1) * (count // 2)]
    rows = [jnp.ones_like(x), x, y, z, xx, yy, zz, x * y, x * z, y * z, x * square, y * square, z * square]
    rows += [jnp.zeros_like(x)] * (ROWS - NMOM)
    full = jnp.concatenate(rows, axis=0) * (weight_ref[...] * (1.0 / total))
    high, low = split(full)
    table = jnp.concatenate([high, low], axis=0)
    for h in range(2):
        table_ref[h] = table[:, h * (count // 2) : (h + 1) * (count // 2)]
    for c in range(chunks):
        parts[c].wait()
        tab = table[:, c * chunk : (c + 1) * chunk]
        for i in range(0, nx, 1):
            pair = range(min(1, nx - i))
            planes = [dist_ref[pl.ds(c * chunk * nx + i + k, chunk, stride=nx), :] for k in pair]
            lanes = planes[0].shape[1]
            got = project(tab, jnp.concatenate(planes, axis=1))
            for k in pair:
                part = got[:NMOM, k * lanes : (k + 1) * lanes]
                place = pl.ds(i + k, NMOM, stride=nx)
                if c == 0:
                    mom_ref[place, :] = part
                else:
                    mom_ref[place, :] += part


def old_moments(total, nx, side, speed, cross, weight, dist):
    count, lanes = speed.shape[1], dist.shape[1]
    chunks = max(1, count // 256)
    whole = pl.BlockSpec(memory_space=pltpu.VMEM)
    return pl.pallas_call(
        functools.partial(moments_kernel, total, nx, chunks),
        in_specs=[pl.BlockSpec(memory_space=pltpu.HBM)] * 5,
        out_specs=[whole] * 4,
        out_shape=[
            pltpu.VMEM((NMOM * nx, lanes), jnp.float32),
            pltpu.VMEM((2, 2 * ROWS, count // 2), jnp.bfloat16),
            pltpu.VMEM((2, 8, count // 2), jnp.float32),
            pltpu.VMEM(dist.shape, jnp.float32),
        ],
        scratch_shapes=[
            pltpu.VMEM(side.shape, jnp.int32),
            pltpu.VMEM(speed.shape, jnp.float32),
            pltpu.VMEM(cross.shape, jnp.float32),
            pltpu.VMEM(weight.shape, jnp.float32),
            pltpu.SemaphoreType.DMA((chunks + 4,)),
        ],
        compiler_params=params(),
        cost_estimate=cost(2 * 48 * count * nx * lanes, 4 * count * nx * lanes),
        name="moments",
    )(*[pltpu.with_memory_space_constraint(a, pltpu.HBM) for a in (side, speed, cross, weight, dist)])


def half_index(own):
    core = lax.axis_index("gx") % 2
    return core if own else 1 - core


def slope_kernel(nx, own, rows_ref, dist_ref, slope_ref, speed_ref, feature_ref, comp_ref):
    count = slope_ref.shape[1]
    lanes = dist_ref.shape[1]
    half = half_index(own)
    start = pl.multiple_of(half * count, count)
    rows = rows_ref[half]
    columns = jnp.transpose(rows)
    speed_ref[...] = jnp.broadcast_to(jnp.abs(columns[:, 0:1]), (count, lanes))
    for k in range(2):
        comp_ref[k] = jnp.broadcast_to(columns[:, k + 1 : k + 2], (count, lanes))
    x, y, z = rows[0:1], rows[1:2], rows[2:3]
    high, mid, low = split3(jnp.concatenate([x * x + y * y + z * z, x, y, z, jnp.ones_like(x)], axis=0))
    terms = jnp.concatenate([high, high, mid, mid, high, low], axis=0)
    terms = jnp.concatenate([terms, jnp.zeros((DEPTH - 6 * TERMS, count), jnp.float32)], axis=0)
    feature_ref[...] = jnp.transpose(terms).astype(jnp.bfloat16)
    group = 32

    def one(g, carry):
        at = pl.multiple_of(g * group, group)
        y = comp_ref[0, pl.ds(at, group), :]
        z = comp_ref[1, pl.ds(at, group), :]
        lane = lax.broadcasted_iota(jnp.int32, (group, lanes), 1)
        from_y = jnp.where(y > 0, lane + (lanes - NZ), lane + NZ) & (lanes - 1)
        from_z = (lane & ~(NZ - 1)) | (jnp.where(z > 0, lane + (NZ - 1), lane + 1) & (NZ - 1))
        ay, az = KAPPA_CELL * jnp.abs(y), KAPPA_CELL * jnp.abs(z)
        both = ay + az
        for i in range(nx):
            d = dist_ref[pl.ds((start + at) * nx + i, group, stride=nx), :]
            near_y = jnp.take_along_axis(d, from_y, axis=1)
            near_z = jnp.take_along_axis(d, from_z, axis=1)
            slope_ref[i, pl.ds(at, group), :] = both * d - ay * near_y - az * near_z
        return carry

    lax.fori_loop(0, count // group, one, 0)


def slopes(nx, own, rows, dist):
    count, lanes = rows.shape[2], dist.shape[1]
    whole = pl.BlockSpec(memory_space=pltpu.VMEM)
    return pl.pallas_call(
        functools.partial(slope_kernel, nx, own),
        in_specs=[whole] * 2,
        out_specs=[whole] * 3,
        out_shape=[
            pltpu.VMEM((nx, count, lanes), jnp.float32),
            pltpu.VMEM((count, lanes), jnp.float32),
            pltpu.VMEM((count, DEPTH), jnp.bfloat16),
        ],
        scratch_shapes=[pltpu.VMEM((2, count, lanes), jnp.float32)],
        compiler_params=params(),
        cost_estimate=cost(20 * count * nx * lanes, 8 * count * nx * lanes),
        name="slope",
    )(rows, dist)


def state_of(nx, ma_ref, mb_ref, state, bulk_terms, flux_terms):
    lanes = ma_ref.shape[1]
    m = [ma_ref[k * nx : (k + 1) * nx, :] + mb_ref[k * nx : (k + 1) * nx, :] for k in range(NMOM)]
    n = m[0]
    inv_n = 1.0 / n
    u = [m[1] * inv_n, m[2] * inv_n, m[3] * inv_n]
    energy = m[4] + m[5] + m[6]
    uu = u[0] * u[0] + u[1] * u[1] + u[2] * u[2]
    temp = (energy * inv_n - uu) * (1.0 / 3.0)
    second = ((m[4], m[7], m[8]), (m[7], m[5], m[9]), (m[8], m[9], m[6]))
    inv_t = 1.0 / temp
    nu = KAPPA_CELL * n * jnp.exp(SHEAR * jnp.log(temp))
    rate = inv_t * (-0.5 * LOG2E)
    flux_scale = inv_n * inv_t * inv_t * (RATIO / 15.0)
    q = []
    for k in range(3):
        inner = u[0] * second[k][0] + u[1] * second[k][1] + u[2] * second[k][2]
        q.append(0.5 * flux_scale * (m[10 + k] - 2.0 * inner - u[k] * energy + 2.0 * n * u[k] * uu))
    twice = -2.0 * rate
    bulk = [rate, twice * u[0], twice * u[1], twice * u[2], rate * uu]
    flux = [jnp.zeros_like(n), q[0], q[1], q[2], -(u[0] * q[0] + u[1] * q[1] + u[2] * q[2])]
    for terms, ref in ((bulk, bulk_terms), (flux, flux_terms)):
        for k in range(TERMS):
            high, mid, low = split3(terms[k])
            for i, one in enumerate((high, mid, high, mid, low, high)):
                ref[(i * TERMS + k) * nx : (i * TERMS + k + 1) * nx, :] = one
        ref[6 * TERMS * nx :, :] = jnp.zeros(((32 - 6 * TERMS) * nx, lanes), jnp.float32)
    state[0] = nu * n * inv_t * jnp.sqrt(inv_t)
    state[1] = nu


def sweep(nx, sign_ref, state, bulk_terms, flux_terms, slope_ref, speed_ref, feature_ref, decay_ref, source_ref, send_ref):
    count, lanes = speed_ref.shape
    forward = sign_ref[0:1, 0:1][0, 0] > 0
    rest = jnp.zeros((DEPTH - 32, 2 * lanes), jnp.bfloat16)
    group = 32
    places, cells = [], []
    for j in range(nx):
        at_x = jnp.where(forward, j, nx - 1 - j)
        both = jnp.concatenate([ref[pl.ds(at_x, 32, stride=nx), :] for ref in (bulk_terms, flux_terms)], axis=1)
        places.append(at_x)
        cells.append(jnp.concatenate([both.astype(jnp.bfloat16), rest], axis=0))
    group = 32
    for at in range(0, count, group):
        rows = slice(at, at + group)
        speed = speed_ref[rows, :]
        run_decay = run_source = None
        for j in range(nx):
            at_x = places[j]
            both = jnp.dot(feature_ref[rows, :], cells[j], preferred_element_type=jnp.float32)
            exponent, wq = both[:, :lanes], both[:, lanes:]
            shape = 1.0 + wq * (exponent - 5.0 / RATIO)
            target = state[0, pl.ds(at_x, 1), :] * jnp.exp2(exponent) * shape
            inv = 1.0 / (speed + state[1, pl.ds(at_x, 1), :])
            decay = speed * inv
            source = (target - slope_ref[at_x, rows, :]) * inv
            if j > 0:
                source = decay * run_source + source
                decay = decay * run_decay
            run_decay, run_source = decay, source
            decay_ref[at_x, rows, :] = decay
            source_ref[at_x, rows, :] = source
        if send_ref is not None:
            send_ref[0, rows, :] = run_decay
            send_ref[1, rows, :] = run_source


def partner_kernel(nx, ma_ref, mb_ref, rows_ref, slope_ref, speed_ref, feature_ref,
                   decay_ref, source_ref, send_ref, sign_ref, state, bulk_terms, flux_terms):
    state_of(nx, ma_ref, mb_ref, state, bulk_terms, flux_terms)
    sign_ref[...] = jnp.broadcast_to(rows_ref[0, 0:1, 0:1], sign_ref.shape)
    sweep(nx, sign_ref, state, bulk_terms, flux_terms, slope_ref, speed_ref, feature_ref, decay_ref, source_ref, send_ref)


def partner_maps(nx, ma, mb, rows, part):
    count, lanes = part[1].shape
    whole = pl.BlockSpec(memory_space=pltpu.VMEM)
    field = pltpu.VMEM((nx, count, lanes), jnp.float32)
    terms = pltpu.VMEM((32 * nx, lanes), jnp.float32)
    return pl.pallas_call(
        functools.partial(partner_kernel, nx),
        in_specs=[whole] * 6,
        out_specs=[whole] * 7,
        out_shape=[
            field,
            field,
            pltpu.VMEM((2, count, lanes), jnp.float32),
            pltpu.VMEM((8, lanes), jnp.float32),
            pltpu.VMEM((2, nx, lanes), jnp.float32),
            terms,
            terms,
        ],
        compiler_params=params(),
        cost_estimate=cost(40 * count * nx * lanes, 12 * count * nx * lanes),
        name="partner_maps",
    )(ma, mb, rows, *part)


def own_kernel(nx, sign_ref, state, bulk_terms, flux_terms, slope_ref, speed_ref, feature_ref, decay_ref, source_ref):
    sweep(nx, sign_ref, state, bulk_terms, flux_terms, slope_ref, speed_ref, feature_ref, decay_ref, source_ref, None)


def own_maps(nx, sign, state, part):
    count, lanes = part[1].shape
    whole = pl.BlockSpec(memory_space=pltpu.VMEM)
    field = pltpu.VMEM((nx, count, lanes), jnp.float32)
    return pl.pallas_call(
        functools.partial(own_kernel, nx),
        in_specs=[whole] * 7,
        out_specs=[whole] * 2,
        out_shape=[field, field],
        compiler_params=params(),
        cost_estimate=cost(40 * count * nx * lanes, 12 * count * nx * lanes),
        name="own_maps",
    )(sign, *state, *part)


def standing(sign_ref):
    place, chips = lax.axis_index("gx"), lax.axis_size("gx") // 2
    chip, core = place // 2, place % 2
    forward = sign_ref[0:1, :] > 0
    return jnp.where(forward, core, 1 - core) == 0, jnp.where(forward, chip, chips - 1 - chip)


def compose_kernel(nx, sign_ref, got_ref, decay_ref, source_ref, inflow_ref, near_ref, face_ref, entry_ref, *chip_ref):
    first, _ = standing(sign_ref)
    half = entry_ref.shape[0]
    mine = pl.ds(pl.multiple_of(half_index(True) * half, half), half)
    last = jnp.where(sign_ref[0:1, 0:1][0, 0] > 0, nx - 1, 0)
    decay, source = decay_ref[last], source_ref[last]
    got_decay, got_source = got_ref[0], got_ref[1]
    near_decay = jnp.where(first, decay, got_decay)
    near_source = jnp.where(first, source, got_source)
    far_decay = jnp.where(first, got_decay, decay)
    far_source = jnp.where(first, got_source, source)
    chip_decay, chip_source = far_decay * near_decay, far_decay * near_source + far_source
    near_ref[0], near_ref[1] = near_decay, near_source
    if chip_ref:
        chip_ref[0][0], chip_ref[0][1] = chip_decay, chip_source
    entry = inflow_ref[mine, :]
    entry_ref[...] = entry
    face_ref[...] = chip_decay * entry + chip_source


def compose_chip(nx, sign, got, decay, source, inflow):
    _, half, lanes = got.shape
    whole = pl.BlockSpec(memory_space=pltpu.VMEM)
    pair = pltpu.VMEM((2, half, lanes), jnp.float32)
    outs = [pair] + [pltpu.VMEM((half, lanes), jnp.float32)] * 2
    if lax.axis_size("gx") > 4:
        outs.append(pair)
    return pl.pallas_call(
        functools.partial(compose_kernel, nx),
        in_specs=[whole] * 5,
        out_specs=[whole] * len(outs),
        out_shape=outs,
        compiler_params=params(),
        cost_estimate=cost(10 * half * lanes, 40 * half * lanes),
        name="compose",
    )(sign, got, decay, source, inflow)


def pass_kernel(step, sign_ref, got_ref, entry_ref, chip_ref, next_ref, face_ref):
    _, before = standing(sign_ref)
    entry = jnp.where(before == step, got_ref[...], entry_ref[...])
    next_ref[...] = entry
    face_ref[...] = chip_ref[0] * entry + chip_ref[1]


def pass_face(step, sign, got, entry, chip):
    whole = pl.BlockSpec(memory_space=pltpu.VMEM)
    out = pltpu.VMEM(entry.shape, jnp.float32)
    return pl.pallas_call(
        functools.partial(pass_kernel, step),
        in_specs=[whole] * 4,
        out_specs=[whole] * 2,
        out_shape=[out, out],
        compiler_params=params(),
        cost_estimate=cost(3 * entry.size, 20 * entry.size),
        name="face",
    )(sign, got, entry, chip)


def share_kernel(step, sign_ref, got_ref, entry_ref, near_ref, keep_ref, send_ref):
    first, before = standing(sign_ref)
    entry = jnp.where(before == step, got_ref[...], entry_ref[...])
    middle = near_ref[0] * entry + near_ref[1]
    keep_ref[...] = jnp.where(first, entry, middle)
    send_ref[...] = jnp.where(first, middle, entry)


def share_entry(step, sign, got, entry, near):
    whole = pl.BlockSpec(memory_space=pltpu.VMEM)
    out = pltpu.VMEM(entry.shape, jnp.float32)
    return pl.pallas_call(
        functools.partial(share_kernel, step),
        in_specs=[whole] * 4,
        out_specs=[whole] * 2,
        out_shape=[out, out],
        compiler_params=params(),
        cost_estimate=cost(3 * entry.size, 20 * entry.size),
        name="share",
    )(sign, got, entry, near)


def chip_exchange(a):
    n = lax.axis_size("gx")
    return lax.ppermute(a, "gx", [(i, i ^ 1) for i in range(n)])


def chip_hop(face, step):
    chips = lax.axis_size("gx") // 2
    up, down = (step, step + 1), (chips - 1 - step, chips - 2 - step)
    pairs = [(2 * a + c, 2 * b + c) for a, b in (up, down) for c in range(2)]
    if chips % 2 == 0:
        got = lax.ppermute(face, "gx", pairs)
        return got, got
    return lax.ppermute(face, "gx", pairs[:2]), lax.ppermute(face, "gx", pairs[2:])


def new_moments_kernel(nx, own, entry_ref, table_ref, decay_ref, source_ref, *refs):
    mom_ref = refs[-1]
    entry = entry_ref[...]
    lanes = entry.shape[1]
    table = table_ref[half_index(own)]
    for i in range(0, nx, 1):
        pair = range(min(1, nx - i))
        planes = [decay_ref[i + k] * entry + source_ref[i + k] for k in pair]
        got = project(table, jnp.concatenate(planes, axis=1))
        for k in pair:
            part = got[:NMOM, k * lanes : (k + 1) * lanes]
            place = pl.ds(i + k, NMOM, stride=nx)
            mom_ref[place, :] = part + refs[0][place, :] if len(refs) > 1 else part


def new_moments(nx, own, entry, table, decay, source, *more):
    count, lanes = entry.shape
    whole = pl.BlockSpec(memory_space=pltpu.VMEM)
    return pl.pallas_call(
        functools.partial(new_moments_kernel, nx, own),
        in_specs=[whole] * (4 + len(more)),
        out_specs=whole,
        out_shape=pltpu.VMEM((NMOM * nx, lanes), jnp.float32),
        compiler_params=params(),
        cost_estimate=cost(2 * 48 * count * nx * lanes, 8 * count * nx * lanes),
        name="new_moments",
    )(entry, table, decay, source, *more)


def write_kernel(nx, pieces, *refs):
    halves, (out_hbm, held, sems) = (refs[:3], refs[3:6]), refs[6:]
    half, lanes = halves[0][0].shape
    size = half // pieces
    copies = []
    for h, (entry_ref, decay_ref, source_ref) in enumerate(halves):
        start = half_index(h == 0) * half
        for p in range(pieces):
            rows = slice(p * size, (p + 1) * size)
            entry = entry_ref[rows, :]
            base = (h * half + p * size) * nx
            for i in range(nx):
                held[pl.ds(base + i, size, stride=nx), :] = decay_ref[i, rows, :] * entry + source_ref[i, rows, :]
            to = pl.ds(pl.multiple_of((start + p * size) * nx, size * nx), size * nx)
            copy = pltpu.make_async_copy(
                held.at[pl.ds(base, size * nx), :], out_hbm.at[to, :], sems.at[h * pieces + p]
            )
            copy.start()
            copies.append(copy)
    for copy in copies:
        copy.wait()


def write_dist(nx, *halves):
    half, lanes = halves[0].shape
    pieces = max(1, half // 64)
    whole = pl.BlockSpec(memory_space=pltpu.VMEM)
    return pl.pallas_call(
        functools.partial(write_kernel, nx, pieces),
        in_specs=[whole] * 6,
        out_specs=pl.BlockSpec(memory_space=pltpu.HBM),
        out_shape=jax.ShapeDtypeStruct((2 * half * nx, lanes), jnp.float32),
        scratch_shapes=[
            pltpu.VMEM((2 * half * nx, lanes), jnp.float32),
            pltpu.SemaphoreType.DMA((2 * pieces,)),
        ],
        compiler_params=params(),
        cost_estimate=cost(4 * half * nx * lanes, 24 * half * nx * lanes),
        name="write_dist",
    )(*halves)


def stages_of(n):
    out, bit = [], 1
    while bit < n:
        if bit * 4 <= n:
            out.append((bit, 2 * bit, 3 * bit))
            bit *= 4
        else:
            out.append((bit,))
            bit *= 2
    return out


def exchange(a, axis, mask):
    n = lax.axis_size(axis)
    return lax.ppermute(a, axis, [(i, i ^ mask) for i in range(n)])


def partial_sums(a, axis, beside=()):
    n = lax.axis_size(axis)
    beside = list(beside)
    if n & (n - 1) or n == 1:
        total = lax.psum(a, axis)
        return (total, jnp.zeros_like(total)), [f(a) for f in beside]
    stages = stages_of(n)
    done = []
    for i, masks in enumerate(stages):
        got = [exchange(a, axis, m) for m in masks]
        take = beside if i == len(stages) - 1 else beside[:1]
        beside = beside[len(take) :]
        made = [f(a) for f in take]
        got, made = lax.optimization_barrier((got, made))
        done += made
        other = functools.reduce(jnp.add, got)
        if i == len(stages) - 1:
            return (a, other), done
        a = a + other


def local(total, dist, inflow, speed_x, transverse, quad_weight, side):
    count, nx, lanes = dist.shape
    flat = dist.reshape(count * nx, lanes)
    row = lambda a: a.reshape(1, count)
    partial, table, rows, held = old_moments(total, nx, row(side), row(speed_x), transverse, row(quad_weight), flat)

    def slope_half(own):
        return lambda sent: slopes(nx, own, *lax.optimization_barrier((rows, held, sent))[:2])

    (ma, mb), (part, own_part) = partial_sums(partial, "vert", [slope_half(False), slope_half(True)])
    decay, source, send, sign, *state = partner_maps(nx, ma, mb, rows, part)
    arrived = chip_exchange(send)
    own_decay, own_source = own_maps(nx, sign, state, own_part)
    arrived, own_decay, own_source = lax.optimization_barrier((arrived, own_decay, own_source))
    near, face, entry, *chip = compose_chip(nx, sign, arrived, own_decay, own_source, inflow)
    got = entry
    chips = lax.axis_size("gx") // 2
    for step in range(chips - 1):
        if step > 0:
            entry, face = pass_face(step, sign, got, entry, chip[0])
        low, high = chip_hop(face, step)
        got = low if low is high else jnp.where(side[0] == 1, low, high)
    keep, share = share_entry(chips - 1, sign, got, entry, near)
    other = chip_exchange(share)
    own_moments = new_moments(nx, True, keep, table, own_decay, own_source)
    other, own_moments = lax.optimization_barrier((other, own_moments))
    new_partial = new_moments(nx, False, other, table, decay, source, own_moments)

    def write(sent):
        args = lax.optimization_barrier((keep, own_decay, own_source, other, decay, source, sent))[:6]
        return write_dist(nx, *args)

    (na, nb), (new_flat,) = partial_sums(new_partial, "vert", [write])
    return new_flat.reshape(count, nx, lanes), (na + nb).reshape(NMOM, nx, lanes)


def solution(mesh):
    def whole(dist, inflow, speed_x, transverse, quad_weight, side):
        body = functools.partial(local, dist.shape[0])
        return jax.shard_map(
            body,
            mesh=mesh,
            in_specs=(P("vert", "gx", None), P("vert", None), P("vert"), P(None, "vert"), P("vert"), P("vert")),
            out_specs=(P("vert", "gx", None), P(None, "gx", None)),
            check_vma=False,
        )(dist, inflow, speed_x, transverse, quad_weight, side)

    return whole
```

```python
import functools

import jax
import jax.numpy as jnp
from jax import lax
from jax.experimental import pallas as pl
from jax.experimental.pallas import tpu as pltpu
from jax.sharding import PartitionSpec as P

NZ = 32
KAPPA_CELL = 0.02
LOG2E = 1.4426950408889634
RATIO = -2.0 / LOG2E
SHEAR = 0.19
NMOM = 13
ROWS = 16
TERMS = 5
DEPTH = 128


def params(**kw):
    return pltpu.CompilerParams(vmem_limit_bytes=20 * 1024 * 1024, **kw)


def cost(flops, nbytes):
    return pl.CostEstimate(flops=flops, bytes_accessed=nbytes, transcendentals=0)


def split(a):
    high = a.astype(jnp.bfloat16)
    low = (a - high.astype(jnp.float32)).astype(jnp.bfloat16)
    return high, low


def split3(a):
    high, rest = split(a)
    mid, low = split(a - high.astype(jnp.float32))
    return [high.astype(jnp.float32), mid.astype(jnp.float32), low.astype(jnp.float32)]


def project(table, plane):
    high, low = split(plane)
    first = jnp.dot(table, high, preferred_element_type=jnp.float32)
    second = jnp.dot(table[:ROWS], low, preferred_element_type=jnp.float32)
    return first[:ROWS] + first[ROWS:] + second


def moments_kernel(total, nx, side_hbm, speed_hbm, cross_hbm, weight_hbm, dist_hbm,
                   mom_ref, table_ref, rows_ref, own_ref, other_ref, side_ref, speed_ref, cross_ref, weight_ref, sems):
    half = speed_ref.shape[1] // 2
    size = half * nx
    small = [(side_hbm, side_ref), (speed_hbm, speed_ref), (cross_hbm, cross_ref), (weight_hbm, weight_ref)]
    copies = [pltpu.make_async_copy(a, b, sems.at[2 + i]) for i, (a, b) in enumerate(small)]
    parts = []
    for i, ref in enumerate((own_ref, other_ref)):
        rows = pl.ds(pl.multiple_of(half_index(i == 0) * size, size), size)
        parts.append(pltpu.make_async_copy(dist_hbm.at[rows, :], ref, sems.at[i]))
    for c in copies + parts:
        c.start()
    for c in copies:
        c.wait()
    speed = speed_ref[...]
    x = jnp.where(side_ref[...] == 1, speed, -speed)
    y = cross_ref[0:1, :]
    z = cross_ref[1:2, :]
    xx, yy, zz = x * x, y * y, z * z
    square = xx + yy + zz
    stacked = jnp.concatenate([x, y, z] + [jnp.zeros_like(x)] * 5, axis=0)
    for h in range(2):
        rows_ref[h] = stacked[:, h * half : (h + 1) * half]
    rows = [jnp.ones_like(x), x, y, z, xx, yy, zz, x * y, x * z, y * z, x * square, y * square, z * square]
    rows += [jnp.zeros_like(x)] * (ROWS - NMOM)
    full = jnp.concatenate(rows, axis=0) * (weight_ref[...] * (1.0 / total))
    high, low = split(full)
    table = jnp.concatenate([high, low], axis=0)
    for h in range(2):
        table_ref[h] = table[:, h * half : (h + 1) * half]
    for c, ref in enumerate((own_ref, other_ref)):
        parts[c].wait()
        tab = table_ref[half_index(c == 0)]
        for i in range(nx):
            part = project(tab, ref[pl.ds(i, half, stride=nx), :])[:NMOM]
            place = pl.ds(i, NMOM, stride=nx)
            mom_ref[place, :] = part if c == 0 else mom_ref[place, :] + part


def old_moments(total, nx, side, speed, cross, weight, dist):
    count, lanes = speed.shape[1], dist.shape[1]
    whole = pl.BlockSpec(memory_space=pltpu.VMEM)
    return pl.pallas_call(
        functools.partial(moments_kernel, total, nx),
        in_specs=[pl.BlockSpec(memory_space=pltpu.HBM)] * 5,
        out_specs=[whole] * 5,
        out_shape=[
            pltpu.VMEM((NMOM * nx, lanes), jnp.float32),
            pltpu.VMEM((2, 2 * ROWS, count // 2), jnp.bfloat16),
            pltpu.VMEM((2, 8, count // 2), jnp.float32),
            pltpu.VMEM((count * nx // 2, lanes), jnp.float32),
            pltpu.VMEM((count * nx // 2, lanes), jnp.float32),
        ],
        scratch_shapes=[
            pltpu.VMEM(side.shape, jnp.int32),
            pltpu.VMEM(speed.shape, jnp.float32),
            pltpu.VMEM(cross.shape, jnp.float32),
            pltpu.VMEM(weight.shape, jnp.float32),
            pltpu.SemaphoreType.DMA((6,)),
        ],
        compiler_params=params(),
        cost_estimate=cost(2 * 48 * count * nx * lanes, 4 * count * nx * lanes),
        name="moments",
    )(*[pltpu.with_memory_space_constraint(a, pltpu.HBM) for a in (side, speed, cross, weight, dist)])


def half_index(own):
    core = lax.axis_index("gx") % 2
    return core if own else 1 - core


def slope_kernel(nx, own, rows_ref, dist_ref, slope_ref, speed_ref, feature_ref, comp_ref):
    count = slope_ref.shape[1]
    lanes = dist_ref.shape[1]
    rows = rows_ref[half_index(own)]
    columns = jnp.transpose(rows)
    speed_ref[...] = jnp.broadcast_to(jnp.abs(columns[:, 0:1]), (count, lanes))
    for k in range(2):
        comp_ref[k] = jnp.broadcast_to(columns[:, k + 1 : k + 2], (count, lanes))
    x, y, z = rows[0:1], rows[1:2], rows[2:3]
    high, mid, low = split3(jnp.concatenate([x * x + y * y + z * z, x, y, z, jnp.ones_like(x)], axis=0))
    terms = jnp.concatenate([high, high, mid, mid, high, low], axis=0)
    terms = jnp.concatenate([terms, jnp.zeros((DEPTH - 6 * TERMS, count), jnp.float32)], axis=0)
    feature_ref[...] = jnp.transpose(terms).astype(jnp.bfloat16)
    group = 32

    def one(g, carry):
        at = pl.multiple_of(g * group, group)
        y = comp_ref[0, pl.ds(at, group), :]
        z = comp_ref[1, pl.ds(at, group), :]
        lane = lax.broadcasted_iota(jnp.int32, (group, lanes), 1)
        from_y = jnp.where(y > 0, lane + (lanes - NZ), lane + NZ) & (lanes - 1)
        from_z = (lane & ~(NZ - 1)) | (jnp.where(z > 0, lane + (NZ - 1), lane + 1) & (NZ - 1))
        ay, az = KAPPA_CELL * jnp.abs(y), KAPPA_CELL * jnp.abs(z)
        both = ay + az
        for i in range(nx):
            d = dist_ref[pl.ds(at * nx + i, group, stride=nx), :]
            near_y = jnp.take_along_axis(d, from_y, axis=1)
            near_z = jnp.take_along_axis(d, from_z, axis=1)
            slope_ref[i, pl.ds(at, group), :] = both * d - ay * near_y - az * near_z
        return carry

    lax.fori_loop(0, count // group, one, 0)


def slopes(nx, own, rows, dist):
    count, lanes = rows.shape[2], dist.shape[1]
    whole = pl.BlockSpec(memory_space=pltpu.VMEM)
    return pl.pallas_call(
        functools.partial(slope_kernel, nx, own),
        in_specs=[whole] * 2,
        out_specs=[whole] * 3,
        out_shape=[
            pltpu.VMEM((nx, count, lanes), jnp.float32),
            pltpu.VMEM((count, lanes), jnp.float32),
            pltpu.VMEM((count, DEPTH), jnp.bfloat16),
        ],
        scratch_shapes=[pltpu.VMEM((2, count, lanes), jnp.float32)],
        compiler_params=params(),
        cost_estimate=cost(20 * count * nx * lanes, 8 * count * nx * lanes),
        name="slope",
    )(rows, dist)


def state_of(nx, sum_ref, state, bulk_terms, flux_terms):
    lanes = sum_ref.shape[1]
    m = [sum_ref[k * nx : (k + 1) * nx, :] for k in range(NMOM)]
    n = m[0]
    inv_n = 1.0 / n
    u = [m[1] * inv_n, m[2] * inv_n, m[3] * inv_n]
    energy = m[4] + m[5] + m[6]
    uu = u[0] * u[0] + u[1] * u[1] + u[2] * u[2]
    temp = (energy * inv_n - uu) * (1.0 / 3.0)
    second = ((m[4], m[7], m[8]), (m[7], m[5], m[9]), (m[8], m[9], m[6]))
    inv_t = 1.0 / temp
    nu = KAPPA_CELL * n * jnp.exp(SHEAR * jnp.log(temp))
    rate = inv_t * (-0.5 * LOG2E)
    flux_scale = inv_n * inv_t * inv_t * (RATIO / 15.0)
    q = []
    for k in range(3):
        inner = u[0] * second[k][0] + u[1] * second[k][1] + u[2] * second[k][2]
        q.append(0.5 * flux_scale * (m[10 + k] - 2.0 * inner - u[k] * energy + 2.0 * n * u[k] * uu))
    twice = -2.0 * rate
    bulk = [rate, twice * u[0], twice * u[1], twice * u[2], rate * uu]
    flux = [jnp.zeros_like(n), q[0], q[1], q[2], -(u[0] * q[0] + u[1] * q[1] + u[2] * q[2])]
    for terms, ref in ((bulk, bulk_terms), (flux, flux_terms)):
        for k in range(TERMS):
            high, mid, low = split3(terms[k])
            for i, one in enumerate((high, mid, high, mid, low, high)):
                ref[(i * TERMS + k) * nx : (i * TERMS + k + 1) * nx, :] = one
        ref[6 * TERMS * nx :, :] = jnp.zeros(((32 - 6 * TERMS) * nx, lanes), jnp.float32)
    state[0] = nu * n * inv_t * jnp.sqrt(inv_t)
    state[1] = nu


def sweep(nx, forward, state, bulk_terms, flux_terms, slope_ref, speed_ref, feature_ref, fields, last_ref):
    count, lanes = speed_ref.shape
    rest = jnp.zeros((DEPTH - 32, 2 * lanes), jnp.bfloat16)
    group = 32
    places, cells = [], []
    for j in range(nx):
        at_x = jnp.where(forward, j, nx - 1 - j)
        both = jnp.concatenate([ref[pl.ds(at_x, 32, stride=nx), :] for ref in (bulk_terms, flux_terms)], axis=1)
        places.append(at_x)
        cells.append(jnp.concatenate([both.astype(jnp.bfloat16), rest], axis=0))
    group = 32
    for at in range(0, count, group):
        rows = slice(at, at + group)
        speed = speed_ref[rows, :]
        run_decay = run_source = None
        for j in range(nx):
            at_x = places[j]
            both = jnp.dot(feature_ref[rows, :], cells[j], preferred_element_type=jnp.float32)
            exponent, wq = both[:, :lanes], both[:, lanes:]
            shape = 1.0 + wq * (exponent - 5.0 / RATIO)
            target = state[0, pl.ds(at_x, 1), :] * jnp.exp2(exponent) * shape
            inv = 1.0 / (speed + state[1, pl.ds(at_x, 1), :])
            decay = speed * inv
            source = (target - slope_ref[at_x, rows, :]) * inv
            if j > 0:
                source = decay * run_source + source
                decay = decay * run_decay
            run_decay, run_source = decay, source
            if fields:
                fields[0][at_x, rows, :] = decay
                fields[1][at_x, rows, :] = source
        if last_ref is not None:
            last_ref[0, rows, :] = run_decay
            last_ref[1, rows, :] = run_source


def map_kernel(nx, kind, sum_ref, rows_ref, slope_ref, speed_ref, feature_ref, *refs):
    outs, (state, bulk_terms, flux_terms) = refs[:-3], refs[-3:]
    state_of(nx, sum_ref, state, bulk_terms, flux_terms)
    forward = rows_ref[0, 0:1, 0:1][0, 0] > 0
    if kind == "own":
        outs[2][...] = jnp.broadcast_to(rows_ref[0, 0:1, 0:1], outs[2].shape)
    fields, last_ref = outs[:2], None
    sweep(nx, forward, state, bulk_terms, flux_terms, slope_ref, speed_ref, feature_ref, fields, last_ref)


def map_scratch(nx, lanes):
    return [pltpu.VMEM((rows, lanes), jnp.float32) if rows else pltpu.VMEM((2, nx, lanes), jnp.float32)
            for rows in (0, 32 * nx, 32 * nx)]


def maps(nx, kind, total, rows, part):
    count, lanes = part[1].shape
    whole = pl.BlockSpec(memory_space=pltpu.VMEM)
    field = pltpu.VMEM((nx, count, lanes), jnp.float32)
    outs = [field, field] + ([pltpu.VMEM((8, lanes), jnp.float32)] if kind == "own" else [])
    return pl.pallas_call(
        functools.partial(map_kernel, nx, kind),
        in_specs=[whole] * 5,
        out_specs=[whole] * len(outs),
        out_shape=outs,
        scratch_shapes=map_scratch(nx, lanes),
        compiler_params=params(),
        cost_estimate=cost(40 * count * nx * lanes, 12 * count * nx * lanes),
        name=kind + "_maps",
    )(total, rows, *part)


def standing(sign_ref):
    place, chips = lax.axis_index("gx"), lax.axis_size("gx") // 2
    chip, core = place // 2, place % 2
    forward = sign_ref[0:1, :] > 0
    return jnp.where(forward, core, 1 - core) == 0, jnp.where(forward, chip, chips - 1 - chip)


def compose_kernel(nx, sum_ref, rows_ref, slope_ref, speed_ref, feature_ref, sign_ref, decay_ref, source_ref, inflow_ref,
                   near_ref, face_ref, entry_ref, *refs):
    chip_ref, (got_ref, state, bulk_terms, flux_terms) = refs[:-4], refs[-4:]
    state_of(nx, sum_ref, state, bulk_terms, flux_terms)
    forward = rows_ref[0, 0:1, 0:1][0, 0] > 0
    sweep(nx, forward, state, bulk_terms, flux_terms, slope_ref, speed_ref, feature_ref, (), got_ref)
    first, _ = standing(sign_ref)
    half = entry_ref.shape[0]
    mine = pl.ds(pl.multiple_of(half_index(True) * half, half), half)
    last = jnp.where(forward, nx - 1, 0)
    decay, source = decay_ref[last], source_ref[last]
    got_decay, got_source = got_ref[0], got_ref[1]
    near_decay = jnp.where(first, decay, got_decay)
    near_source = jnp.where(first, source, got_source)
    far_decay = jnp.where(first, got_decay, decay)
    far_source = jnp.where(first, got_source, source)
    chip_decay, chip_source = far_decay * near_decay, far_decay * near_source + far_source
    near_ref[0], near_ref[1] = near_decay, near_source
    if chip_ref:
        chip_ref[0][0], chip_ref[0][1] = chip_decay, chip_source
    entry = inflow_ref[mine, :]
    entry_ref[...] = entry
    face_ref[...] = chip_decay * entry + chip_source


def compose_chip(nx, total, rows, part, sign, decay, source, inflow):
    half, lanes = part[1].shape
    whole = pl.BlockSpec(memory_space=pltpu.VMEM)
    pair = pltpu.VMEM((2, half, lanes), jnp.float32)
    outs = [pair] + [pltpu.VMEM((half, lanes), jnp.float32)] * 2
    if lax.axis_size("gx") > 4:
        outs.append(pair)
    return pl.pallas_call(
        functools.partial(compose_kernel, nx),
        in_specs=[whole] * 9,
        out_specs=[whole] * len(outs),
        out_shape=outs,
        scratch_shapes=[pair] + map_scratch(nx, lanes),
        compiler_params=params(),
        cost_estimate=cost(40 * half * nx * lanes, 12 * half * nx * lanes),
        name="compose",
    )(total, rows, *part, sign, decay, source, inflow)


def pass_kernel(step, sign_ref, got_ref, entry_ref, chip_ref, next_ref, face_ref):
    _, before = standing(sign_ref)
    entry = jnp.where(before == step, got_ref[...], entry_ref[...])
    next_ref[...] = entry
    face_ref[...] = chip_ref[0] * entry + chip_ref[1]


def pass_face(step, sign, got, entry, chip):
    whole = pl.BlockSpec(memory_space=pltpu.VMEM)
    out = pltpu.VMEM(entry.shape, jnp.float32)
    return pl.pallas_call(
        functools.partial(pass_kernel, step),
        in_specs=[whole] * 4,
        out_specs=[whole] * 2,
        out_shape=[out, out],
        compiler_params=params(),
        cost_estimate=cost(3 * entry.size, 20 * entry.size),
        name="face",
    )(sign, got, entry, chip)


def share_kernel(step, sign_ref, got_ref, entry_ref, near_ref, keep_ref, send_ref):
    first, before = standing(sign_ref)
    entry = jnp.where(before == step, got_ref[...], entry_ref[...])
    middle = near_ref[0] * entry + near_ref[1]
    keep_ref[...] = jnp.where(first, entry, middle)
    send_ref[...] = jnp.where(first, middle, entry)


def share_entry(step, sign, got, entry, near):
    whole = pl.BlockSpec(memory_space=pltpu.VMEM)
    out = pltpu.VMEM(entry.shape, jnp.float32)
    return pl.pallas_call(
        functools.partial(share_kernel, step),
        in_specs=[whole] * 4,
        out_specs=[whole] * 2,
        out_shape=[out, out],
        compiler_params=params(),
        cost_estimate=cost(3 * entry.size, 20 * entry.size),
        name="share",
    )(sign, got, entry, near)


def chip_exchange(a):
    n = lax.axis_size("gx")
    return lax.ppermute(a, "gx", [(i, i ^ 1) for i in range(n)])


def chip_hop(face, step):
    chips = lax.axis_size("gx") // 2
    up, down = (step, step + 1), (chips - 1 - step, chips - 2 - step)
    pairs = [(2 * a + c, 2 * b + c) for a, b in (up, down) for c in range(2)]
    if chips % 2 == 0:
        got = lax.ppermute(face, "gx", pairs)
        return got, got
    return lax.ppermute(face, "gx", pairs[:2]), lax.ppermute(face, "gx", pairs[2:])


def new_moments_kernel(nx, own, entry_ref, table_ref, decay_ref, source_ref, *refs):
    mom_ref = refs[-1]
    entry = entry_ref[...]
    lanes = entry.shape[1]
    table = table_ref[half_index(own)]
    for i in range(0, nx, 1):
        pair = range(min(1, nx - i))
        planes = [decay_ref[i + k] * entry + source_ref[i + k] for k in pair]
        got = project(table, jnp.concatenate(planes, axis=1))
        for k in pair:
            part = got[:NMOM, k * lanes : (k + 1) * lanes]
            place = pl.ds(i + k, NMOM, stride=nx)
            mom_ref[place, :] = part + refs[0][place, :] if len(refs) > 1 else part


def new_moments(nx, own, entry, table, decay, source, *more):
    count, lanes = entry.shape
    whole = pl.BlockSpec(memory_space=pltpu.VMEM)
    return pl.pallas_call(
        functools.partial(new_moments_kernel, nx, own),
        in_specs=[whole] * (4 + len(more)),
        out_specs=whole,
        out_shape=pltpu.VMEM((NMOM * nx, lanes), jnp.float32),
        compiler_params=params(),
        cost_estimate=cost(2 * 48 * count * nx * lanes, 8 * count * nx * lanes),
        name="new_moments",
    )(entry, table, decay, source, *more)


def write_kernel(nx, pieces, *refs):
    halves, (out_hbm, held, sems) = (refs[:3], refs[3:6]), refs[6:]
    half, lanes = halves[0][0].shape
    size = half // pieces
    copies = []
    for h, (entry_ref, decay_ref, source_ref) in enumerate(halves):
        start = half_index(h == 0) * half
        for p in range(pieces):
            rows = slice(p * size, (p + 1) * size)
            entry = entry_ref[rows, :]
            base = (h * half + p * size) * nx
            for i in range(nx):
                held[pl.ds(base + i, size, stride=nx), :] = decay_ref[i, rows, :] * entry + source_ref[i, rows, :]
            to = pl.ds(pl.multiple_of((start + p * size) * nx, size * nx), size * nx)
            copy = pltpu.make_async_copy(
                held.at[pl.ds(base, size * nx), :], out_hbm.at[to, :], sems.at[h * pieces + p]
            )
            copy.start()
            copies.append(copy)
    for copy in copies:
        copy.wait()


def write_dist(nx, *halves):
    half, lanes = halves[0].shape
    pieces = max(1, half // 64)
    whole = pl.BlockSpec(memory_space=pltpu.VMEM)
    return pl.pallas_call(
        functools.partial(write_kernel, nx, pieces),
        in_specs=[whole] * 6,
        out_specs=pl.BlockSpec(memory_space=pltpu.HBM),
        out_shape=jax.ShapeDtypeStruct((2 * half * nx, lanes), jnp.float32),
        scratch_shapes=[
            pltpu.VMEM((2 * half * nx, lanes), jnp.float32),
            pltpu.SemaphoreType.DMA((2 * pieces,)),
        ],
        compiler_params=params(),
        cost_estimate=cost(4 * half * nx * lanes, 24 * half * nx * lanes),
        name="write_dist",
    )(*halves)


def stages_of(n):
    out, bit = [], 1
    while bit < n:
        if bit * 4 <= n:
            out.append((bit, 2 * bit, 3 * bit))
            bit *= 4
        else:
            out.append((bit,))
            bit *= 2
    return out


def exchange(a, axis, mask):
    n = lax.axis_size(axis)
    return lax.ppermute(a, axis, [(i, i ^ mask) for i in range(n)])


def partial_sums(a, axis, beside=()):
    n = lax.axis_size(axis)
    beside = list(beside)
    if n & (n - 1) or n == 1:
        total = lax.psum(a, axis)
        return (total, jnp.zeros_like(total)), [f(a) for f in beside]
    stages = stages_of(n)
    done = []
    for i, masks in enumerate(stages):
        got = [exchange(a, axis, m) for m in masks]
        take = beside if i == len(stages) - 1 else beside[:1]
        beside = beside[len(take) :]
        made = [f(a) for f in take]
        got, made = lax.optimization_barrier((got, made))
        done += made
        other = functools.reduce(jnp.add, got)
        if i == len(stages) - 1:
            return (a, other), done
        a = a + other


def local(total, dist, inflow, speed_x, transverse, quad_weight, side):
    count, nx, lanes = dist.shape
    flat = dist.reshape(count * nx, lanes)
    row = lambda a: a.reshape(1, count)
    partial, table, rows, own_dist, other_dist = old_moments(total, nx, row(side), row(speed_x), transverse, row(quad_weight), flat)
    received = []

    def own_planes(sent):
        received.append(chip_exchange(other_dist))
        return slopes(nx, True, *lax.optimization_barrier((rows, own_dist, sent))[:2])

    def partner_planes(sent):
        return slopes(nx, True, *lax.optimization_barrier((rows, received[0], sent))[:2])

    (ma, mb), (own_part, far_part) = partial_sums(partial, "vert", [own_planes, partner_planes])
    summed = ma + mb
    arrived = chip_exchange(summed)
    own_decay, own_source, sign = maps(nx, "own", summed, rows, own_part)
    arrived, own_decay, own_source = lax.optimization_barrier((arrived, own_decay, own_source))
    near, face, entry, *chip = compose_chip(nx, arrived, rows, far_part, sign, own_decay, own_source, inflow)
    got = entry
    chips = lax.axis_size("gx") // 2
    for step in range(chips - 1):
        if step > 0:
            entry, face = pass_face(step, sign, got, entry, chip[0])
        low, high = chip_hop(face, step)
        got = low if low is high else jnp.where(side[0] == 1, low, high)
        if step == 0:
            other_part = slopes(nx, False, *lax.optimization_barrier((rows, other_dist, face))[:2])
            decay, source = maps(nx, "other", summed, rows, other_part)
            got, decay, source = lax.optimization_barrier((got, decay, source))
    if chips == 1:
        decay, source = maps(nx, "other", summed, rows, slopes(nx, False, rows, other_dist))
    keep, share = share_entry(chips - 1, sign, got, entry, near)
    other = chip_exchange(share)
    own_moments = new_moments(nx, True, keep, table, own_decay, own_source)
    other, own_moments = lax.optimization_barrier((other, own_moments))
    new_partial = new_moments(nx, False, other, table, decay, source, own_moments)

    def write(sent):
        args = lax.optimization_barrier((keep, own_decay, own_source, other, decay, source, sent))[:6]
        return write_dist(nx, *args)

    (na, nb), (new_flat,) = partial_sums(new_partial, "vert", [write])
    return new_flat.reshape(count, nx, lanes), (na + nb).reshape(NMOM, nx, lanes)


def solution(mesh):
    def whole(dist, inflow, speed_x, transverse, quad_weight, side):
        body = functools.partial(local, dist.shape[0])
        return jax.shard_map(
            body,
            mesh=mesh,
            in_specs=(P("vert", "gx", None), P("vert", None), P("vert"), P(None, "vert"), P("vert"), P("vert")),
            out_specs=(P("vert", "gx", None), P(None, "gx", None)),
            check_vma=False,
        )(dist, inflow, speed_x, transverse, quad_weight, side)

    return whole
```

```python
import functools

import jax
import jax.numpy as jnp
from jax import lax
from jax.experimental import pallas as pl
from jax.experimental.pallas import tpu as pltpu
from jax.sharding import PartitionSpec as P

NZ = 32
KAPPA_CELL = 0.02
LOG2E = 1.4426950408889634
RATIO = -2.0 / LOG2E
SHEAR = 0.19
NMOM = 13
ROWS = 16
TERMS = 5
DEPTH = 128


def params(**kw):
    return pltpu.CompilerParams(vmem_limit_bytes=20 * 1024 * 1024, **kw)


def cost(flops, nbytes):
    return pl.CostEstimate(flops=flops, bytes_accessed=nbytes, transcendentals=0)


def split(a):
    high = a.astype(jnp.bfloat16)
    low = (a - high.astype(jnp.float32)).astype(jnp.bfloat16)
    return high, low


def split3(a):
    high, rest = split(a)
    mid, low = split(a - high.astype(jnp.float32))
    return [high.astype(jnp.float32), mid.astype(jnp.float32), low.astype(jnp.float32)]


def project(table, plane):
    high, low = split(plane)
    first = jnp.dot(table, high, preferred_element_type=jnp.float32)
    second = jnp.dot(table[:ROWS], low, preferred_element_type=jnp.float32)
    return first[:ROWS] + first[ROWS:] + second


def moments_kernel(total, nx, side_hbm, speed_hbm, cross_hbm, weight_hbm, dist_hbm,
                   mom_ref, table_ref, rows_ref, own_ref, other_ref, side_ref, speed_ref, cross_ref, weight_ref, sems):
    half = speed_ref.shape[1] // 2
    size = half * nx
    small = [(side_hbm, side_ref), (speed_hbm, speed_ref), (cross_hbm, cross_ref), (weight_hbm, weight_ref)]
    copies = [pltpu.make_async_copy(a, b, sems.at[2 + i]) for i, (a, b) in enumerate(small)]
    parts = []
    for i, ref in enumerate((own_ref, other_ref)):
        rows = pl.ds(pl.multiple_of(half_index(i == 0) * size, size), size)
        parts.append(pltpu.make_async_copy(dist_hbm.at[rows, :], ref, sems.at[i]))
    for c in copies + parts:
        c.start()
    for c in copies:
        c.wait()
    speed = speed_ref[...]
    x = jnp.where(side_ref[...] == 1, speed, -speed)
    y = cross_ref[0:1, :]
    z = cross_ref[1:2, :]
    xx, yy, zz = x * x, y * y, z * z
    square = xx + yy + zz
    stacked = jnp.concatenate([x, y, z] + [jnp.zeros_like(x)] * 5, axis=0)
    for h in range(2):
        rows_ref[h] = stacked[:, h * half : (h + 1) * half]
    rows = [jnp.ones_like(x), x, y, z, xx, yy, zz, x * y, x * z, y * z, x * square, y * square, z * square]
    rows += [jnp.zeros_like(x)] * (ROWS - NMOM)
    full = jnp.concatenate(rows, axis=0) * (weight_ref[...] * (1.0 / total))
    high, low = split(full)
    table = jnp.concatenate([high, low], axis=0)
    for h in range(2):
        table_ref[h] = table[:, h * half : (h + 1) * half]
    for c, ref in enumerate((own_ref, other_ref)):
        parts[c].wait()
        tab = table_ref[half_index(c == 0)]
        for i in range(nx):
            part = project(tab, ref[pl.ds(i, half, stride=nx), :])[:NMOM]
            place = pl.ds(i, NMOM, stride=nx)
            mom_ref[place, :] = part if c == 0 else mom_ref[place, :] + part


def old_moments(total, nx, side, speed, cross, weight, dist):
    count, lanes = speed.shape[1], dist.shape[1]
    whole = pl.BlockSpec(memory_space=pltpu.VMEM)
    return pl.pallas_call(
        functools.partial(moments_kernel, total, nx),
        in_specs=[pl.BlockSpec(memory_space=pltpu.HBM)] * 5,
        out_specs=[whole] * 5,
        out_shape=[
            pltpu.VMEM((NMOM * nx, lanes), jnp.float32),
            pltpu.VMEM((2, 2 * ROWS, count // 2), jnp.bfloat16),
            pltpu.VMEM((2, 8, count // 2), jnp.float32),
            pltpu.VMEM((count * nx // 2, lanes), jnp.float32),
            pltpu.VMEM((count * nx // 2, lanes), jnp.float32),
        ],
        scratch_shapes=[
            pltpu.VMEM(side.shape, jnp.int32),
            pltpu.VMEM(speed.shape, jnp.float32),
            pltpu.VMEM(cross.shape, jnp.float32),
            pltpu.VMEM(weight.shape, jnp.float32),
            pltpu.SemaphoreType.DMA((6,)),
        ],
        compiler_params=params(),
        cost_estimate=cost(2 * 48 * count * nx * lanes, 4 * count * nx * lanes),
        name="moments",
    )(*[pltpu.with_memory_space_constraint(a, pltpu.HBM) for a in (side, speed, cross, weight, dist)])


def half_index(own):
    core = lax.axis_index("gx") % 2
    return core if own else 1 - core


def slope_kernel(nx, own, rows_ref, dist_ref, slope_ref, speed_ref, feature_ref, comp_ref):
    count = slope_ref.shape[1]
    lanes = dist_ref.shape[1]
    rows = rows_ref[half_index(own)]
    columns = jnp.transpose(rows)
    speed_ref[...] = jnp.broadcast_to(jnp.abs(columns[:, 0:1]), (count, lanes))
    for k in range(2):
        comp_ref[k] = jnp.broadcast_to(columns[:, k + 1 : k + 2], (count, lanes))
    x, y, z = rows[0:1], rows[1:2], rows[2:3]
    high, mid, low = split3(jnp.concatenate([x * x + y * y + z * z, x, y, z, jnp.ones_like(x)], axis=0))
    terms = jnp.concatenate([high, high, mid, mid, high, low], axis=0)
    terms = jnp.concatenate([terms, jnp.zeros((DEPTH - 6 * TERMS, count), jnp.float32)], axis=0)
    feature_ref[...] = jnp.transpose(terms).astype(jnp.bfloat16)
    group = 32

    def one(g, carry):
        at = pl.multiple_of(g * group, group)
        y = comp_ref[0, pl.ds(at, group), :]
        z = comp_ref[1, pl.ds(at, group), :]
        lane = lax.broadcasted_iota(jnp.int32, (group, lanes), 1)
        from_y = jnp.where(y > 0, lane + (lanes - NZ), lane + NZ) & (lanes - 1)
        from_z = (lane & ~(NZ - 1)) | (jnp.where(z > 0, lane + (NZ - 1), lane + 1) & (NZ - 1))
        ay, az = KAPPA_CELL * jnp.abs(y), KAPPA_CELL * jnp.abs(z)
        both = ay + az
        for i in range(nx):
            d = dist_ref[pl.ds(at * nx + i, group, stride=nx), :]
            near_y = jnp.take_along_axis(d, from_y, axis=1)
            near_z = jnp.take_along_axis(d, from_z, axis=1)
            slope_ref[i, pl.ds(at, group), :] = both * d - ay * near_y - az * near_z
        return carry

    lax.fori_loop(0, count // group, one, 0)


def slopes(nx, own, rows, dist):
    count, lanes = rows.shape[2], dist.shape[1]
    whole = pl.BlockSpec(memory_space=pltpu.VMEM)
    return pl.pallas_call(
        functools.partial(slope_kernel, nx, own),
        in_specs=[whole] * 2,
        out_specs=[whole] * 3,
        out_shape=[
            pltpu.VMEM((nx, count, lanes), jnp.float32),
            pltpu.VMEM((count, lanes), jnp.float32),
            pltpu.VMEM((count, DEPTH), jnp.bfloat16),
        ],
        scratch_shapes=[pltpu.VMEM((2, count, lanes), jnp.float32)],
        compiler_params=params(),
        cost_estimate=cost(20 * count * nx * lanes, 8 * count * nx * lanes),
        name="slope",
    )(rows, dist)


def state_of(nx, sum_ref, state, bulk_terms, flux_terms):
    lanes = sum_ref.shape[1]
    m = [sum_ref[k * nx : (k + 1) * nx, :] for k in range(NMOM)]
    n = m[0]
    inv_n = 1.0 / n
    u = [m[1] * inv_n, m[2] * inv_n, m[3] * inv_n]
    energy = m[4] + m[5] + m[6]
    uu = u[0] * u[0] + u[1] * u[1] + u[2] * u[2]
    temp = (energy * inv_n - uu) * (1.0 / 3.0)
    second = ((m[4], m[7], m[8]), (m[7], m[5], m[9]), (m[8], m[9], m[6]))
    inv_t = 1.0 / temp
    nu = KAPPA_CELL * n * jnp.exp(SHEAR * jnp.log(temp))
    rate = inv_t * (-0.5 * LOG2E)
    flux_scale = inv_n * inv_t * inv_t * (RATIO / 15.0)
    q = []
    for k in range(3):
        inner = u[0] * second[k][0] + u[1] * second[k][1] + u[2] * second[k][2]
        q.append(0.5 * flux_scale * (m[10 + k] - 2.0 * inner - u[k] * energy + 2.0 * n * u[k] * uu))
    twice = -2.0 * rate
    bulk = [rate, twice * u[0], twice * u[1], twice * u[2], rate * uu]
    flux = [jnp.zeros_like(n), q[0], q[1], q[2], -(u[0] * q[0] + u[1] * q[1] + u[2] * q[2])]
    for terms, ref in ((bulk, bulk_terms), (flux, flux_terms)):
        for k in range(TERMS):
            high, mid, low = split3(terms[k])
            for i, one in enumerate((high, mid, high, mid, low, high)):
                ref[(i * TERMS + k) * nx : (i * TERMS + k + 1) * nx, :] = one
        ref[6 * TERMS * nx :, :] = jnp.zeros(((32 - 6 * TERMS) * nx, lanes), jnp.float32)
    state[0] = nu * n * inv_t * jnp.sqrt(inv_t)
    state[1] = nu


def sweep(nx, forward, state, bulk_terms, flux_terms, slope_ref, speed_ref, feature_ref, fields, last_ref):
    count, lanes = speed_ref.shape
    rest = jnp.zeros((DEPTH - 32, 2 * lanes), jnp.bfloat16)
    group = 32
    places, cells = [], []
    for j in range(nx):
        at_x = jnp.where(forward, j, nx - 1 - j)
        both = jnp.concatenate([ref[pl.ds(at_x, 32, stride=nx), :] for ref in (bulk_terms, flux_terms)], axis=1)
        places.append(at_x)
        cells.append(jnp.concatenate([both.astype(jnp.bfloat16), rest], axis=0))
    group = 32
    for at in range(0, count, group):
        rows = slice(at, at + group)
        speed = speed_ref[rows, :]
        run_decay = run_source = None
        for j in range(nx):
            at_x = places[j]
            both = jnp.dot(feature_ref[rows, :], cells[j], preferred_element_type=jnp.float32)
            exponent, wq = both[:, :lanes], both[:, lanes:]
            shape = 1.0 + wq * (exponent - 5.0 / RATIO)
            target = state[0, pl.ds(at_x, 1), :] * jnp.exp2(exponent) * shape
            inv = 1.0 / (speed + state[1, pl.ds(at_x, 1), :])
            decay = speed * inv
            source = (target - slope_ref[at_x, rows, :]) * inv
            if j > 0:
                source = decay * run_source + source
                decay = decay * run_decay
            run_decay, run_source = decay, source
            if fields:
                fields[0][at_x, rows, :] = decay
                fields[1][at_x, rows, :] = source
        if last_ref is not None:
            last_ref[0, rows, :] = run_decay
            last_ref[1, rows, :] = run_source


def map_kernel(nx, kind, sum_ref, rows_ref, slope_ref, speed_ref, feature_ref, *refs):
    outs, (state, bulk_terms, flux_terms) = refs[:-3], refs[-3:]
    state_of(nx, sum_ref, state, bulk_terms, flux_terms)
    forward = rows_ref[0, 0:1, 0:1][0, 0] > 0
    if kind == "own":
        outs[2][...] = jnp.broadcast_to(rows_ref[0, 0:1, 0:1], outs[2].shape)
    fields, last_ref = outs[:2], None
    sweep(nx, forward, state, bulk_terms, flux_terms, slope_ref, speed_ref, feature_ref, fields, last_ref)


def map_scratch(nx, lanes):
    return [pltpu.VMEM((rows, lanes), jnp.float32) if rows else pltpu.VMEM((2, nx, lanes), jnp.float32)
            for rows in (0, 32 * nx, 32 * nx)]


def maps(nx, kind, total, rows, part):
    count, lanes = part[1].shape
    whole = pl.BlockSpec(memory_space=pltpu.VMEM)
    field = pltpu.VMEM((nx, count, lanes), jnp.float32)
    outs = [field, field] + ([pltpu.VMEM((8, lanes), jnp.float32)] if kind == "own" else [])
    return pl.pallas_call(
        functools.partial(map_kernel, nx, kind),
        in_specs=[whole] * 5,
        out_specs=[whole] * len(outs),
        out_shape=outs,
        scratch_shapes=map_scratch(nx, lanes),
        compiler_params=params(),
        cost_estimate=cost(40 * count * nx * lanes, 12 * count * nx * lanes),
        name=kind + "_maps",
    )(total, rows, *part)


def standing(sign_ref):
    place, chips = lax.axis_index("gx"), lax.axis_size("gx") // 2
    chip, core = place // 2, place % 2
    forward = sign_ref[0:1, :] > 0
    return jnp.where(forward, core, 1 - core) == 0, jnp.where(forward, chip, chips - 1 - chip)


def compose_kernel(nx, sum_ref, rows_ref, slope_ref, speed_ref, feature_ref, sign_ref, decay_ref, source_ref, inflow_ref,
                   near_ref, face_ref, entry_ref, *refs):
    chip_ref, (got_ref, state, bulk_terms, flux_terms) = refs[:-4], refs[-4:]
    state_of(nx, sum_ref, state, bulk_terms, flux_terms)
    forward = rows_ref[0, 0:1, 0:1][0, 0] > 0
    sweep(nx, forward, state, bulk_terms, flux_terms, slope_ref, speed_ref, feature_ref, (), got_ref)
    first, _ = standing(sign_ref)
    half = entry_ref.shape[0]
    mine = pl.ds(pl.multiple_of(half_index(True) * half, half), half)
    last = jnp.where(forward, nx - 1, 0)
    decay, source = decay_ref[last], source_ref[last]
    got_decay, got_source = got_ref[0], got_ref[1]
    near_decay = jnp.where(first, decay, got_decay)
    near_source = jnp.where(first, source, got_source)
    far_decay = jnp.where(first, got_decay, decay)
    far_source = jnp.where(first, got_source, source)
    chip_decay, chip_source = far_decay * near_decay, far_decay * near_source + far_source
    near_ref[0], near_ref[1] = near_decay, near_source
    if chip_ref:
        chip_ref[0][0], chip_ref[0][1] = chip_decay, chip_source
    entry = inflow_ref[mine, :]
    entry_ref[...] = entry
    face_ref[...] = chip_decay * entry + chip_source


def compose_chip(nx, total, rows, part, sign, decay, source, inflow):
    half, lanes = part[1].shape
    whole = pl.BlockSpec(memory_space=pltpu.VMEM)
    pair = pltpu.VMEM((2, half, lanes), jnp.float32)
    outs = [pair] + [pltpu.VMEM((half, lanes), jnp.float32)] * 2
    if lax.axis_size("gx") > 4:
        outs.append(pair)
    return pl.pallas_call(
        functools.partial(compose_kernel, nx),
        in_specs=[whole] * 9,
        out_specs=[whole] * len(outs),
        out_shape=outs,
        scratch_shapes=[pair] + map_scratch(nx, lanes),
        compiler_params=params(),
        cost_estimate=cost(40 * half * nx * lanes, 12 * half * nx * lanes),
        name="compose",
    )(total, rows, *part, sign, decay, source, inflow)


def pass_kernel(step, sign_ref, got_ref, entry_ref, chip_ref, next_ref, face_ref):
    _, before = standing(sign_ref)
    entry = jnp.where(before == step, got_ref[...], entry_ref[...])
    next_ref[...] = entry
    face_ref[...] = chip_ref[0] * entry + chip_ref[1]


def pass_face(step, sign, got, entry, chip):
    whole = pl.BlockSpec(memory_space=pltpu.VMEM)
    out = pltpu.VMEM(entry.shape, jnp.float32)
    return pl.pallas_call(
        functools.partial(pass_kernel, step),
        in_specs=[whole] * 4,
        out_specs=[whole] * 2,
        out_shape=[out, out],
        compiler_params=params(),
        cost_estimate=cost(3 * entry.size, 20 * entry.size),
        name="face",
    )(sign, got, entry, chip)


def share_kernel(step, sign_ref, got_ref, entry_ref, near_ref, keep_ref, send_ref):
    first, before = standing(sign_ref)
    entry = jnp.where(before == step, got_ref[...], entry_ref[...])
    middle = near_ref[0] * entry + near_ref[1]
    keep_ref[...] = jnp.where(first, entry, middle)
    send_ref[...] = jnp.where(first, middle, entry)


def share_entry(step, sign, got, entry, near):
    whole = pl.BlockSpec(memory_space=pltpu.VMEM)
    out = pltpu.VMEM(entry.shape, jnp.float32)
    return pl.pallas_call(
        functools.partial(share_kernel, step),
        in_specs=[whole] * 4,
        out_specs=[whole] * 2,
        out_shape=[out, out],
        compiler_params=params(),
        cost_estimate=cost(3 * entry.size, 20 * entry.size),
        name="share",
    )(sign, got, entry, near)


def chip_exchange(a):
    n = lax.axis_size("gx")
    return lax.ppermute(a, "gx", [(i, i ^ 1) for i in range(n)])


def chip_hop(face, step):
    chips = lax.axis_size("gx") // 2
    up, down = (step, step + 1), (chips - 1 - step, chips - 2 - step)
    pairs = [(2 * a + c, 2 * b + c) for a, b in (up, down) for c in range(2)]
    if chips % 2 == 0:
        got = lax.ppermute(face, "gx", pairs)
        return got, got
    return lax.ppermute(face, "gx", pairs[:2]), lax.ppermute(face, "gx", pairs[2:])


def new_moments_kernel(nx, own, entry_ref, table_ref, decay_ref, source_ref, *refs):
    mom_ref = refs[-1]
    entry = entry_ref[...]
    lanes = entry.shape[1]
    table = table_ref[half_index(own)]
    for i in range(0, nx, 1):
        pair = range(min(1, nx - i))
        planes = [decay_ref[i + k] * entry + source_ref[i + k] for k in pair]
        got = project(table, jnp.concatenate(planes, axis=1))
        for k in pair:
            part = got[:NMOM, k * lanes : (k + 1) * lanes]
            place = pl.ds(i + k, NMOM, stride=nx)
            mom_ref[place, :] = part + refs[0][place, :] if len(refs) > 1 else part


def new_moments(nx, own, entry, table, decay, source, *more):
    count, lanes = entry.shape
    whole = pl.BlockSpec(memory_space=pltpu.VMEM)
    return pl.pallas_call(
        functools.partial(new_moments_kernel, nx, own),
        in_specs=[whole] * (4 + len(more)),
        out_specs=whole,
        out_shape=pltpu.VMEM((NMOM * nx, lanes), jnp.float32),
        compiler_params=params(),
        cost_estimate=cost(2 * 48 * count * nx * lanes, 8 * count * nx * lanes),
        name="new_moments",
    )(entry, table, decay, source, *more)


def write_kernel(nx, pieces, *refs):
    halves, (out_hbm, held, sems) = (refs[:3], refs[3:6]), refs[6:]
    half, lanes = halves[0][0].shape
    size = half // pieces
    copies = []
    for h, (entry_ref, decay_ref, source_ref) in enumerate(halves):
        start = half_index(h == 0) * half
        for p in range(pieces):
            rows = slice(p * size, (p + 1) * size)
            entry = entry_ref[rows, :]
            base = (h * half + p * size) * nx
            for i in range(nx):
                held[pl.ds(base + i, size, stride=nx), :] = decay_ref[i, rows, :] * entry + source_ref[i, rows, :]
            to = pl.ds(pl.multiple_of((start + p * size) * nx, size * nx), size * nx)
            copy = pltpu.make_async_copy(
                held.at[pl.ds(base, size * nx), :], out_hbm.at[to, :], sems.at[h * pieces + p]
            )
            copy.start()
            copies.append(copy)
    for copy in copies:
        copy.wait()


def write_dist(nx, *halves):
    half, lanes = halves[0].shape
    pieces = max(1, half // 64)
    whole = pl.BlockSpec(memory_space=pltpu.VMEM)
    return pl.pallas_call(
        functools.partial(write_kernel, nx, pieces),
        in_specs=[whole] * 6,
        out_specs=pl.BlockSpec(memory_space=pltpu.HBM),
        out_shape=jax.ShapeDtypeStruct((2 * half * nx, lanes), jnp.float32),
        scratch_shapes=[
            pltpu.VMEM((2 * half * nx, lanes), jnp.float32),
            pltpu.SemaphoreType.DMA((2 * pieces,)),
        ],
        compiler_params=params(),
        cost_estimate=cost(4 * half * nx * lanes, 24 * half * nx * lanes),
        name="write_dist",
    )(*halves)


def stages_of(n):
    out, bit = [], 1
    while bit < n:
        if bit * 4 <= n:
            out.append((bit, 2 * bit, 3 * bit))
            bit *= 4
        else:
            out.append((bit,))
            bit *= 2
    return out


def exchange(a, axis, mask):
    n = lax.axis_size(axis)
    return lax.ppermute(a, axis, [(i, i ^ mask) for i in range(n)])


def partial_sums(a, axis, beside=()):
    n = lax.axis_size(axis)
    beside = list(beside)
    if n & (n - 1) or n == 1:
        total = lax.psum(a, axis)
        return (total, jnp.zeros_like(total)), [f(a) for f in beside]
    stages = stages_of(n)
    done = []
    for i, masks in enumerate(stages):
        got = [exchange(a, axis, m) for m in masks]
        take = beside if i == len(stages) - 1 else beside[:1]
        beside = beside[len(take) :]
        made = [f(a) for f in take]
        got, made = lax.optimization_barrier((got, made))
        done += made
        other = functools.reduce(jnp.add, got)
        if i == len(stages) - 1:
            return (a, other), done
        a = a + other


def local(total, dist, inflow, speed_x, transverse, quad_weight, side):
    count, nx, lanes = dist.shape
    flat = dist.reshape(count * nx, lanes)
    row = lambda a: a.reshape(1, count)
    partial, table, rows, own_dist, other_dist = old_moments(total, nx, row(side), row(speed_x), transverse, row(quad_weight), flat)
    received = []

    def own_planes(sent):
        received.append(chip_exchange(other_dist))
        return slopes(nx, True, *lax.optimization_barrier((rows, own_dist, sent))[:2])

    def partner_planes(sent):
        return slopes(nx, True, *lax.optimization_barrier((rows, received[0], sent))[:2])

    (ma, mb), (own_part, far_part) = partial_sums(partial, "vert", [own_planes, partner_planes])
    summed = ma + mb
    arrived = chip_exchange(summed)
    own_decay, own_source, sign = maps(nx, "own", summed, rows, own_part)
    arrived, own_decay, own_source = lax.optimization_barrier((arrived, own_decay, own_source))
    near, face, entry, *chip = compose_chip(nx, arrived, rows, far_part, sign, own_decay, own_source, inflow)
    got = entry
    chips = lax.axis_size("gx") // 2
    for step in range(chips - 1):
        if step > 0:
            entry, face = pass_face(step, sign, got, entry, chip[0])
        low, high = chip_hop(face, step)
        got = low if low is high else jnp.where(side[0] == 1, low, high)
        if step == 0:
            other_part = slopes(nx, False, *lax.optimization_barrier((rows, other_dist, face))[:2])
            decay, source = maps(nx, "other", summed, rows, other_part)
            got, decay, source = lax.optimization_barrier((got, decay, source))
    if chips == 1:
        decay, source = maps(nx, "other", summed, rows, slopes(nx, False, rows, other_dist))
    keep, share = share_entry(chips - 1, sign, got, entry, near)
    other = chip_exchange(share)
    own_moments = new_moments(nx, True, keep, table, own_decay, own_source)
    other, own_moments = lax.optimization_barrier((other, own_moments))
    new_partial = new_moments(nx, False, other, table, decay, source, own_moments)

    def write(sent):
        args = lax.optimization_barrier((keep, own_decay, own_source, other, decay, source, sent))[:6]
        return write_dist(nx, *args)

    (na, nb), (_, new_flat) = partial_sums(new_partial, "vert", [lambda sent: sent, write])
    return new_flat.reshape(count, nx, lanes), (na + nb).reshape(NMOM, nx, lanes)


def solution(mesh):
    def whole(dist, inflow, speed_x, transverse, quad_weight, side):
        body = functools.partial(local, dist.shape[0])
        return jax.shard_map(
            body,
            mesh=mesh,
            in_specs=(P("vert", "gx", None), P("vert", None), P("vert"), P(None, "vert"), P("vert"), P("vert")),
            out_specs=(P("vert", "gx", None), P(None, "gx", None)),
            check_vma=False,
        )(dist, inflow, speed_x, transverse, quad_weight, side)

    return whole
```
